256 devices in a mesh: rows: 8 (over x, core), cols: 32 (over z, y).
Axes of the slice: x: 4, y: 4, z: 8, core: 2. Of those that a mesh axis runs over, the one named last changes fastest.
Arguments:
- hidden_states: bfloat16 [2, 2048, 1024], P(None, 'rows', 'cols'), may hold values from -24 to 24
- ln_in_gain: bfloat16 [1024], P('cols'), may hold values from 0.25 to 1.75
- w_in: bfloat16 [1024, 4096], P(None, 'cols'), may hold values from -0.1875 to 0.1875
- w_out: bfloat16 [4096, 1024], P('cols'), may hold values from -0.09375 to 0.09375
- ln_out_gain: bfloat16 [1024], P('cols'), may hold values from 0.25 to 1.75
- prototypes: bfloat16 [65536, 1024], P('cols'), may hold values from -0.375 to 0.375
Outputs:
- embed_grad: float32 [2, 2048, 1024], P(None, 'rows', 'cols')
- proto_grad: float32 [1024, 65536], P('rows', 'cols')
The draws below stay inside these ranges and needn't reach their ends.
All inputs are finite; a program needn't handle non-finite values.
Results may differ from the reference program's by a relative error of at most 0.0031.
Values may be sent and summed in bfloat16 or wider, within the bound.
No kernel may reach another device: no remote copies, remote signals or barrier semaphores. Data moves between devices by JAX's collectives and lax.ppermute only.
A program may use at most 128 MiB of HBM per device.

```python
import math
import jax
import jax.numpy as jnp
from jax import lax

D = 1024
FF = 4096
PROTOS = 65536
SINK_ITERS = 3
IMAGES = 2048


cluster_count = 64


label_blocks = 256


def cluster_centers(key):
    return jax.random.normal(jax.random.fold_in(key, 11), (cluster_count, D), jnp.float32)


def image_labels(key):
    base_key = jax.random.fold_in(key, 12)
    first_key, second_key, third_key, order_key = jax.random.split(base_key, 4)
    first = jax.random.randint(first_key, (IMAGES,), 0, cluster_count)
    second = jax.random.randint(second_key, (IMAGES,), 0, cluster_count)
    third = jax.random.randint(third_key, (IMAGES,), 0, cluster_count)
    smallest = jnp.minimum(jnp.minimum(first, second), third)
    order = jax.random.permutation(order_key, cluster_count)
    return jnp.take(order, smallest, axis=0)


def proto_labels(key):
    block_labels = jax.random.randint(jax.random.fold_in(key, 13), (label_blocks,), 0, cluster_count)
    return jnp.repeat(block_labels, PROTOS // label_blocks)


def draw_hidden_states(key, part):
    centers = cluster_centers(key)
    labels = image_labels(key)
    shared = jnp.take(centers, labels, axis=0)[None, :, :]
    strength = jax.random.uniform(jax.random.fold_in(key, 22), (2, IMAGES, 1), jnp.float32, minval=0.35, maxval=0.85)
    noise_key = jax.random.fold_in(key, 21)
    noise_part = jax.random.normal(noise_key, (2, IMAGES, D), jnp.float32)
    values = strength * shared + noise_part
    return jnp.clip(values, -24.0, 24.0).astype(jnp.bfloat16)


def draw_prototypes(key, part):
    centers = cluster_centers(key)
    labels = proto_labels(key)
    shared = jnp.take(centers, labels, axis=0)
    pull_factor = jax.random.uniform(jax.random.fold_in(key, 31), (PROTOS, 1), jnp.float32, minval=0.5, maxval=0.9)
    noise_key = jax.random.fold_in(key, 32)
    noise_part = jax.random.normal(noise_key, (PROTOS, D), jnp.float32)
    length = jnp.ones((PROTOS, 1), jnp.float32)
    values = 0.03125 * length * (pull_factor * shared + noise_part) / jnp.sqrt(1.0 + pull_factor * pull_factor)
    return jnp.clip(values, -0.375, 0.375).astype(jnp.bfloat16)


def shard_levels(stream_key, dims, shards, low, largest):
    def one(dim, shards_of):
        heights = jax.random.uniform(jax.random.fold_in(jax.random.fold_in(stream_key, 6), dim), (shards_of,), jnp.float32, low / len(shards), largest / len(shards))
        return jnp.repeat(jnp.exp(heights), dims[dim] // shards_of).reshape((-1,) + (1,) * (len(dims) - dim - 1))

    level = one(*shards[0])
    for cut in shards[1:]:
        level = level * one(*cut)
    return level


def normal_values(stream_key, dims, scale, most, pieces=(), dtype=jnp.bfloat16):
    factor_of = shard_levels(stream_key, dims, pieces, -0.22, 0.18) if pieces else 1.0
    array = jax.random.normal(stream_key, dims, jnp.float32) * scale * factor_of
    return jnp.minimum(jnp.maximum(array, -most), most).astype(dtype)


def setup_inputs(seed: int = 0) -> dict:
    streams_of = jax.random.split(jax.random.key(seed), 7)
    return {
        "hidden_states": draw_hidden_states(jax.random.fold_in(streams_of[6], 71), 0),
        "ln_in_gain": jnp.clip(1.0 + 0.15 * jax.random.normal(streams_of[1], (D,), jnp.float32), 0.25, 1.75).astype(jnp.bfloat16),
        "w_in": normal_values(streams_of[2], (D, FF), D ** -0.5, 0.1875, ((1, 32),)),
        "w_out": normal_values(streams_of[3], (FF, D), FF ** -0.5, 0.09375, ((0, 32),)),
        "ln_out_gain": jnp.clip(1.0 + 0.15 * jax.random.normal(streams_of[4], (D,), jnp.float32), 0.25, 1.75).astype(jnp.bfloat16),
        "prototypes": draw_prototypes(jax.random.fold_in(streams_of[6], 71), 0),
    }


sink_temp = 0.05
soft_temp = 0.1
norm_eps = 1e-05
unit_eps = 1e-06

def layer_norm(values, gain):
    center = lax.optimization_barrier(jnp.mean(values, axis=1, keepdims=True))
    spread = lax.optimization_barrier(jnp.mean(values * values, axis=1, keepdims=True)) - center * center
    return (values - center) * lax.rsqrt(spread + norm_eps) * gain

def reference(hidden_states, ln_in_gain, w_in, w_out, ln_out_gain, prototypes):
    row_total = 2 * IMAGES
    inputs_f = hidden_states.astype(jnp.float32).reshape(row_total, D)
    normed = layer_norm(inputs_f, ln_in_gain.astype(jnp.float32)).astype(jnp.bfloat16)
    hidden = jax.nn.gelu(jnp.dot(normed, w_in, preferred_element_type=jnp.float32), approximate=False).astype(jnp.bfloat16)
    resid = inputs_f + jnp.dot(hidden, w_out, preferred_element_type=jnp.float32)
    final = layer_norm(resid, ln_out_gain.astype(jnp.float32))
    squared = lax.optimization_barrier(jnp.sum(final * final, axis=1, keepdims=True))
    embed = (final * lax.rsqrt(squared + unit_eps)).astype(jnp.bfloat16)
    proto_f = prototypes.astype(jnp.float32)
    proto_len = jnp.sqrt(lax.optimization_barrier(jnp.sum(proto_f * proto_f, axis=1)) + unit_eps)
    unit = (proto_f / proto_len[:, None]).astype(jnp.bfloat16)
    width = math.gcd(PROTOS, 2048)
    block_count = PROTOS // width
    unit_blocks = unit.reshape(block_count, width, D)
    proto_blocks = proto_f.reshape(block_count, width, D)
    len_blocks = proto_len.reshape(block_count, width)

    def block_scores(unit_block):
        flat = lax.dot_general(embed, unit_block, (((1,), (1,)), ((), ())), preferred_element_type=jnp.float32)
        return flat.reshape(2, IMAGES, width)

    def sweep(scale_image):

        def visit(carry, unit_block):
            image_sum, soft_sum = carry
            scores = block_scores(unit_block)
            base = jnp.exp(scores / sink_temp)
            scale_proto = 1.0 / lax.optimization_barrier(jnp.sum(base * scale_image[:, :, None], axis=1))
            image_sum = image_sum + lax.optimization_barrier(jnp.sum(base * scale_proto[:, None, :], axis=2))
            soft_sum = soft_sum + lax.optimization_barrier(jnp.sum(jnp.exp(scores / soft_temp), axis=2))
            return ((image_sum, soft_sum), scale_proto)
        zeros = jnp.zeros((2, IMAGES), jnp.float32)
        (image_sum, soft_sum), scale_proto = lax.scan(visit, (zeros, zeros), unit_blocks)
        return (1.0 / image_sum, soft_sum, scale_proto)
    scale_image = jnp.ones((2, IMAGES), jnp.float32)
    soft_total = scale_image
    scale_proto = jnp.zeros((block_count, 2, width), jnp.float32)
    for repeat in range(SINK_ITERS):
        scale_image, soft_total, scale_proto = sweep(scale_image)
    factor = 0.5 * math.sqrt(PROTOS * D)

    def backward(carry, blocks_in):
        unit_block, proto_block, len_block, proto_scale = blocks_in
        scores = block_scores(unit_block)
        codes = jnp.exp(scores / sink_temp) * proto_scale[:, None, :] * scale_image[:, :, None]
        prob = jnp.exp(scores / soft_temp) / soft_total[:, :, None]
        grad_scores = (factor * (prob - codes[::-1])).astype(jnp.bfloat16)
        flat = grad_scores.reshape(row_total, width)
        carry = carry + jnp.dot(flat, unit_block, preferred_element_type=jnp.float32)
        direct = lax.dot_general(embed, flat, (((0,), (0,)), ((), ())), preferred_element_type=jnp.float32)
        radial = lax.optimization_barrier(jnp.sum(grad_scores.astype(jnp.float32) * scores, axis=(0, 1)))
        grad_block = (direct - proto_block.T * (radial / len_block)[None, :]) / len_block[None, :]
        return (carry, grad_block)
    embed_grad, grad_blocks = lax.scan(backward, jnp.zeros((row_total, D), jnp.float32), (unit_blocks, proto_blocks, len_blocks, scale_proto))
    proto_grad = jnp.transpose(grad_blocks, (1, 0, 2)).reshape(D, PROTOS)
    return (embed_grad.reshape(2, IMAGES, D), proto_grad)
```

```python
import math

import jax
import jax.numpy as jnp
from jax import lax
from jax.sharding import Mesh, PartitionSpec as P

D = 1024
PROTOS = 65536
SINK_ITERS = 3


sink_temp = 0.05
soft_temp = 0.1
norm_eps = 1e-05
unit_eps = 1e-06

ROWS = ("x", "core")
COLS = ("z", "y")
f32 = jnp.float32
bf16 = jnp.bfloat16


def gather_all(values, axes):
    count = lax.axis_size(axes)
    copies = jnp.broadcast_to(values[None], (count,) + values.shape)
    return lax.all_to_all(copies, axes, 0, 0)


def sum_small(values, axes):
    return jnp.sum(gather_all(values, axes), axis=0)


def scatter_sum(blocks, axes):
    return jnp.sum(lax.all_to_all(blocks, axes, 0, 0).astype(f32), axis=0)


def body(hidden_states, ln_in_gain, w_in, w_out, ln_out_gain, prototypes):
    view_count, image_rows, local_width = hidden_states.shape
    row_count = view_count * image_rows
    col_count = lax.axis_size(COLS)
    row_block = row_count // col_count
    col_index = lax.axis_index(COLS)

    gains = gather_all(jnp.stack([ln_in_gain, ln_out_gain]), COLS)
    gain_in = gains[:, 0].reshape(D).astype(f32)
    gain_out = gains[:, 1].reshape(D).astype(f32)

    inputs_t = gather_all(hidden_states.reshape(row_count, local_width).T, COLS).reshape(D, row_count)
    inputs_f = inputs_t.astype(f32)
    center = jnp.mean(inputs_f, axis=0)
    spread = jnp.mean(inputs_f * inputs_f, axis=0) - center * center
    normed_t = (
        (inputs_f - center[None, :]) * lax.rsqrt(spread + norm_eps)[None, :] * gain_in[:, None]
    ).astype(bf16)
    hidden_t = jax.nn.gelu(
        lax.dot_general(w_in, normed_t, (((0,), (0,)), ((), ())), preferred_element_type=f32),
        approximate=False,
    ).astype(bf16)
    block_part = lax.dot_general(
        hidden_t, w_out, (((0,), (0,)), ((), ())), preferred_element_type=f32
    ).astype(bf16)
    block = scatter_sum(block_part.reshape(col_count, row_block, D), COLS)
    picked = (
        jnp.arange(row_count)[None, :] == col_index * row_block + jnp.arange(row_block)[:, None]
    ).astype(bf16)
    own = lax.dot_general(picked, inputs_t, (((1,), (1,)), ((), ())), preferred_element_type=f32)
    resid = own + block
    center = jnp.mean(resid, axis=1, keepdims=True)
    spread = jnp.mean(resid * resid, axis=1, keepdims=True) - center * center
    final = (resid - center) * lax.rsqrt(spread + norm_eps) * gain_out[None, :]
    squared = jnp.sum(final * final, axis=1, keepdims=True)
    embed_part = (final * lax.rsqrt(squared + unit_eps)).astype(bf16)
    embed = gather_all(embed_part, COLS).reshape(row_count, D)

    proto_count = prototypes.shape[0]
    proto_f = prototypes.astype(f32)
    proto_len = jnp.sqrt(jnp.sum(proto_f * proto_f, axis=1) + unit_eps)
    unit = (proto_f / proto_len[:, None]).astype(bf16)
    proto_t = prototypes.T

    flat_scores = lax.dot_general(
        embed, unit, (((1,), (1,)), ((), ())), preferred_element_type=f32
    )
    scores = flat_scores.reshape(view_count, image_rows, proto_count)
    base = jnp.exp(scores / sink_temp)
    soft = jnp.exp(scores / soft_temp)
    soft_part = jnp.sum(soft, axis=2)
    scale_image = jnp.ones((view_count, image_rows), f32)
    scale_proto = jnp.ones((view_count, proto_count), f32)
    soft_total = scale_image
    for repeat in range(SINK_ITERS):
        proto_mass = sum_small(jnp.sum(base * scale_image[:, :, None], axis=1), ROWS)
        scale_proto = 1.0 / proto_mass
        image_part = jnp.sum(base * scale_proto[:, None, :], axis=2)
        if repeat == 0:
            image_mass, soft_total = sum_small(jnp.stack([image_part, soft_part]), COLS)
        else:
            image_mass = sum_small(image_part, COLS)
        scale_image = 1.0 / image_mass
    codes = base * scale_proto[:, None, :] * scale_image[:, :, None]
    prob = soft / soft_total[:, :, None]
    factor = 0.5 * math.sqrt(PROTOS * D)
    grad_scores = (factor * (prob - codes[::-1])).astype(bf16)
    grad_flat = grad_scores.reshape(row_count, proto_count)

    radial = jnp.sum(grad_scores.astype(f32) * scores, axis=(0, 1))
    direct = lax.dot_general(embed, grad_flat, (((0,), (0,)), ((), ())), preferred_element_type=f32)
    proto_part = (direct - proto_t.astype(f32) * (radial / proto_len)[None, :]) / proto_len[None, :]
    core = lax.axis_index("core")
    halves = proto_part.reshape(lax.axis_size("x"), 2, -1, proto_count)
    away = lax.dynamic_index_in_dim(halves, 1 - core, 1, False).astype(bf16)
    stay = lax.dynamic_index_in_dim(halves, core, 1, False)
    arrived = lax.ppermute(away, "core", [(0, 1), (1, 0)])
    paired = (stay + arrived.astype(f32)).astype(bf16)
    proto_grad = scatter_sum(paired, "x")

    embed_terms = lax.dot_general(
        unit, grad_flat, (((0,), (1,)), ((), ())), preferred_element_type=f32
    ).astype(bf16)
    embed_grad_t = scatter_sum(embed_terms.reshape(col_count, local_width, row_count), COLS)
    embed_grad = embed_grad_t.T.reshape(view_count, image_rows, local_width)
    return (embed_grad, proto_grad)


def solution(mesh):
    sizes = {"x": mesh.shape["rows"] // 2, "core": 2, "z": mesh.shape["cols"] // 4, "y": 4}
    fine = Mesh(mesh.devices.reshape(tuple(sizes.values())), tuple(sizes))
    placed = (
        P(None, ROWS, COLS),
        P(COLS),
        P(None, COLS),
        P(COLS, None),
        P(COLS),
        P(COLS, None),
    )
    return jax.shard_map(
        body,
        mesh=fine,
        in_specs=placed,
        out_specs=(P(None, ROWS, COLS), P(ROWS, COLS)),
        check_vma=False,
    )
```

```python
import math

import jax
import jax.numpy as jnp
from jax import lax
from jax.sharding import Mesh, PartitionSpec as P

D = 1024
PROTOS = 65536
SINK_ITERS = 3


sink_temp = 0.05
soft_temp = 0.1
norm_eps = 1e-05
unit_eps = 1e-06

ROWS = ("x", "core")
COLS = ("z", "y")
f32 = jnp.float32
bf16 = jnp.bfloat16


def gather_all(values, axes):
    count = lax.axis_size(axes)
    copies = jnp.broadcast_to(values[None], (count,) + values.shape)
    return lax.all_to_all(copies, axes, 0, 0)


def sum_small(values, axes):
    return jnp.sum(gather_all(values, axes), axis=0)


def scatter_sum(blocks, axes):
    return jnp.sum(lax.all_to_all(blocks, axes, 0, 0).astype(f32), axis=0)


def body(hidden_states, ln_in_gain, w_in, w_out, ln_out_gain, prototypes):
    view_count, image_rows, local_width = hidden_states.shape
    row_count = view_count * image_rows
    col_count = lax.axis_size(COLS)
    row_block = row_count // col_count

    y_count = lax.axis_size("y")
    z_count = lax.axis_size("z")
    tall = row_count // y_count

    states_t = hidden_states.reshape(row_count, local_width).T
    gain_row = jnp.pad(jnp.concatenate([ln_in_gain, ln_out_gain]), (0, tall - 2 * local_width))
    pieces = jnp.concatenate(
        [
            states_t.reshape(local_width, y_count, tall).transpose(1, 0, 2),
            jnp.broadcast_to(gain_row[None, None], (y_count, 8, tall)),
        ],
        axis=1,
    )
    sent = jnp.broadcast_to(pieces[None], (z_count,) + pieces.shape)
    received = lax.all_to_all(
        sent.reshape(col_count, local_width + 8, tall), COLS, 0, 0
    )
    gains = received[:, local_width]
    gain_in = gains[:, :local_width].reshape(D).astype(f32)
    gain_out = gains[:, local_width : 2 * local_width].reshape(D).astype(f32)
    inputs_t = received[:, :local_width].reshape(D, tall)

    turns = [[(i, (i + step) % y_count) for i in range(y_count)] for step in range(y_count)]
    first = [w_in] + [lax.ppermute(w_in, "y", turns[step]) for step in range(1, y_count)]
    second = [w_out] + [lax.ppermute(w_out, "y", turns[step]) for step in range(1, y_count)]

    inputs_f = inputs_t.astype(f32)
    center = jnp.mean(inputs_f, axis=0)
    spread = jnp.mean(inputs_f * inputs_f, axis=0) - center * center
    normed_t = (
        (inputs_f - center[None, :]) * lax.rsqrt(spread + norm_eps)[None, :] * gain_in[:, None]
    ).astype(bf16)
    block_part = jnp.zeros((tall, D), f32)
    for enter, leave in zip(first, second):
        hidden_t = jax.nn.gelu(
            lax.dot_general(enter, normed_t, (((0,), (0,)), ((), ())), preferred_element_type=f32),
            approximate=False,
        ).astype(bf16)
        block_part = block_part + lax.dot_general(
            hidden_t, leave, (((0,), (0,)), ((), ())), preferred_element_type=f32
        )
    block = scatter_sum(block_part.astype(bf16).reshape(z_count, row_block, D), "z")
    picked = (
        jnp.arange(tall)[None, :]
        == lax.axis_index("z") * row_block + jnp.arange(row_block)[:, None]
    ).astype(bf16)
    own = lax.dot_general(picked, inputs_t, (((1,), (1,)), ((), ())), preferred_element_type=f32)
    resid = own + block
    center = jnp.mean(resid, axis=1, keepdims=True)
    spread = jnp.mean(resid * resid, axis=1, keepdims=True) - center * center
    final = (resid - center) * lax.rsqrt(spread + norm_eps) * gain_out[None, :]
    squared = jnp.sum(final * final, axis=1, keepdims=True)
    embed_part = (final * lax.rsqrt(squared + unit_eps)).astype(bf16)
    embed = gather_all(embed_part, ("y", "z")).reshape(row_count, D)

    proto_count = prototypes.shape[0]
    proto_f = prototypes.astype(f32)
    proto_len = jnp.sqrt(jnp.sum(proto_f * proto_f, axis=1) + unit_eps)
    unit = (proto_f / proto_len[:, None]).astype(bf16)
    proto_t = prototypes.T

    flat_scores = lax.dot_general(
        embed, unit, (((1,), (1,)), ((), ())), preferred_element_type=f32
    )
    scores = flat_scores.reshape(view_count, image_rows, proto_count)
    base = jnp.exp(scores / sink_temp)
    soft = jnp.exp(scores / soft_temp)
    soft_part = jnp.sum(soft, axis=2)
    scale_image = jnp.ones((view_count, image_rows), f32)
    scale_proto = jnp.ones((view_count, proto_count), f32)
    soft_total = scale_image
    for repeat in range(SINK_ITERS):
        proto_mass = sum_small(jnp.sum(base * scale_image[:, :, None], axis=1), ROWS)
        scale_proto = 1.0 / proto_mass
        image_part = jnp.sum(base * scale_proto[:, None, :], axis=2)
        if repeat == 0:
            image_mass, soft_total = sum_small(jnp.stack([image_part, soft_part]), COLS)
        else:
            image_mass = sum_small(image_part, COLS)
        scale_image = 1.0 / image_mass
    codes = base * scale_proto[:, None, :] * scale_image[:, :, None]
    prob = soft / soft_total[:, :, None]
    factor = 0.5 * math.sqrt(PROTOS * D)
    grad_scores = (factor * (prob - codes[::-1])).astype(bf16)
    grad_flat = grad_scores.reshape(row_count, proto_count)

    radial = jnp.sum(grad_scores.astype(f32) * scores, axis=(0, 1))
    core = lax.axis_index("core")
    x_index = lax.axis_index("x")
    x_count = lax.axis_size("x")
    scaled = radial / proto_len

    def proto_part(side):
        left = lax.dynamic_index_in_dim(embed.reshape(row_count, x_count, 2, -1), side, 2, False)
        mine = lax.dynamic_index_in_dim(proto_t.reshape(x_count, 2, -1, proto_count), side, 1, False)
        direct = lax.dot_general(
            left.reshape(row_count, -1), grad_flat, (((0,), (0,)), ((), ())), preferred_element_type=f32
        )
        return (
            direct - mine.reshape(-1, proto_count).astype(f32) * scaled[None, :]
        ) / proto_len[None, :]

    away = proto_part(1 - core).astype(bf16)
    arrived = lax.ppermute(away, "core", [(0, 1), (1, 0)]).reshape(x_count, -1, proto_count)
    stay = proto_part(core).reshape(x_count, -1, proto_count)

    def paired(block):
        return lax.dynamic_index_in_dim(stay, block, 0, False) + lax.dynamic_index_in_dim(
            arrived, block, 0, False
        ).astype(f32)

    proto_grad = paired(x_index)
    for step in (2, 1, 3):
        moved = paired((x_index + step) % x_count).astype(bf16)
        turn = [(i, (i + step) % x_count) for i in range(x_count)]
        proto_grad = proto_grad + lax.ppermute(moved, "x", turn).astype(f32)

    embed_terms = lax.dot_general(
        unit, grad_flat, (((0,), (1,)), ((), ())), preferred_element_type=f32
    ).astype(bf16)
    embed_grad_t = scatter_sum(embed_terms.reshape(col_count, local_width, row_count), COLS)
    embed_grad = embed_grad_t.T.reshape(view_count, image_rows, local_width)
    return (embed_grad, proto_grad)


def solution(mesh):
    sizes = {"x": mesh.shape["rows"] // 2, "core": 2, "z": mesh.shape["cols"] // 4, "y": 4}
    fine = Mesh(mesh.devices.reshape(tuple(sizes.values())), tuple(sizes))
    placed = (
        P(None, ROWS, COLS),
        P(COLS),
        P(None, COLS),
        P(COLS, None),
        P(COLS),
        P(COLS, None),
    )
    return jax.shard_map(
        body,
        mesh=fine,
        in_specs=placed,
        out_specs=(P(None, ROWS, COLS), P(ROWS, COLS)),
        check_vma=False,
    )
```

```python
import math

import jax
import jax.numpy as jnp
from jax import lax
from jax.sharding import Mesh, PartitionSpec as P

D = 1024
PROTOS = 65536
SINK_ITERS = 3


sink_temp = 0.05
soft_temp = 0.1
norm_eps = 1e-05
unit_eps = 1e-06

ROWS = ("x", "core")
COLS = ("z", "y")
f32 = jnp.float32
bf16 = jnp.bfloat16


def gather_all(values, axes):
    count = lax.axis_size(axes)
    copies = jnp.broadcast_to(values[None], (count,) + values.shape)
    return lax.all_to_all(copies, axes, 0, 0)


def sum_small(values, axes):
    return jnp.sum(gather_all(values, axes), axis=0)


def scatter_sum(blocks, axes):
    return jnp.sum(lax.all_to_all(blocks, axes, 0, 0).astype(f32), axis=0)


def body(hidden_states, ln_in_gain, w_in, w_out, ln_out_gain, prototypes):
    view_count, image_rows, local_width = hidden_states.shape
    row_count = view_count * image_rows
    col_count = lax.axis_size(COLS)
    row_block = row_count // col_count

    y_count = lax.axis_size("y")
    z_count = lax.axis_size("z")
    tall = row_count // y_count

    states_t = hidden_states.reshape(row_count, local_width).T
    gain_row = jnp.pad(jnp.concatenate([ln_in_gain, ln_out_gain]), (0, tall - 2 * local_width))
    pieces = jnp.concatenate(
        [
            states_t.reshape(local_width, y_count, tall).transpose(1, 0, 2),
            jnp.broadcast_to(gain_row[None, None], (y_count, 8, tall)),
        ],
        axis=1,
    )
    sent = jnp.broadcast_to(pieces[None], (z_count,) + pieces.shape)
    received = lax.all_to_all(
        sent.reshape(col_count, local_width + 8, tall), COLS, 0, 0
    )
    gains = received[:, local_width]
    gain_in = gains[:, :local_width].reshape(D).astype(f32)
    gain_out = gains[:, local_width : 2 * local_width].reshape(D).astype(f32)
    inputs_t = received[:, :local_width].reshape(D, tall)

    core = lax.axis_index("core")
    swap = [(0, 1), (1, 0)]
    w_in_t = w_in.T
    share = jnp.where(core == 0, w_in_t, w_out)
    shares = jnp.stack(
        [
            lax.ppermute(share, "y", [(i, (i + step) % y_count) for i in range(y_count)])
            for step in range(1, y_count)
        ]
    )
    others = lax.ppermute(shares, "core", swap)
    first = [w_in_t] + list(jnp.where(core == 0, shares, others))
    second = [w_out] + list(jnp.where(core == 0, others, shares))

    inputs_f = inputs_t.astype(f32)
    center = jnp.mean(inputs_f, axis=0)
    spread = jnp.mean(inputs_f * inputs_f, axis=0) - center * center
    normed_t = (
        (inputs_f - center[None, :]) * lax.rsqrt(spread + norm_eps)[None, :] * gain_in[:, None]
    ).astype(bf16)
    block_part = jnp.zeros((tall, D), f32)
    for enter, leave in zip(first, second):
        hidden_t = jax.nn.gelu(
            jnp.dot(enter, normed_t, preferred_element_type=f32),
            approximate=False,
        ).astype(bf16)
        block_part = block_part + lax.dot_general(
            hidden_t, leave, (((0,), (0,)), ((), ())), preferred_element_type=f32
        )
    block = scatter_sum(block_part.astype(bf16).reshape(z_count, row_block, D), "z")
    picked = (
        jnp.arange(tall)[None, :]
        == lax.axis_index("z") * row_block + jnp.arange(row_block)[:, None]
    ).astype(bf16)
    own = lax.dot_general(picked, inputs_t, (((1,), (1,)), ((), ())), preferred_element_type=f32)
    resid = own + block
    center = jnp.mean(resid, axis=1, keepdims=True)
    spread = jnp.mean(resid * resid, axis=1, keepdims=True) - center * center
    final = (resid - center) * lax.rsqrt(spread + norm_eps) * gain_out[None, :]
    squared = jnp.sum(final * final, axis=1, keepdims=True)
    embed_part = (final * lax.rsqrt(squared + unit_eps)).astype(bf16)
    embed = gather_all(embed_part, ("y", "z")).reshape(row_count, D)

    proto_count = prototypes.shape[0]
    proto_f = prototypes.astype(f32)
    proto_len = jnp.sqrt(jnp.sum(proto_f * proto_f, axis=1) + unit_eps)
    unit = (proto_f / proto_len[:, None]).astype(bf16)
    slice_width = D // lax.axis_size(ROWS)
    proto_slice = (
        lax.dynamic_slice_in_dim(prototypes, lax.axis_index(ROWS) * slice_width, slice_width, 1).T
    ).astype(f32)

    flat_scores = lax.dot_general(
        embed, unit, (((1,), (1,)), ((), ())), preferred_element_type=f32
    )
    scores = flat_scores.reshape(view_count, image_rows, proto_count)
    base = jnp.exp(scores / sink_temp)
    soft = jnp.exp(scores / soft_temp)
    soft_part = jnp.sum(soft, axis=2)
    scale_image = jnp.ones((view_count, image_rows), f32)
    scale_proto = jnp.ones((view_count, proto_count), f32)
    soft_total = scale_image
    for repeat in range(SINK_ITERS):
        proto_mass = sum_small(jnp.sum(base * scale_image[:, :, None], axis=1), ROWS)
        scale_proto = 1.0 / proto_mass
        image_part = jnp.sum(base * scale_proto[:, None, :], axis=2)
        if repeat == 0:
            image_mass, soft_total = sum_small(jnp.stack([image_part, soft_part]), COLS)
        else:
            image_mass = sum_small(image_part, COLS)
        scale_image = 1.0 / image_mass
    codes = base * scale_proto[:, None, :] * scale_image[:, :, None]
    prob = soft / soft_total[:, :, None]
    factor = 0.5 * math.sqrt(PROTOS * D)
    grad_scores = (factor * (prob - codes[::-1])).astype(bf16)
    grad_flat = grad_scores.reshape(row_count, proto_count)

    x_index = lax.axis_index("x")
    x_count = lax.axis_size("x")
    x_turns = {
        step: [(i, (i + step) % x_count) for i in range(x_count)] for step in range(1, x_count)
    }

    def half(side):
        left = lax.dynamic_index_in_dim(embed.reshape(row_count, x_count, 2, -1), side, 2, False)
        return lax.dot_general(
            left.reshape(row_count, -1), grad_flat, (((0,), (0,)), ((), ())), preferred_element_type=f32
        ).reshape(x_count, slice_width, proto_count)

    away = half(1 - core).astype(bf16)
    arrived = lax.ppermute(away, "core", swap)
    stay = half(core)

    def paired(block):
        return lax.dynamic_index_in_dim(stay, block, 0, False) + lax.dynamic_index_in_dim(
            arrived, block, 0, False
        ).astype(f32)

    moved = {step: paired((x_index + step) % x_count).astype(bf16) for step in (2, 1, 3)}
    moved, grad_later = lax.optimization_barrier((moved, grad_flat))
    direct = paired(x_index)
    for step in (2, 1, 3):
        direct = direct + lax.ppermute(moved[step], "x", x_turns[step]).astype(f32)

    radial = jnp.sum(grad_scores.astype(f32) * scores, axis=(0, 1))
    radial = radial + lax.ppermute(radial, "core", swap)
    radial = radial + sum(lax.ppermute(radial, "x", x_turns[step]) for step in (2, 1, 3))
    proto_grad = (direct - proto_slice * (radial / proto_len)[None, :]) / proto_len[None, :]

    embed_terms = lax.dot_general(
        unit, grad_later, (((0,), (1,)), ((), ())), preferred_element_type=f32
    ).astype(bf16)
    embed_grad_t = scatter_sum(embed_terms.reshape(col_count, local_width, row_count), COLS)
    embed_grad = embed_grad_t.T.reshape(view_count, image_rows, local_width)
    return (embed_grad, proto_grad)


def solution(mesh):
    sizes = {"x": mesh.shape["rows"] // 2, "core": 2, "z": mesh.shape["cols"] // 4, "y": 4}
    fine = Mesh(mesh.devices.reshape(tuple(sizes.values())), tuple(sizes))
    placed = (
        P(None, ROWS, COLS),
        P(COLS),
        P(None, COLS),
        P(COLS, None),
        P(COLS),
        P(COLS, None),
    )
    return jax.shard_map(
        body,
        mesh=fine,
        in_specs=placed,
        out_specs=(P(None, ROWS, COLS), P(ROWS, COLS)),
        check_vma=False,
    )
```

```python
import functools
import math

import jax
import jax.numpy as jnp
from jax import lax
from jax.experimental import pallas as pl
from jax.experimental.pallas import tpu as pltpu
from jax.sharding import Mesh, PartitionSpec as P

D = 1024
PROTOS = 65536
SINK_ITERS = 3


sink_temp = 0.05
soft_temp = 0.1
norm_eps = 1e-05
unit_eps = 1e-06

ROWS = ("x", "core")
COLS = ("z", "y")
f32 = jnp.float32
bf16 = jnp.bfloat16


def gather_all(values, axes):
    count = lax.axis_size(axes)
    copies = jnp.broadcast_to(values[None], (count,) + values.shape)
    return lax.all_to_all(copies, axes, 0, 0)


def sum_small(values, axes):
    return jnp.sum(gather_all(values, axes), axis=0)


def scatter_sum(blocks, axes):
    return jnp.sum(lax.all_to_all(blocks, axes, 0, 0).astype(f32), axis=0)


TILE = 512
LANES = 128
factor = 0.5 * math.sqrt(PROTOS * D)
NT = (((1,), (1,)), ((), ()))


def params():
    return pltpu.CompilerParams(
        dimension_semantics=("arbitrary",), vmem_limit_bytes=32 * 1024 * 1024
    )


def whole(shape):
    return pl.BlockSpec(shape, lambda i: (0,) * len(shape))


def cost(flops, bytes_accessed, transcendentals=0):
    return pl.CostEstimate(
        flops=flops, bytes_accessed=bytes_accessed, transcendentals=transcendentals
    )


def fold_lanes(values):
    width = values.shape[1]
    return sum(values[:, j : j + LANES] for j in range(0, width, LANES))


def as_column(row):
    return jnp.broadcast_to(row, (LANES, row.shape[1])).T


def spread_lanes(column, width):
    return jnp.concatenate([column] * (width // LANES), axis=1)


def view_rows(pair, count):
    half = count // 2
    width = pair.shape[1]
    return jnp.concatenate(
        [jnp.broadcast_to(pair[v : v + 1], (half, width)) for v in range(2)], axis=0
    )


def view_sums(values):
    half = values.shape[0] // 2
    return jnp.concatenate(
        [jnp.sum(values[v * half : (v + 1) * half], axis=0, keepdims=True) for v in range(2)],
        axis=0,
    )


def accumulate(total, part):
    @pl.when(pl.program_id(0) == 0)
    def _():
        total[...] = part

    @pl.when(pl.program_id(0) > 0)
    def _():
        total[...] += part


def ffn_kernel(core_ref, normed_ref, w_in_ref, w_out_ref, shares_ref, others_ref, out_ref):
    normed = normed_ref[...]
    even = core_ref[0] == 0
    total = jnp.zeros(out_ref.shape, f32)
    for step in range(shares_ref.shape[0] + 1):
        if step == 0:
            enter, leave = w_in_ref[...], w_out_ref[...]
        else:
            one, other = shares_ref[step - 1], others_ref[step - 1]
            enter, leave = jnp.where(even, one, other), jnp.where(even, other, one)
        wide = lax.dot_general(normed, enter, NT, preferred_element_type=f32)
        hidden = (0.5 * wide * (1.0 + lax.erf(wide * math.sqrt(0.5)))).astype(bf16)
        total = total + jnp.dot(hidden, leave, preferred_element_type=f32)
    out_ref[...] = total.astype(bf16)


def feed_forward(core, normed, w_in_t, w_out, shares, others):
    rows = normed.shape[0]
    arrays = (normed, w_in_t, w_out, shares, others)
    return pl.pallas_call(
        ffn_kernel,
        grid=(1,),
        in_specs=[pl.BlockSpec(memory_space=pltpu.SMEM)] + [whole(a.shape) for a in arrays],
        out_specs=whole((rows, D)),
        out_shape=jax.ShapeDtypeStruct((rows, D), bf16),
        compiler_params=params(),
        cost_estimate=cost(4 * rows * D * 4 * w_out.shape[0], 8 * w_out.size),
    )(core.reshape(1), *arrays)


def scores_kernel(copies, embed_ref, unit_ref, scores_ref, base_ref, mass_ref, soft_ref, total):
    scores = lax.dot_general(embed_ref[...], unit_ref[...], NT, preferred_element_type=f32)
    scores_ref[...] = scores
    soft = jnp.exp(scores * (1.0 / soft_temp))
    base = soft * soft
    base_ref[...] = base.astype(bf16)
    mass = view_sums(base)
    mass_ref[...] = jnp.broadcast_to(mass[None], (copies,) + mass.shape)
    accumulate(total, fold_lanes(soft))

    @pl.when(pl.program_id(0) == pl.num_programs(0) - 1)
    def _():
        soft_ref[...] = jnp.sum(total[...].T, axis=0, keepdims=True)


def score_pass(embed, unit, copies):
    rows, protos = embed.shape[0], unit.shape[0]
    return pl.pallas_call(
        functools.partial(scores_kernel, copies),
        grid=(protos // TILE,),
        in_specs=[whole(embed.shape), pl.BlockSpec((TILE, D), lambda i: (i, 0))],
        out_specs=[
            pl.BlockSpec((rows, TILE), lambda i: (0, i)),
            pl.BlockSpec((rows, TILE), lambda i: (0, i)),
            pl.BlockSpec((copies, 2, TILE), lambda i: (0, 0, i)),
            whole((1, rows)),
        ],
        out_shape=[
            jax.ShapeDtypeStruct((rows, protos), f32),
            jax.ShapeDtypeStruct((rows, protos), bf16),
            jax.ShapeDtypeStruct((copies, 2, protos), f32),
            jax.ShapeDtypeStruct((1, rows), f32),
        ],
        scratch_shapes=[pltpu.VMEM((rows, LANES), f32)],
        compiler_params=params(),
        cost_estimate=cost(2 * rows * protos * D, 14 * rows * protos, rows * protos),
    )(embed, unit)


def image_kernel(copies, mass_ref, base_ref, *rest):
    *extra, out_ref, total = rest
    scale = 1.0 / jnp.sum(mass_ref[...], axis=0)
    values = base_ref[...].astype(f32) * view_rows(scale, base_ref.shape[0])
    accumulate(total, fold_lanes(values))

    @pl.when(pl.program_id(0) == pl.num_programs(0) - 1)
    def _():
        row = jnp.sum(total[...].T, axis=0, keepdims=True)
        row = jnp.concatenate([row] + [ref[...] for ref in extra], axis=0)
        out_ref[...] = jnp.broadcast_to(row[None], (copies,) + row.shape)


def image_pass(masses, base, copies, *extra):
    rows, protos = base.shape
    out = (copies, 1 + len(extra), rows)
    return pl.pallas_call(
        functools.partial(image_kernel, copies),
        grid=(protos // TILE,),
        in_specs=[
            pl.BlockSpec((masses.shape[0], 2, TILE), lambda i: (0, 0, i)),
            pl.BlockSpec((rows, TILE), lambda i: (0, i)),
        ]
        + [whole(e.shape) for e in extra],
        out_specs=whole(out),
        out_shape=jax.ShapeDtypeStruct(out, f32),
        scratch_shapes=[pltpu.VMEM((rows, LANES), f32)],
        compiler_params=params(),
        cost_estimate=cost(3 * rows * protos, 2 * rows * protos),
    )(masses, base, *extra)


def proto_kernel(copies, image_ref, base_ref, mass_ref, column):
    @pl.when(pl.program_id(0) == 0)
    def _():
        column[...] = as_column(1.0 / jnp.sum(image_ref[...], axis=0)[:1])

    values = base_ref[...].astype(f32) * spread_lanes(column[...], base_ref.shape[1])
    mass = view_sums(values)
    mass_ref[...] = jnp.broadcast_to(mass[None], (copies,) + mass.shape)


def proto_pass(images, base, copies):
    rows, protos = base.shape
    return pl.pallas_call(
        functools.partial(proto_kernel, copies),
        grid=(protos // TILE,),
        in_specs=[whole(images.shape), pl.BlockSpec((rows, TILE), lambda i: (0, i))],
        out_specs=pl.BlockSpec((copies, 2, TILE), lambda i: (0, 0, i)),
        out_shape=jax.ShapeDtypeStruct((copies, 2, protos), f32),
        scratch_shapes=[pltpu.VMEM((rows, LANES), f32)],
        compiler_params=params(),
        cost_estimate=cost(3 * rows * protos, 2 * rows * protos),
    )(images, base)


def grad_kernel(
    image_ref, soft_ref, mass_ref, scores_ref, away_t_ref, stay_t_ref,
    grad_ref, radial_ref, away_ref, stay_ref, code_column, prob_column,
):
    @pl.when(pl.program_id(0) == 0)
    def _():
        code_column[...] = as_column(factor / jnp.sum(image_ref[...], axis=0)[:1])
        prob_column[...] = as_column(factor / jnp.sum(soft_ref[...], axis=0)[1:2])

    scores = scores_ref[...]
    rows, width = scores.shape
    half = rows // 2
    soft = jnp.exp(scores * (1.0 / soft_temp))
    scale = 1.0 / jnp.sum(mass_ref[...], axis=0)
    codes = (
        soft * soft * view_rows(scale, rows) * spread_lanes(code_column[...], width)
    )
    swapped = jnp.concatenate([codes[half:], codes[:half]], axis=0)
    grad = (soft * spread_lanes(prob_column[...], width) - swapped).astype(bf16)
    grad_ref[...] = grad
    radial_ref[...] = jnp.sum(grad.astype(f32) * scores, axis=0, keepdims=True)
    away_ref[...] = jnp.dot(away_t_ref[...], grad, preferred_element_type=f32).astype(bf16)
    stay_ref[...] = jnp.dot(stay_t_ref[...], grad, preferred_element_type=f32)


def grad_pass(images, softs, masses, scores, away_t, stay_t):
    rows, protos = scores.shape
    depth = away_t.shape[0]

    def tile(height):
        return pl.BlockSpec((height, TILE), lambda i: (0, i))

    return pl.pallas_call(
        grad_kernel,
        grid=(protos // TILE,),
        in_specs=[
            whole(images.shape),
            whole(softs.shape),
            pl.BlockSpec((masses.shape[0], 2, TILE), lambda i: (0, 0, i)),
            tile(rows),
            whole(away_t.shape),
            whole(stay_t.shape),
        ],
        out_specs=[tile(rows), tile(1), tile(depth), tile(depth)],
        out_shape=[
            jax.ShapeDtypeStruct((rows, protos), bf16),
            jax.ShapeDtypeStruct((1, protos), f32),
            jax.ShapeDtypeStruct((depth, protos), bf16),
            jax.ShapeDtypeStruct((depth, protos), f32),
        ],
        scratch_shapes=[pltpu.VMEM((rows, LANES), f32)] * 2,
        compiler_params=params(),
        cost_estimate=cost(4 * depth * rows * protos, 12 * rows * protos, rows * protos),
    )(images, softs, masses, scores, away_t, stay_t)


def body(hidden_states, ln_in_gain, w_in, w_out, ln_out_gain, prototypes):
    view_count, image_rows, local_width = hidden_states.shape
    row_count = view_count * image_rows
    col_count = lax.axis_size(COLS)
    row_block = row_count // col_count

    y_count = lax.axis_size("y")
    z_count = lax.axis_size("z")
    tall = row_count // y_count

    states_t = hidden_states.reshape(row_count, local_width).T
    gain_row = jnp.pad(jnp.concatenate([ln_in_gain, ln_out_gain]), (0, tall - 2 * local_width))
    pieces = jnp.concatenate(
        [
            states_t.reshape(local_width, y_count, tall).transpose(1, 0, 2),
            jnp.broadcast_to(gain_row[None, None], (y_count, 8, tall)),
        ],
        axis=1,
    )
    sent = jnp.broadcast_to(pieces[None], (z_count,) + pieces.shape)
    received = lax.all_to_all(
        sent.reshape(col_count, local_width + 8, tall), COLS, 0, 0
    )
    gains = received[:, local_width]
    gain_in = gains[:, :local_width].reshape(D).astype(f32)
    gain_out = gains[:, local_width : 2 * local_width].reshape(D).astype(f32)
    inputs_t = received[:, :local_width].reshape(D, tall)

    core = lax.axis_index("core")
    swap = [(0, 1), (1, 0)]
    w_in_t = w_in.T
    share = jnp.where(core == 0, w_in_t, w_out)
    shares = jnp.stack(
        [
            lax.ppermute(share, "y", [(i, (i + step) % y_count) for i in range(y_count)])
            for step in range(1, y_count)
        ]
    )
    others = lax.ppermute(shares, "core", swap)

    inputs_f = inputs_t.astype(f32)
    center = jnp.mean(inputs_f, axis=0)
    spread = jnp.mean(inputs_f * inputs_f, axis=0) - center * center
    normed_t = (
        (inputs_f - center[None, :]) * lax.rsqrt(spread + norm_eps)[None, :] * gain_in[:, None]
    ).astype(bf16)
    block_part = feed_forward(core, normed_t.T, w_in_t, w_out, shares, others)
    block = scatter_sum(block_part.reshape(z_count, row_block, D), "z")
    picked = (
        jnp.arange(tall)[None, :]
        == lax.axis_index("z") * row_block + jnp.arange(row_block)[:, None]
    ).astype(bf16)
    own = lax.dot_general(picked, inputs_t, (((1,), (1,)), ((), ())), preferred_element_type=f32)
    resid = own + block
    center = jnp.mean(resid, axis=1, keepdims=True)
    spread = jnp.mean(resid * resid, axis=1, keepdims=True) - center * center
    final = (resid - center) * lax.rsqrt(spread + norm_eps) * gain_out[None, :]
    squared = jnp.sum(final * final, axis=1, keepdims=True)
    embed_part = (final * lax.rsqrt(squared + unit_eps)).astype(bf16)
    embed = gather_all(embed_part, ("y", "z")).reshape(row_count, D)

    proto_count = prototypes.shape[0]
    proto_f = prototypes.astype(f32)
    proto_len = jnp.sqrt(jnp.sum(proto_f * proto_f, axis=1) + unit_eps)
    unit = (proto_f / proto_len[:, None]).astype(bf16)
    slice_width = D // lax.axis_size(ROWS)
    proto_slice = (
        lax.dynamic_slice_in_dim(prototypes, lax.axis_index(ROWS) * slice_width, slice_width, 1).T
    ).astype(f32)

    row_parts = lax.axis_size(ROWS)
    scores, base, masses, soft_part = score_pass(embed, unit, row_parts)
    masses = lax.all_to_all(masses, ROWS, 0, 0)
    softs = images = lax.all_to_all(image_pass(masses, base, col_count, soft_part), COLS, 0, 0)
    for repeat in range(1, SINK_ITERS):
        masses = lax.all_to_all(proto_pass(images, base, row_parts), ROWS, 0, 0)
        images = lax.all_to_all(image_pass(masses, base, col_count), COLS, 0, 0)

    x_index = lax.axis_index("x")
    x_count = lax.axis_size("x")
    x_turns = {
        step: [(i, (i + step) % x_count) for i in range(x_count)] for step in range(1, x_count)
    }
    embed_t = embed.T.reshape(x_count, 2, slice_width, row_count)
    away_t, stay_t = (
        lax.dynamic_index_in_dim(embed_t, side, 1, False).reshape(-1, row_count)
        for side in (1 - core, core)
    )
    grad_flat, radial, away, stay = grad_pass(images, softs, masses, scores, away_t, stay_t)
    arrived = lax.ppermute(away, "core", swap).reshape(x_count, slice_width, proto_count)
    stay = stay.reshape(x_count, slice_width, proto_count)

    def paired(block):
        return lax.dynamic_index_in_dim(stay, block, 0, False) + lax.dynamic_index_in_dim(
            arrived, block, 0, False
        ).astype(f32)

    moved = {step: paired((x_index + step) % x_count).astype(bf16) for step in (2, 1, 3)}
    moved, grad_later = lax.optimization_barrier((moved, grad_flat))
    direct = paired(x_index)
    for step in (2, 1, 3):
        direct = direct + lax.ppermute(moved[step], "x", x_turns[step]).astype(f32)

    radial = radial[0]
    radial = radial + lax.ppermute(radial, "core", swap)
    radial = radial + sum(lax.ppermute(radial, "x", x_turns[step]) for step in (2, 1, 3))
    proto_grad = (direct - proto_slice * (radial / proto_len)[None, :]) / proto_len[None, :]

    embed_terms = lax.dot_general(
        unit, grad_later, (((0,), (1,)), ((), ())), preferred_element_type=f32
    ).astype(bf16)
    embed_grad_t = scatter_sum(embed_terms.reshape(col_count, local_width, row_count), COLS)
    embed_grad = embed_grad_t.T.reshape(view_count, image_rows, local_width)
    return (embed_grad, proto_grad)


def solution(mesh):
    sizes = {"x": mesh.shape["rows"] // 2, "core": 2, "z": mesh.shape["cols"] // 4, "y": 4}
    fine = Mesh(mesh.devices.reshape(tuple(sizes.values())), tuple(sizes))
    placed = (
        P(None, ROWS, COLS),
        P(COLS),
        P(None, COLS),
        P(COLS, None),
        P(COLS),
        P(COLS, None),
    )
    return jax.shard_map(
        body,
        mesh=fine,
        in_specs=placed,
        out_specs=(P(None, ROWS, COLS), P(ROWS, COLS)),
        check_vma=False,
    )
```

```python
import functools
import math

import jax
import jax.numpy as jnp
from jax import lax
from jax.experimental import pallas as pl
from jax.experimental.pallas import tpu as pltpu
from jax.sharding import Mesh, PartitionSpec as P

D = 1024
PROTOS = 65536
SINK_ITERS = 3


sink_temp = 0.05
soft_temp = 0.1
norm_eps = 1e-05
unit_eps = 1e-06

ROWS = ("x", "core")
COLS = ("z", "y")
f32 = jnp.float32
bf16 = jnp.bfloat16


def gather_all(values, axes):
    count = lax.axis_size(axes)
    copies = jnp.broadcast_to(values[None], (count,) + values.shape)
    return lax.all_to_all(copies, axes, 0, 0)


def sum_small(values, axes):
    return jnp.sum(gather_all(values, axes), axis=0)


def scatter_sum(blocks, axes):
    return jnp.sum(lax.all_to_all(blocks, axes, 0, 0).astype(f32), axis=0)


TILE = 512
LANES = 128
factor = 0.5 * math.sqrt(PROTOS * D)
NT = (((1,), (1,)), ((), ()))


def params(mib):
    return pltpu.CompilerParams(
        dimension_semantics=("arbitrary",), vmem_limit_bytes=mib * 1024 * 1024
    )


def whole(shape):
    return pl.BlockSpec(shape, lambda i: (0,) * len(shape))


def cost(flops, bytes_accessed, transcendentals=0):
    return pl.CostEstimate(
        flops=flops, bytes_accessed=bytes_accessed, transcendentals=transcendentals
    )


def fold_lanes(values):
    width = values.shape[1]
    return sum(values[:, j : j + LANES] for j in range(0, width, LANES))


def as_column(row):
    return jnp.broadcast_to(row, (LANES, row.shape[1])).T


def spread_lanes(column, width):
    return jnp.concatenate([column] * (width // LANES), axis=1)


def view_rows(pair, count):
    half = count // 2
    width = pair.shape[1]
    return jnp.concatenate(
        [jnp.broadcast_to(pair[v : v + 1], (half, width)) for v in range(2)], axis=0
    )


def view_sums(values):
    half = values.shape[0] // 2
    return jnp.concatenate(
        [jnp.sum(values[v * half : (v + 1) * half], axis=0, keepdims=True) for v in range(2)],
        axis=0,
    )


def accumulate(total, part):
    @pl.when(pl.program_id(0) == 0)
    def _():
        total[...] = part

    @pl.when(pl.program_id(0) > 0)
    def _():
        total[...] += part


def stack_kernel(first_ref, second_ref, third_ref, out_ref):
    for place, ref in enumerate((first_ref, second_ref, third_ref)):
        out_ref[place] = ref[...]


def stack_shares(parts):
    shape = parts[0].shape
    return pl.pallas_call(
        stack_kernel,
        grid=(1,),
        in_specs=[whole(shape)] * 3,
        out_specs=whole((3,) + shape),
        out_shape=jax.ShapeDtypeStruct((3,) + shape, bf16),
        compiler_params=params(6),
        cost_estimate=cost(40 * 10**9, 4 * parts[0].size),
    )(*parts)


def ffn_kernel(core_ref, normed_ref, w_in_ref, w_out_ref, shares_ref, others_ref, out_ref):
    normed = normed_ref[...]
    even = core_ref[0] == 0
    total = jnp.zeros(out_ref.shape, f32)
    for step in range(shares_ref.shape[0] + 1):
        if step == 0:
            enter, leave = w_in_ref[...], w_out_ref[...]
        else:
            one, other = shares_ref[step - 1], others_ref[step - 1]
            enter, leave = jnp.where(even, one, other), jnp.where(even, other, one)
        wide = lax.dot_general(normed, enter, NT, preferred_element_type=f32)
        hidden = (0.5 * wide * (1.0 + lax.erf(wide * math.sqrt(0.5)))).astype(bf16)
        total = total + jnp.dot(hidden, leave, preferred_element_type=f32)
    out_ref[...] = total.astype(bf16)


def feed_forward(core, normed, w_in_t, w_out, shares, others):
    rows = normed.shape[0]
    arrays = (normed, w_in_t, w_out, shares, others)
    return pl.pallas_call(
        ffn_kernel,
        grid=(1,),
        in_specs=[pl.BlockSpec(memory_space=pltpu.SMEM)] + [whole(a.shape) for a in arrays],
        out_specs=whole((rows, D)),
        out_shape=jax.ShapeDtypeStruct((rows, D), bf16),
        compiler_params=params(8),
        cost_estimate=cost(4 * rows * D * 4 * w_out.shape[0], 8 * w_out.size),
    )(core.reshape(1), *arrays)


def prepare_kernel(core_ref, proto_ref, unit_ref, length_ref, turned_ref):
    values = proto_ref[...].astype(f32)
    squares = values * values
    inverse = lax.rsqrt(jnp.sum(squares, axis=1, keepdims=True) + unit_eps)
    unit_ref[...] = (values * inverse).astype(bf16)
    length_ref[...] = jnp.sqrt(
        jnp.sum(fold_lanes(squares).T, axis=0, keepdims=True) + unit_eps
    )
    even = core_ref[0] == 0
    for block in range(turned_ref.shape[0]):
        start = 2 * block * LANES
        picked = jnp.where(
            even, values[:, start : start + LANES], values[:, start + LANES : start + 2 * LANES]
        )
        turned_ref[block] = picked.T.astype(bf16)


def prepare(core, prototypes, x_count):
    protos = prototypes.shape[0]
    return pl.pallas_call(
        prepare_kernel,
        grid=(protos // TILE,),
        in_specs=[
            pl.BlockSpec(memory_space=pltpu.SMEM),
            pl.BlockSpec((TILE, D), lambda i: (i, 0)),
        ],
        out_specs=[
            pl.BlockSpec((TILE, D), lambda i: (i, 0)),
            pl.BlockSpec((1, TILE), lambda i: (0, i)),
            pl.BlockSpec((x_count, LANES, TILE), lambda i: (0, 0, i)),
        ],
        out_shape=[
            jax.ShapeDtypeStruct((protos, D), bf16),
            jax.ShapeDtypeStruct((1, protos), f32),
            jax.ShapeDtypeStruct((x_count, LANES, protos), bf16),
        ],
        compiler_params=params(18),
        cost_estimate=cost(6 * protos * D, 5 * protos * D),
    )(core.reshape(1), prototypes)


def scores_kernel(copies, embed_ref, unit_ref, scores_ref, base_ref, mass_ref, soft_ref, total):
    scores = lax.dot_general(embed_ref[...], unit_ref[...], NT, preferred_element_type=f32)
    scores_ref[...] = scores
    soft = jnp.exp(scores * (1.0 / soft_temp))
    base = soft * soft
    base_ref[...] = base.astype(bf16)
    mass = view_sums(base)
    mass_ref[...] = jnp.broadcast_to(mass[None], (copies,) + mass.shape)
    accumulate(total, fold_lanes(soft))

    @pl.when(pl.program_id(0) == pl.num_programs(0) - 1)
    def _():
        soft_ref[...] = jnp.sum(total[...].T, axis=0, keepdims=True)


def score_pass(embed, unit, copies):
    rows, protos = embed.shape[0], unit.shape[0]
    return pl.pallas_call(
        functools.partial(scores_kernel, copies),
        grid=(protos // TILE,),
        in_specs=[whole(embed.shape), pl.BlockSpec((TILE, D), lambda i: (i, 0))],
        out_specs=[
            pl.BlockSpec((rows, TILE), lambda i: (0, i)),
            pl.BlockSpec((rows, TILE), lambda i: (0, i)),
            pl.BlockSpec((copies, 2, TILE), lambda i: (0, 0, i)),
            whole((1, rows)),
        ],
        out_shape=[
            jax.ShapeDtypeStruct((rows, protos), f32),
            jax.ShapeDtypeStruct((rows, protos), bf16),
            jax.ShapeDtypeStruct((copies, 2, protos), f32),
            jax.ShapeDtypeStruct((1, rows), f32),
        ],
        scratch_shapes=[pltpu.VMEM((rows, LANES), f32)],
        compiler_params=params(18),
        cost_estimate=cost(2 * rows * protos * D, 14 * rows * protos, rows * protos),
    )(embed, unit)


def image_kernel(copies, mass_ref, base_ref, *rest):
    *extra, out_ref, total = rest
    scale = 1.0 / jnp.sum(mass_ref[...], axis=0)
    values = base_ref[...].astype(f32) * view_rows(scale, base_ref.shape[0])
    accumulate(total, fold_lanes(values))

    @pl.when(pl.program_id(0) == pl.num_programs(0) - 1)
    def _():
        row = jnp.sum(total[...].T, axis=0, keepdims=True)
        row = jnp.concatenate([row] + [ref[...] for ref in extra], axis=0)
        out_ref[...] = jnp.broadcast_to(row[None], (copies,) + row.shape)


def image_pass(masses, base, copies, *extra):
    rows, protos = base.shape
    out = (copies, 1 + len(extra), rows)
    return pl.pallas_call(
        functools.partial(image_kernel, copies),
        grid=(protos // TILE,),
        in_specs=[
            pl.BlockSpec((masses.shape[0], 2, TILE), lambda i: (0, 0, i)),
            pl.BlockSpec((rows, TILE), lambda i: (0, i)),
        ]
        + [whole(e.shape) for e in extra],
        out_specs=whole(out),
        out_shape=jax.ShapeDtypeStruct(out, f32),
        scratch_shapes=[pltpu.VMEM((rows, LANES), f32)],
        compiler_params=params(10),
        cost_estimate=cost(3 * rows * protos, 2 * rows * protos),
    )(masses, base, *extra)


def proto_kernel(copies, image_ref, base_ref, mass_ref, column):
    @pl.when(pl.program_id(0) == 0)
    def _():
        column[...] = as_column(1.0 / jnp.sum(image_ref[...], axis=0)[:1])

    values = base_ref[...].astype(f32) * spread_lanes(column[...], base_ref.shape[1])
    mass = view_sums(values)
    mass_ref[...] = jnp.broadcast_to(mass[None], (copies,) + mass.shape)


def proto_pass(images, base, copies):
    rows, protos = base.shape
    return pl.pallas_call(
        functools.partial(proto_kernel, copies),
        grid=(protos // TILE,),
        in_specs=[whole(images.shape), pl.BlockSpec((rows, TILE), lambda i: (0, i))],
        out_specs=pl.BlockSpec((copies, 2, TILE), lambda i: (0, 0, i)),
        out_shape=jax.ShapeDtypeStruct((copies, 2, protos), f32),
        scratch_shapes=[pltpu.VMEM((rows, LANES), f32)],
        compiler_params=params(10),
        cost_estimate=cost(3 * rows * protos, 2 * rows * protos),
    )(images, base)


def grad_kernel(
    image_ref, soft_ref, mass_ref, scores_ref, away_t_ref, stay_t_ref,
    grad_ref, radial_ref, away_ref, stay_ref, code_column, prob_column,
):
    @pl.when(pl.program_id(0) == 0)
    def _():
        code_column[...] = as_column(factor / jnp.sum(image_ref[...], axis=0)[:1])
        prob_column[...] = as_column(factor / jnp.sum(soft_ref[...], axis=0)[1:2])

    scores = scores_ref[...]
    rows, width = scores.shape
    half = rows // 2
    soft = jnp.exp(scores * (1.0 / soft_temp))
    scale = 1.0 / jnp.sum(mass_ref[...], axis=0)
    codes = (
        soft * soft * view_rows(scale, rows) * spread_lanes(code_column[...], width)
    )
    swapped = jnp.concatenate([codes[half:], codes[:half]], axis=0)
    grad = (soft * spread_lanes(prob_column[...], width) - swapped).astype(bf16)
    grad_ref[...] = grad
    radial_ref[...] = jnp.sum(grad.astype(f32) * scores, axis=0, keepdims=True)
    away_ref[...] = jnp.dot(away_t_ref[...], grad, preferred_element_type=f32).astype(bf16)
    stay_ref[...] = jnp.dot(stay_t_ref[...], grad, preferred_element_type=f32)


def grad_pass(images, softs, masses, scores, away_t, stay_t):
    rows, protos = scores.shape
    depth = away_t.shape[0]

    def tile(height):
        return pl.BlockSpec((height, TILE), lambda i: (0, i))

    return pl.pallas_call(
        grad_kernel,
        grid=(protos // TILE,),
        in_specs=[
            whole(images.shape),
            whole(softs.shape),
            pl.BlockSpec((masses.shape[0], 2, TILE), lambda i: (0, 0, i)),
            tile(rows),
            whole(away_t.shape),
            whole(stay_t.shape),
        ],
        out_specs=[tile(rows), tile(1), tile(depth), tile(depth)],
        out_shape=[
            jax.ShapeDtypeStruct((rows, protos), bf16),
            jax.ShapeDtypeStruct((1, protos), f32),
            jax.ShapeDtypeStruct((depth, protos), bf16),
            jax.ShapeDtypeStruct((depth, protos), f32),
        ],
        scratch_shapes=[pltpu.VMEM((rows, LANES), f32)] * 2,
        compiler_params=params(20),
        cost_estimate=cost(4 * depth * rows * protos, 12 * rows * protos, rows * protos),
    )(images, softs, masses, scores, away_t, stay_t)


def pair(stay, arrived, turned, radials, length):
    radial = radials[0] + radials[1]
    inverse = 1.0 / length
    return (stay + arrived.astype(f32) - turned.astype(f32) * (radial * inverse)) * inverse


def pair_kernel(place_ref, stay_ref, arrived_ref, turned_ref, one_ref, two_ref, length_ref, out_ref):
    out_ref[...] = pair(
        stay_ref[0], arrived_ref[0], turned_ref[0], (one_ref[...], two_ref[...]), length_ref[...]
    ).astype(bf16)


def final_kernel(
    place_ref, stay_ref, arrived_ref, turned_ref, one_ref, two_ref, length_ref, *rest
):
    *others, out_ref = rest
    total = pair(
        stay_ref[0], arrived_ref[0], turned_ref[0], (one_ref[...], two_ref[...]), length_ref[...]
    )
    for ref in others:
        total = total + ref[...].astype(f32)
    out_ref[...] = total


def pair_call(place, stay, arrived, turned, radials, length, others=()):
    blocks, height, protos = stay.shape
    wide = 2 * TILE
    picked = pl.BlockSpec((1, height, wide), lambda i, p: (p[0], 0, i))
    line = pl.BlockSpec((1, wide), lambda i, p: (0, i))
    flat = pl.BlockSpec((height, wide), lambda i, p: (0, i))
    return pl.pallas_call(
        final_kernel if others else pair_kernel,
        grid_spec=pltpu.PrefetchScalarGridSpec(
            num_scalar_prefetch=1,
            grid=(protos // wide,),
            in_specs=[picked] * 3 + [line] * 3 + [flat] * len(others),
            out_specs=flat,
        ),
        out_shape=jax.ShapeDtypeStruct((height, protos), f32 if others else bf16),
        compiler_params=params(12),
        cost_estimate=cost(6 * height * protos, 10 * height * protos),
    )(place.reshape(1), stay, arrived, turned, *radials, length, *others)


def body(hidden_states, ln_in_gain, w_in, w_out, ln_out_gain, prototypes):
    view_count, image_rows, local_width = hidden_states.shape
    row_count = view_count * image_rows
    col_count = lax.axis_size(COLS)
    row_block = row_count // col_count

    y_count = lax.axis_size("y")
    z_count = lax.axis_size("z")
    tall = row_count // y_count

    states_t = hidden_states.reshape(row_count, local_width).T
    gain_row = jnp.pad(jnp.concatenate([ln_in_gain, ln_out_gain]), (0, tall - 2 * local_width))
    pieces = jnp.concatenate(
        [
            states_t.reshape(local_width, y_count, tall).transpose(1, 0, 2),
            jnp.broadcast_to(gain_row[None, None], (y_count, 8, tall)),
        ],
        axis=1,
    )
    sent = jnp.broadcast_to(pieces[None], (z_count,) + pieces.shape)
    received = lax.all_to_all(
        sent.reshape(col_count, local_width + 8, tall), COLS, 0, 0
    )
    gains = received[:, local_width]
    gain_in = gains[:, :local_width].reshape(D).astype(f32)
    gain_out = gains[:, local_width : 2 * local_width].reshape(D).astype(f32)
    inputs_t = received[:, :local_width].reshape(D, tall)

    core = lax.axis_index("core")
    swap = [(0, 1), (1, 0)]
    w_in_t = w_in.T
    share = jnp.where(core == 0, w_in_t, w_out)
    shares = stack_shares(
        [
            lax.ppermute(share, "y", [(i, (i + step) % y_count) for i in range(y_count)])
            for step in range(1, y_count)
        ]
    )
    others = lax.ppermute(shares, "core", swap)

    inputs_f = inputs_t.astype(f32)
    center = jnp.mean(inputs_f, axis=0)
    spread = jnp.mean(inputs_f * inputs_f, axis=0) - center * center
    normed_t = (
        (inputs_f - center[None, :]) * lax.rsqrt(spread + norm_eps)[None, :] * gain_in[:, None]
    ).astype(bf16)
    block_part = feed_forward(core, normed_t.T, w_in_t, w_out, shares, others)
    block = scatter_sum(block_part.reshape(z_count, row_block, D), "z")
    picked = (
        jnp.arange(tall)[None, :]
        == lax.axis_index("z") * row_block + jnp.arange(row_block)[:, None]
    ).astype(bf16)
    own = lax.dot_general(picked, inputs_t, (((1,), (1,)), ((), ())), preferred_element_type=f32)
    resid = own + block
    center = jnp.mean(resid, axis=1, keepdims=True)
    spread = jnp.mean(resid * resid, axis=1, keepdims=True) - center * center
    final = (resid - center) * lax.rsqrt(spread + norm_eps) * gain_out[None, :]
    squared = jnp.sum(final * final, axis=1, keepdims=True)
    embed_part = (final * lax.rsqrt(squared + unit_eps)).astype(bf16)
    embed = gather_all(embed_part, ("y", "z")).reshape(row_count, D)

    x_index = lax.axis_index("x")
    x_count = lax.axis_size("x")
    unit, proto_len, turned = prepare(core, prototypes, x_count)
    proto_count = prototypes.shape[0]
    slice_width = turned.shape[1]

    row_parts = lax.axis_size(ROWS)
    scores, base, masses, soft_part = score_pass(embed, unit, row_parts)
    masses = lax.all_to_all(masses, ROWS, 0, 0)
    softs = images = lax.all_to_all(image_pass(masses, base, col_count, soft_part), COLS, 0, 0)
    for repeat in range(1, SINK_ITERS):
        masses = lax.all_to_all(proto_pass(images, base, row_parts), ROWS, 0, 0)
        images = lax.all_to_all(image_pass(masses, base, col_count), COLS, 0, 0)

    embed_t = embed.T.reshape(x_count, 2, slice_width, row_count)
    away_t, stay_t = (
        lax.dynamic_index_in_dim(embed_t, side, 1, False).reshape(-1, row_count)
        for side in (1 - core, core)
    )
    grad_flat, radial, away, stay = grad_pass(images, softs, masses, scores, away_t, stay_t)
    embed_terms = lax.dot_general(
        unit, grad_flat, (((0,), (1,)), ((), ())), preferred_element_type=f32
    ).astype(bf16)
    stay, arrived = (
        part.reshape(x_count, slice_width, proto_count)
        for part in (stay, lax.ppermute(away, "core", swap))
    )
    radials = (radial, lax.ppermute(radial, "core", swap))

    def paired(step, others=()):
        place = (x_index + step) % x_count
        return pair_call(place, stay, arrived, turned, radials, proto_len, others)

    landed = tuple(
        lax.ppermute(paired(step), "x", [(i, (i + step) % x_count) for i in range(x_count)])
        for step in (2, 1, 3)
    )
    proto_grad = paired(0, landed)
    embed_grad_t = scatter_sum(embed_terms.reshape(col_count, local_width, row_count), COLS)
    embed_grad = embed_grad_t.T.reshape(view_count, image_rows, local_width)
    return (embed_grad, proto_grad)


def solution(mesh):
    sizes = {"x": mesh.shape["rows"] // 2, "core": 2, "z": mesh.shape["cols"] // 4, "y": 4}
    fine = Mesh(mesh.devices.reshape(tuple(sizes.values())), tuple(sizes))
    placed = (
        P(None, ROWS, COLS),
        P(COLS),
        P(None, COLS),
        P(COLS, None),
        P(COLS),
        P(COLS, None),
    )
    return jax.shard_map(
        body,
        mesh=fine,
        in_specs=placed,
        out_specs=(P(None, ROWS, COLS), P(ROWS, COLS)),
        check_vma=False,
    )
```

```python
import functools
import math

import jax
import jax.numpy as jnp
from jax import lax
from jax.experimental import pallas as pl
from jax.experimental.pallas import tpu as pltpu
from jax.sharding import Mesh, PartitionSpec as P

D = 1024
PROTOS = 65536
SINK_ITERS = 3


sink_temp = 0.05
soft_temp = 0.1
norm_eps = 1e-05
unit_eps = 1e-06

ROWS = ("x", "core")
COLS = ("z", "y")
f32 = jnp.float32
bf16 = jnp.bfloat16


def gather_all(values, axes):
    count = lax.axis_size(axes)
    copies = jnp.broadcast_to(values[None], (count,) + values.shape)
    return lax.all_to_all(copies, axes, 0, 0)


def sum_small(values, axes):
    return jnp.sum(gather_all(values, axes), axis=0)


def scatter_sum(blocks, axes):
    return jnp.sum(lax.all_to_all(blocks, axes, 0, 0).astype(f32), axis=0)


TILE = 512
LANES = 128
factor = 0.5 * math.sqrt(PROTOS * D)
NT = (((1,), (1,)), ((), ()))


def params(mib):
    return pltpu.CompilerParams(
        dimension_semantics=("arbitrary",), vmem_limit_bytes=mib * 1024 * 1024
    )


def whole(shape):
    return pl.BlockSpec(shape, lambda i: (0,) * len(shape))


def cost(flops, bytes_accessed, transcendentals=0):
    return pl.CostEstimate(
        flops=flops, bytes_accessed=bytes_accessed, transcendentals=transcendentals
    )


def fold_lanes(values):
    width = values.shape[1]
    return sum(values[:, j : j + LANES] for j in range(0, width, LANES))


def as_column(row):
    return jnp.broadcast_to(row, (LANES, row.shape[1])).T


def spread_lanes(column, width):
    return jnp.concatenate([column] * (width // LANES), axis=1)


def view_rows(pair, count):
    half = count // 2
    width = pair.shape[1]
    return jnp.concatenate(
        [jnp.broadcast_to(pair[v : v + 1], (half, width)) for v in range(2)], axis=0
    )


def view_sums(values):
    half = values.shape[0] // 2
    return jnp.concatenate(
        [jnp.sum(values[v * half : (v + 1) * half], axis=0, keepdims=True) for v in range(2)],
        axis=0,
    )


def accumulate(total, part):
    @pl.when(pl.program_id(0) == 0)
    def _():
        total[...] = part

    @pl.when(pl.program_id(0) > 0)
    def _():
        total[...] += part


def in_hbm(shape, dtype):
    return pltpu.HBM(shape, dtype)


def keep_hbm(values):
    return pltpu.with_memory_space_constraint(values, pltpu.HBM)


def stack_kernel(first_ref, second_ref, third_ref, out_ref):
    for place, ref in enumerate((first_ref, second_ref, third_ref)):
        out_ref[place] = ref[...]


def stack_shares(parts):
    shape = parts[0].shape
    return pl.pallas_call(
        stack_kernel,
        grid=(1,),
        in_specs=[whole(shape)] * 3,
        out_specs=whole((3,) + shape),
        out_shape=jax.ShapeDtypeStruct((3,) + shape, bf16),
        compiler_params=params(6),
        cost_estimate=cost(40 * 10**9, 4 * parts[0].size),
    )(*parts)


def ffn_kernel(core_ref, normed_ref, w_in_ref, w_out_ref, shares_ref, others_ref, out_ref):
    normed = normed_ref[...]
    even = core_ref[0] == 0
    total = jnp.zeros(out_ref.shape, f32)
    for step in range(shares_ref.shape[0] + 1):
        if step == 0:
            enter, leave = w_in_ref[...], w_out_ref[...]
        else:
            one, other = shares_ref[step - 1], others_ref[step - 1]
            enter, leave = jnp.where(even, one, other), jnp.where(even, other, one)
        wide = lax.dot_general(normed, enter, NT, preferred_element_type=f32)
        hidden = (0.5 * wide * (1.0 + lax.erf(wide * math.sqrt(0.5)))).astype(bf16)
        total = total + jnp.dot(hidden, leave, preferred_element_type=f32)
    out_ref[...] = total.astype(bf16)


def feed_forward(core, normed, w_in_t, w_out, shares, others):
    rows = normed.shape[0]
    arrays = (normed, w_in_t, w_out, shares, others)
    return pl.pallas_call(
        ffn_kernel,
        grid=(1,),
        in_specs=[pl.BlockSpec(memory_space=pltpu.SMEM)] + [whole(a.shape) for a in arrays],
        out_specs=whole((rows, D)),
        out_shape=jax.ShapeDtypeStruct((rows, D), bf16),
        compiler_params=params(8),
        cost_estimate=cost(4 * rows * D * 4 * w_out.shape[0], 8 * w_out.size),
    )(core.reshape(1), *arrays)


def prepare_kernel(core_ref, proto_ref, unit_ref, length_ref, turned_ref):
    values = proto_ref[...].astype(f32)
    squares = values * values
    inverse = lax.rsqrt(jnp.sum(squares, axis=1, keepdims=True) + unit_eps)
    unit_ref[...] = (values * inverse).astype(bf16)
    length_ref[...] = jnp.sqrt(
        jnp.sum(fold_lanes(squares).T, axis=0, keepdims=True) + unit_eps
    )
    even = core_ref[0] == 0
    for block in range(turned_ref.shape[0]):
        start = 2 * block * LANES
        picked = jnp.where(
            even, values[:, start : start + LANES], values[:, start + LANES : start + 2 * LANES]
        )
        turned_ref[block] = picked.T.astype(bf16)


def prepare(core, prototypes, x_count):
    protos = prototypes.shape[0]
    return pl.pallas_call(
        prepare_kernel,
        grid=(protos // TILE,),
        in_specs=[
            pl.BlockSpec(memory_space=pltpu.SMEM),
            pl.BlockSpec((TILE, D), lambda i: (i, 0)),
        ],
        out_specs=[
            pl.BlockSpec((TILE, D), lambda i: (i, 0)),
            pl.BlockSpec((1, TILE), lambda i: (0, i)),
            pl.BlockSpec((x_count, LANES, TILE), lambda i: (0, 0, i)),
        ],
        out_shape=[
            in_hbm((protos, D), bf16),
            jax.ShapeDtypeStruct((1, protos), f32),
            in_hbm((x_count, LANES, protos), bf16),
        ],
        compiler_params=params(18),
        cost_estimate=cost(6 * protos * D, 5 * protos * D),
    )(core.reshape(1), keep_hbm(prototypes))


def scores_kernel(first, last, blocks, place_ref, embed_ref, unit_ref, *rest):
    before_ref = None if first else rest[0]
    scores_ref, base_ref, mass_ref, soft_ref, turned_ref, total = rest[-6:]

    @pl.when(pl.program_id(0) == 0)
    def _():
        even = place_ref[1] == 0
        values = embed_ref[...].astype(f32)
        for block in range(D // (2 * LANES)):
            start = 2 * block * LANES
            low = values[:, start : start + LANES]
            high = values[:, start + LANES : start + 2 * LANES]
            rows = slice(block * LANES, (block + 1) * LANES)
            turned_ref[0, rows, :] = jnp.where(even, high, low).T.astype(bf16)
            turned_ref[1, rows, :] = jnp.where(even, low, high).T.astype(bf16)

    scores = lax.dot_general(embed_ref[...], unit_ref[...], NT, preferred_element_type=f32)
    scores_ref[...] = scores
    soft = jnp.exp(scores * (1.0 / soft_temp))
    base = soft * soft
    base_ref[...] = base.astype(bf16)
    line = jnp.sum(base, axis=0, keepdims=True)
    later = place_ref[0] >= blocks // 2
    none = jnp.zeros_like(line)
    mass = jnp.concatenate([jnp.where(later, none, line), jnp.where(later, line, none)], axis=0)
    if not first:
        mass = mass + before_ref[...]
    mass_ref[...] = jnp.broadcast_to(mass, mass_ref.shape) if last else mass
    accumulate(total, fold_lanes(soft))

    @pl.when(pl.program_id(0) == pl.num_programs(0) - 1)
    def _():
        soft_ref[...] = jnp.sum(total[...].T, axis=0, keepdims=True)


def score_pass(place, embed, unit, blocks, copies, last, before=None):
    height, protos = embed.shape[0], unit.shape[0]
    rows = height * blocks
    first = before is None
    mass = (copies, 2, protos) if last else (2, protos)
    mass_spec = (
        pl.BlockSpec((copies, 2, TILE), lambda i, p: (0, 0, i))
        if last
        else pl.BlockSpec((2, TILE), lambda i, p: (0, i))
    )
    shapes = [
        in_hbm((rows, protos), f32),
        jax.ShapeDtypeStruct((rows, protos), bf16),
        jax.ShapeDtypeStruct(mass, f32),
        jax.ShapeDtypeStruct((1, rows), f32),
        jax.ShapeDtypeStruct((2, D // 2, rows), bf16),
    ]
    in_specs = [
        pl.BlockSpec((height, D), lambda i, p: (0, 0)),
        pl.BlockSpec((TILE, D), lambda i, p: (i, 0)),
    ]
    arrays = [embed, keep_hbm(unit)]
    aliases = {}
    if not first:
        scores, base, mass_before, soft, turned = before
        in_specs.append(pl.BlockSpec((2, TILE), lambda i, p: (0, i)))
        in_specs += [pl.BlockSpec(memory_space=pl.ANY)] * 4
        arrays += [mass_before, scores, base, soft, turned]
        aliases = {4: 0, 5: 1, 6: 3, 7: 4}
    return pl.pallas_call(
        functools.partial(scores_kernel, first, last, blocks),
        grid_spec=pltpu.PrefetchScalarGridSpec(
            num_scalar_prefetch=1,
            grid=(protos // TILE,),
            in_specs=in_specs,
            out_specs=[
                pl.BlockSpec((height, TILE), lambda i, p: (p[0], i)),
                pl.BlockSpec((height, TILE), lambda i, p: (p[0], i)),
                mass_spec,
                pl.BlockSpec((1, height), lambda i, p: (0, p[0])),
                pl.BlockSpec((2, D // 2, height), lambda i, p: (0, 0, p[0])),
            ],
            scratch_shapes=[pltpu.VMEM((height, LANES), f32)],
        ),
        out_shape=shapes,
        input_output_aliases=aliases,
        compiler_params=params(12),
        cost_estimate=cost(2 * height * protos * D, 8 * height * protos, height * protos),
    )(place, *arrays)


def image_kernel(copies, mass_ref, base_ref, *rest):
    *extra, out_ref, total = rest
    scale = 1.0 / jnp.sum(mass_ref[...], axis=0)
    values = base_ref[...].astype(f32) * view_rows(scale, base_ref.shape[0])
    accumulate(total, fold_lanes(values))

    @pl.when(pl.program_id(0) == pl.num_programs(0) - 1)
    def _():
        row = jnp.sum(total[...].T, axis=0, keepdims=True)
        row = jnp.concatenate([row] + [ref[...] for ref in extra], axis=0)
        out_ref[...] = jnp.broadcast_to(row[None], (copies,) + row.shape)


def image_pass(masses, base, copies, *extra):
    rows, protos = base.shape
    out = (copies, 1 + len(extra), rows)
    return pl.pallas_call(
        functools.partial(image_kernel, copies),
        grid=(protos // TILE,),
        in_specs=[
            pl.BlockSpec((masses.shape[0], 2, TILE), lambda i: (0, 0, i)),
            pl.BlockSpec((rows, TILE), lambda i: (0, i)),
        ]
        + [whole(e.shape) for e in extra],
        out_specs=whole(out),
        out_shape=jax.ShapeDtypeStruct(out, f32),
        scratch_shapes=[pltpu.VMEM((rows, LANES), f32)],
        compiler_params=params(10),
        cost_estimate=cost(3 * rows * protos, 2 * rows * protos),
    )(masses, base, *extra)


def proto_kernel(copies, image_ref, base_ref, mass_ref, column):
    @pl.when(pl.program_id(0) == 0)
    def _():
        column[...] = as_column(1.0 / jnp.sum(image_ref[...], axis=0)[:1])

    values = base_ref[...].astype(f32) * spread_lanes(column[...], base_ref.shape[1])
    mass = view_sums(values)
    mass_ref[...] = jnp.broadcast_to(mass[None], (copies,) + mass.shape)


def proto_pass(images, base, copies):
    rows, protos = base.shape
    return pl.pallas_call(
        functools.partial(proto_kernel, copies),
        grid=(protos // TILE,),
        in_specs=[whole(images.shape), pl.BlockSpec((rows, TILE), lambda i: (0, i))],
        out_specs=pl.BlockSpec((copies, 2, TILE), lambda i: (0, 0, i)),
        out_shape=jax.ShapeDtypeStruct((copies, 2, protos), f32),
        scratch_shapes=[pltpu.VMEM((rows, LANES), f32)],
        compiler_params=params(10),
        cost_estimate=cost(3 * rows * protos, 2 * rows * protos),
    )(images, base)


def grad_kernel(
    image_ref, soft_ref, mass_ref, scores_ref, embed_t_ref,
    grad_ref, radial_ref, away_ref, stay_ref, code_column, prob_column,
):
    @pl.when(pl.program_id(0) == 0)
    def _():
        code_column[...] = as_column(factor / jnp.sum(image_ref[...], axis=0)[:1])
        prob_column[...] = as_column(factor / jnp.sum(soft_ref[...], axis=0)[1:2])

    scores = scores_ref[...]
    rows, width = scores.shape
    half = rows // 2
    soft = jnp.exp(scores * (1.0 / soft_temp))
    scale = 1.0 / jnp.sum(mass_ref[...], axis=0)
    codes = (
        soft * soft * view_rows(scale, rows) * spread_lanes(code_column[...], width)
    )
    swapped = jnp.concatenate([codes[half:], codes[:half]], axis=0)
    grad = (soft * spread_lanes(prob_column[...], width) - swapped).astype(bf16)
    grad_ref[...] = grad
    radial_ref[...] = jnp.sum(grad.astype(f32) * scores, axis=0, keepdims=True)
    away = jnp.dot(embed_t_ref[0], grad, preferred_element_type=f32).astype(bf16)
    away_ref[...] = away.reshape(away_ref.shape)
    stay = jnp.dot(embed_t_ref[1], grad, preferred_element_type=f32)
    stay_ref[...] = stay.reshape(stay_ref.shape)


def grad_pass(images, softs, masses, scores, embed_t):
    rows, protos = scores.shape
    depth = embed_t.shape[1]
    blocks = depth // LANES

    def tile(height):
        return pl.BlockSpec((height, TILE), lambda i: (0, i))

    halves = pl.BlockSpec((blocks, LANES, TILE), lambda i: (0, 0, i))
    return pl.pallas_call(
        grad_kernel,
        grid=(protos // TILE,),
        in_specs=[
            whole(images.shape),
            whole(softs.shape),
            pl.BlockSpec((masses.shape[0], 2, TILE), lambda i: (0, 0, i)),
            tile(rows),
            whole(embed_t.shape),
        ],
        out_specs=[tile(rows), tile(1), halves, halves],
        out_shape=[
            jax.ShapeDtypeStruct((rows, protos), bf16),
            jax.ShapeDtypeStruct((1, protos), f32),
            in_hbm((blocks, LANES, protos), bf16),
            in_hbm((blocks, LANES, protos), f32),
        ],
        scratch_shapes=[pltpu.VMEM((rows, LANES), f32)] * 2,
        compiler_params=params(20),
        cost_estimate=cost(4 * depth * rows * protos, 12 * rows * protos, rows * protos),
    )(images, softs, masses, keep_hbm(scores), embed_t)


def pair(stay, arrived, turned, radials, length):
    radial = radials[0] + radials[1]
    inverse = 1.0 / length
    return (stay + arrived.astype(f32) - turned.astype(f32) * (radial * inverse)) * inverse


def pair_kernel(place_ref, stay_ref, arrived_ref, turned_ref, one_ref, two_ref, length_ref, out_ref):
    out_ref[...] = pair(
        stay_ref[0], arrived_ref[0], turned_ref[0], (one_ref[...], two_ref[...]), length_ref[...]
    ).astype(bf16)


def final_kernel(
    place_ref, stay_ref, arrived_ref, turned_ref, one_ref, two_ref, length_ref, *rest
):
    *others, out_ref = rest
    total = pair(
        stay_ref[0], arrived_ref[0], turned_ref[0], (one_ref[...], two_ref[...]), length_ref[...]
    )
    for ref in others:
        total = total + ref[...].astype(f32)
    out_ref[...] = total


def pair_call(place, stay, arrived, turned, radials, length, others=()):
    blocks, height, protos = stay.shape
    wide = TILE
    picked = pl.BlockSpec((1, height, wide), lambda i, p: (p[0], 0, i))
    line = pl.BlockSpec((1, wide), lambda i, p: (0, i))
    flat = pl.BlockSpec((height, wide), lambda i, p: (0, i))
    return pl.pallas_call(
        final_kernel if others else pair_kernel,
        grid_spec=pltpu.PrefetchScalarGridSpec(
            num_scalar_prefetch=1,
            grid=(protos // wide,),
            in_specs=[picked] * 3 + [line] * 3 + [flat] * len(others),
            out_specs=flat,
        ),
        out_shape=jax.ShapeDtypeStruct((height, protos), f32 if others else bf16),
        compiler_params=params(12),
        cost_estimate=cost(40 * 10**9 if others else 10**9, 10 * height * protos),
    )(place.reshape(1), keep_hbm(stay), keep_hbm(arrived), keep_hbm(turned), *radials, length, *others)


def body(hidden_states, ln_in_gain, w_in, w_out, ln_out_gain, prototypes):
    view_count, image_rows, local_width = hidden_states.shape
    row_count = view_count * image_rows
    col_count = lax.axis_size(COLS)
    row_block = row_count // col_count

    y_count = lax.axis_size("y")
    z_count = lax.axis_size("z")
    tall = row_count // y_count

    states_t = hidden_states.reshape(row_count, local_width).T
    gain_row = jnp.pad(jnp.concatenate([ln_in_gain, ln_out_gain]), (0, tall - 2 * local_width))
    pieces = jnp.concatenate(
        [
            states_t.reshape(local_width, y_count, tall).transpose(1, 0, 2),
            jnp.broadcast_to(gain_row[None, None], (y_count, 8, tall)),
        ],
        axis=1,
    )
    sent = jnp.broadcast_to(pieces[None], (z_count,) + pieces.shape)
    received = lax.all_to_all(
        sent.reshape(col_count, local_width + 8, tall), COLS, 0, 0
    )
    gains = received[:, local_width]
    gain_in = gains[:, :local_width].reshape(D).astype(f32)
    gain_out = gains[:, local_width : 2 * local_width].reshape(D).astype(f32)
    inputs_t = received[:, :local_width].reshape(D, tall)

    core = lax.axis_index("core")
    swap = [(0, 1), (1, 0)]
    w_in_t = w_in.T
    share = jnp.where(core == 0, w_in_t, w_out)
    shares = stack_shares(
        [
            lax.ppermute(share, "y", [(i, (i + step) % y_count) for i in range(y_count)])
            for step in range(1, y_count)
        ]
    )
    others = lax.ppermute(shares, "core", swap)

    inputs_f = inputs_t.astype(f32)
    center = jnp.mean(inputs_f, axis=0)
    spread = jnp.mean(inputs_f * inputs_f, axis=0) - center * center
    normed_t = (
        (inputs_f - center[None, :]) * lax.rsqrt(spread + norm_eps)[None, :] * gain_in[:, None]
    ).astype(bf16)
    block_part = feed_forward(core, normed_t.T, w_in_t, w_out, shares, others)
    block = scatter_sum(block_part.reshape(z_count, row_block, D), "z")
    picked = (
        jnp.arange(tall)[None, :]
        == lax.axis_index("z") * row_block + jnp.arange(row_block)[:, None]
    ).astype(bf16)
    own = lax.dot_general(picked, inputs_t, (((1,), (1,)), ((), ())), preferred_element_type=f32)
    resid = own + block
    center = jnp.mean(resid, axis=1, keepdims=True)
    spread = jnp.mean(resid * resid, axis=1, keepdims=True) - center * center
    final = (resid - center) * lax.rsqrt(spread + norm_eps) * gain_out[None, :]
    squared = jnp.sum(final * final, axis=1, keepdims=True)
    embed_part = (final * lax.rsqrt(squared + unit_eps)).astype(bf16)
    own_rows = gather_all(embed_part, "z").reshape(tall, D)

    x_index = lax.axis_index("x")
    x_count = lax.axis_size("x")
    unit, proto_len, turned = prepare(core, prototypes, x_count)
    proto_count = prototypes.shape[0]
    slice_width = turned.shape[1]

    row_parts = lax.axis_size(ROWS)
    y_index = lax.axis_index("y")
    steps = (1, 3, 2)
    rows_in = {
        step: lax.ppermute(own_rows, "y", [(i, (i + step) % y_count) for i in range(y_count)])
        for step in steps
    }
    state = None
    for step in (0,) + steps:
        place = jnp.stack([(y_index + y_count - step) % y_count, core])
        block_rows = rows_in[step] if step else own_rows
        state = score_pass(place, block_rows, unit, y_count, row_parts, step == steps[-1], state)
    scores, base, masses, soft_part, embed_t = state
    masses = lax.all_to_all(masses, ROWS, 0, 0)
    softs = images = lax.all_to_all(image_pass(masses, base, col_count, soft_part), COLS, 0, 0)
    for repeat in range(1, SINK_ITERS):
        masses = lax.all_to_all(proto_pass(images, base, row_parts), ROWS, 0, 0)
        images = lax.all_to_all(image_pass(masses, base, col_count), COLS, 0, 0)

    grad_flat, radial, away, stay = grad_pass(images, softs, masses, scores, embed_t)
    embed_terms = lax.dot_general(
        unit, grad_flat, (((0,), (1,)), ((), ())), preferred_element_type=f32
    ).astype(bf16)
    arrived = lax.ppermute(away, "core", swap)
    radials = (radial, lax.ppermute(radial, "core", swap))

    def paired(step, others=()):
        place = (x_index + step) % x_count
        return pair_call(place, stay, arrived, turned, radials, proto_len, others)

    landed = tuple(
        lax.ppermute(paired(step), "x", [(i, (i + step) % x_count) for i in range(x_count)])
        for step in (2, 1, 3)
    )
    proto_grad = paired(0, landed)
    embed_grad_t = scatter_sum(embed_terms.reshape(col_count, local_width, row_count), COLS)
    embed_grad = embed_grad_t.T.reshape(view_count, image_rows, local_width)
    return (embed_grad, proto_grad)


def solution(mesh):
    sizes = {"x": mesh.shape["rows"] // 2, "core": 2, "z": mesh.shape["cols"] // 4, "y": 4}
    fine = Mesh(mesh.devices.reshape(tuple(sizes.values())), tuple(sizes))
    placed = (
        P(None, ROWS, COLS),
        P(COLS),
        P(None, COLS),
        P(COLS, None),
        P(COLS),
        P(COLS, None),
    )
    return jax.shard_map(
        body,
        mesh=fine,
        in_specs=placed,
        out_specs=(P(None, ROWS, COLS), P(ROWS, COLS)),
        check_vma=False,
    )
```

```python
import math

import jax
import jax.numpy as jnp
from jax import lax
from jax.experimental import pallas as pl
from jax.experimental.pallas import tpu as pltpu
from jax.sharding import Mesh, PartitionSpec as P

D = 1024
PROTOS = 65536
SINK_ITERS = 3


sink_temp = 0.05
soft_temp = 0.1
norm_eps = 1e-05
unit_eps = 1e-06

ROWS = ("x", "core")
COLS = ("z", "y")
f32 = jnp.float32
bf16 = jnp.bfloat16


def gather_all(values, axes):
    count = lax.axis_size(axes)
    copies = jnp.broadcast_to(values[None], (count,) + values.shape)
    return lax.all_to_all(copies, axes, 0, 0)


def sum_small(values, axes):
    return jnp.sum(gather_all(values, axes), axis=0)


def scatter_sum(blocks, axes):
    return jnp.sum(lax.all_to_all(blocks, axes, 0, 0).astype(f32), axis=0)


TILE = 512
LANES = 128
factor = 0.5 * math.sqrt(PROTOS * D)
NT = (((1,), (1,)), ((), ()))
VMEM = pl.BlockSpec(memory_space=pltpu.VMEM)
SMEM = pl.BlockSpec(memory_space=pltpu.SMEM)


def keep_hbm(values):
    return pltpu.with_memory_space_constraint(values, pltpu.HBM)


def call(kernel, scalars, arrays, outs, mib, flops, moved, in_hbm=()):
    shapes = [
        pltpu.HBM(shape, dtype) if place in in_hbm else jax.ShapeDtypeStruct(shape, dtype)
        for place, (shape, dtype) in enumerate(outs)
    ]
    many = len(shapes) > 1
    return pl.pallas_call(
        kernel,
        in_specs=[SMEM] * len(scalars) + [VMEM] * len(arrays),
        out_specs=[VMEM] * len(shapes) if many else VMEM,
        out_shape=shapes if many else shapes[0],
        compiler_params=pltpu.CompilerParams(vmem_limit_bytes=mib * 1024 * 1024),
        cost_estimate=pl.CostEstimate(flops=flops, bytes_accessed=moved, transcendentals=0),
    )(*scalars, *arrays)


def fold_lanes(values):
    width = values.shape[1]
    return sum(values[:, j : j + LANES] for j in range(0, width, LANES))


def as_column(row):
    return jnp.broadcast_to(row, (LANES, row.shape[1])).T


def as_row(column):
    return jnp.sum(column.T, axis=0, keepdims=True)


def spread_lanes(column, width):
    return jnp.concatenate([column] * (width // LANES), axis=1)


def view_rows(pair, count):
    half = count // 2
    width = pair.shape[1]
    return jnp.concatenate(
        [jnp.broadcast_to(pair[v : v + 1], (half, width)) for v in range(2)], axis=0
    )


def view_sums(values):
    half = values.shape[0] // 2
    return jnp.concatenate(
        [jnp.sum(values[v * half : (v + 1) * half], axis=0, keepdims=True) for v in range(2)],
        axis=0,
    )


def tiles(count):
    return [slice(j, j + TILE) for j in range(0, count, TILE)]


def stack_kernel(first_ref, second_ref, third_ref, out_ref):
    for place, ref in enumerate((first_ref, second_ref, third_ref)):
        out_ref[place] = ref[...]


def stack_shares(parts):
    return call(
        stack_kernel, (), parts, [((3,) + parts[0].shape, bf16)], 2, 40 * 10**9, 4 * parts[0].size
    )


def ffn_kernel(core_ref, normed_ref, w_in_ref, w_out_ref, shares_ref, others_ref, out_ref):
    normed = normed_ref[...]
    even = core_ref[0] == 0
    total = jnp.zeros(out_ref.shape, f32)
    for step in range(shares_ref.shape[0] + 1):
        if step == 0:
            enter, leave = w_in_ref[...], w_out_ref[...]
        else:
            one, other = shares_ref[step - 1], others_ref[step - 1]
            enter, leave = jnp.where(even, one, other), jnp.where(even, other, one)
        wide = lax.dot_general(normed, enter, NT, preferred_element_type=f32)
        hidden = (0.5 * wide * (1.0 + lax.erf(wide * math.sqrt(0.5)))).astype(bf16)
        total = total + jnp.dot(hidden, leave, preferred_element_type=f32)
    out_ref[...] = total.astype(bf16)


def feed_forward(core, normed, w_in_t, w_out, shares, others):
    rows = normed.shape[0]
    return call(
        ffn_kernel,
        (core.reshape(1),),
        (normed, w_in_t, w_out, shares, others),
        [((rows, D), bf16)],
        8,
        4 * rows * D * 4 * w_out.shape[0],
        8 * w_out.size,
    )


def prepare_kernel(core_ref, proto_ref, unit_ref, length_ref, turned_ref):
    even = core_ref[0] == 0
    for part in tiles(proto_ref.shape[0]):
        values = proto_ref[part, :].astype(f32)
        squares = values * values
        inverse = lax.rsqrt(jnp.sum(squares, axis=1, keepdims=True) + unit_eps)
        unit_ref[part, :] = (values * inverse).astype(bf16)
        length_ref[:, part] = jnp.sqrt(as_row(fold_lanes(squares)) + unit_eps)
        for block in range(turned_ref.shape[0]):
            start = 2 * block * LANES
            low = values[:, start : start + LANES]
            high = values[:, start + LANES : start + 2 * LANES]
            turned_ref[block, :, part] = jnp.where(even, low, high).T.astype(bf16)


def prepare(core, prototypes, x_count):
    protos = prototypes.shape[0]
    return call(
        prepare_kernel,
        (core.reshape(1),),
        (prototypes,),
        [((protos, D), bf16), ((1, protos), f32), ((x_count, LANES, protos), bf16)],
        12,
        6 * protos * D,
        5 * protos * D,
        (2,),
    )


def scores_kernel(place_ref, *rest):
    *block_refs, unit_ref, base_ref, mass_ref, soft_ref, embed_ref = rest
    height = block_refs[0].shape[0]
    for n, ref in enumerate(block_refs):
        embed_ref[pl.ds(pl.multiple_of(place_ref[n] * height, height), height), :] = ref[...]
    total = jnp.zeros((base_ref.shape[0], LANES), f32)
    for part in tiles(unit_ref.shape[0]):
        scores = lax.dot_general(
            embed_ref[...], unit_ref[part, :], NT, preferred_element_type=f32
        )
        soft = jnp.exp(scores * (1.0 / soft_temp))
        base = soft * soft
        base_ref[:, part] = base.astype(bf16)
        mass = view_sums(base)
        mass_ref[:, :, part] = jnp.broadcast_to(mass[None], (mass_ref.shape[0],) + mass.shape)
        total = total + fold_lanes(soft)
    soft_ref[...] = as_row(total)


def score_pass(places, parts, unit, copies):
    height, protos = parts[0].shape[0], unit.shape[0]
    rows = height * len(parts)
    return call(
        scores_kernel,
        (places,),
        (*parts, unit),
        [
            ((rows, protos), bf16),
            ((copies, 2, protos), f32),
            ((1, rows), f32),
            ((rows, D), bf16),
        ],
        10,
        2 * rows * protos * D,
        8 * rows * protos,
    )


def turn_kernel(core_ref, embed_ref, turned_ref):
    even = core_ref[0] == 0
    for block in range(D // (2 * LANES)):
        start = 2 * block * LANES
        low = embed_ref[:, start : start + LANES].astype(f32)
        high = embed_ref[:, start + LANES : start + 2 * LANES].astype(f32)
        rows = slice(block * LANES, (block + 1) * LANES)
        turned_ref[0, rows, :] = jnp.where(even, high, low).T.astype(bf16)
        turned_ref[1, rows, :] = jnp.where(even, low, high).T.astype(bf16)


def turn(core, embed):
    rows = embed.shape[0]
    return call(
        turn_kernel, (core.reshape(1),), (embed,), [((2, D // 2, rows), bf16)], 6, 10**9, 4 * embed.size
    )


def image_kernel(mass_ref, base_ref, *rest):
    *extra, out_ref = rest
    rows, protos = base_ref.shape
    total = jnp.zeros((rows, LANES), f32)
    for part in tiles(protos):
        scale = 1.0 / jnp.sum(mass_ref[:, :, part], axis=0)
        total = total + fold_lanes(base_ref[:, part].astype(f32) * view_rows(scale, rows))
    row = jnp.concatenate([as_row(total)] + [ref[...] for ref in extra], axis=0)
    out_ref[...] = jnp.broadcast_to(row[None], out_ref.shape)


def image_pass(masses, base, copies, *extra):
    rows, protos = base.shape
    return call(
        image_kernel,
        (),
        (masses, base, *extra),
        [((copies, 1 + len(extra), rows), f32)],
        8,
        3 * rows * protos,
        2 * rows * protos,
    )


def proto_kernel(image_ref, base_ref, mass_ref):
    column = as_column(1.0 / jnp.sum(image_ref[...], axis=0)[:1])
    for part in tiles(base_ref.shape[1]):
        mass = view_sums(base_ref[:, part].astype(f32) * spread_lanes(column, TILE))
        mass_ref[:, :, part] = jnp.broadcast_to(mass[None], (mass_ref.shape[0],) + mass.shape)


def proto_pass(images, base, copies):
    rows, protos = base.shape
    return call(
        proto_kernel,
        (),
        (images, base),
        [((copies, 2, protos), f32)],
        8,
        3 * rows * protos,
        2 * rows * protos,
    )


def grad_kernel(
    image_ref, soft_ref, mass_ref, unit_ref, embed_ref, embed_t_ref,
    radial_ref, away_ref, stay_ref, terms_ref, code_column, prob_column, total,
):
    step = pl.program_id(0)

    @pl.when(step == 0)
    def _():
        code_column[...] = as_column(factor / jnp.sum(image_ref[...], axis=0)[:1])
        prob_column[...] = as_column(factor / jnp.sum(soft_ref[...], axis=0)[1:2])
        total[...] = jnp.zeros_like(total)

    scores = lax.dot_general(embed_ref[...], unit_ref[...], NT, preferred_element_type=f32)
    rows = scores.shape[0]
    half = rows // 2
    soft = jnp.exp(scores * (1.0 / soft_temp))
    scale = 1.0 / jnp.sum(mass_ref[...], axis=0)
    codes = soft * soft * view_rows(scale, rows) * spread_lanes(code_column[...], TILE)
    swapped = jnp.concatenate([codes[half:], codes[:half]], axis=0)
    grad = (soft * spread_lanes(prob_column[...], TILE) - swapped).astype(bf16)
    radial_ref[...] = jnp.sum(grad.astype(f32) * scores, axis=0, keepdims=True)
    away = jnp.dot(embed_t_ref[0], grad, preferred_element_type=f32).astype(bf16)
    away_ref[...] = away.reshape(away_ref.shape)
    stay = jnp.dot(embed_t_ref[1], grad, preferred_element_type=f32)
    stay_ref[...] = stay.reshape(stay_ref.shape)
    total[...] += jnp.dot(grad, unit_ref[...], preferred_element_type=f32)

    @pl.when(step == pl.num_programs(0) - 1)
    def _():
        for start in range(0, D, TILE):
            part = slice(start, start + TILE)
            terms_ref[part, :] = total[:, part].T.astype(bf16)


def grad_pass(images, softs, masses, unit, embed, embed_t):
    rows, protos = embed.shape[0], unit.shape[0]
    depth = embed_t.shape[1]
    blocks = depth // LANES

    def full(values):
        return pl.BlockSpec(values.shape, lambda i: (0,) * values.ndim)

    halves = pl.BlockSpec((blocks, LANES, TILE), lambda i: (0, 0, i))
    return pl.pallas_call(
        grad_kernel,
        grid=(protos // TILE,),
        in_specs=[
            full(images),
            full(softs),
            pl.BlockSpec((masses.shape[0], 2, TILE), lambda i: (0, 0, i)),
            pl.BlockSpec((TILE, D), lambda i: (i, 0)),
            VMEM,
            VMEM,
        ],
        out_specs=[
            pl.BlockSpec((1, TILE), lambda i: (0, i)),
            halves,
            halves,
            pl.BlockSpec((D, rows), lambda i: (0, 0)),
        ],
        out_shape=[
            jax.ShapeDtypeStruct((1, protos), f32),
            pltpu.HBM((blocks, LANES, protos), bf16),
            pltpu.HBM((blocks, LANES, protos), f32),
            jax.ShapeDtypeStruct((D, rows), bf16),
        ],
        scratch_shapes=[
            pltpu.VMEM((rows, LANES), f32),
            pltpu.VMEM((rows, LANES), f32),
            pltpu.VMEM((rows, D), f32),
        ],
        compiler_params=pltpu.CompilerParams(
            dimension_semantics=("arbitrary",), vmem_limit_bytes=24 * 1024 * 1024
        ),
        cost_estimate=pl.CostEstimate(
            flops=8 * depth * rows * protos,
            bytes_accessed=10 * depth * protos,
            transcendentals=rows * protos,
        ),
    )(images, softs, masses, keep_hbm(unit), embed, embed_t)


def pair_kernel(place_ref, stay_ref, arrived_ref, turned_ref, one_ref, two_ref, length_ref, *rest):
    *others, out_ref = rest
    for part in tiles(out_ref.shape[1]):
        inverse = 1.0 / length_ref[:, part]
        radial = (one_ref[:, part] + two_ref[:, part]) * inverse
        total = stay_ref[0, :, part] + arrived_ref[0, :, part].astype(f32)
        total = (total - turned_ref[0, :, part].astype(f32) * radial) * inverse
        for ref in others:
            total = total + ref[:, part].astype(f32)
        out_ref[:, part] = total.astype(out_ref.dtype)


def pair_call(place, stay, arrived, turned, radials, length, others=()):
    blocks, height, protos = stay.shape

    def full(values):
        return pl.BlockSpec(values.shape, lambda i, p: (0,) * values.ndim)

    return pl.pallas_call(
        pair_kernel,
        grid_spec=pltpu.PrefetchScalarGridSpec(
            num_scalar_prefetch=1,
            grid=(1,),
            in_specs=[pl.BlockSpec((1, height, protos), lambda i, p: (p[0], 0, 0))] * 3
            + [full(values) for values in (*radials, length, *others)],
            out_specs=pl.BlockSpec((height, protos), lambda i, p: (0, 0)),
        ),
        out_shape=jax.ShapeDtypeStruct((height, protos), f32 if others else bf16),
        compiler_params=pltpu.CompilerParams(vmem_limit_bytes=10 * 1024 * 1024),
        cost_estimate=pl.CostEstimate(
            flops=10**9,
            bytes_accessed=10 * height * protos,
            transcendentals=0,
        ),
    )(
        place.reshape(1),
        keep_hbm(stay),
        arrived,
        keep_hbm(turned),
        *radials,
        length,
        *others,
    )


def body(hidden_states, ln_in_gain, w_in, w_out, ln_out_gain, prototypes):
    view_count, image_rows, local_width = hidden_states.shape
    row_count = view_count * image_rows
    col_count = lax.axis_size(COLS)
    row_block = row_count // col_count

    y_count = lax.axis_size("y")
    z_count = lax.axis_size("z")
    tall = row_count // y_count

    states_t = hidden_states.reshape(row_count, local_width).T
    gain_row = jnp.pad(jnp.concatenate([ln_in_gain, ln_out_gain]), (0, tall - 2 * local_width))
    pieces = jnp.concatenate(
        [
            states_t.reshape(local_width, y_count, tall).transpose(1, 0, 2),
            jnp.broadcast_to(gain_row[None, None], (y_count, 8, tall)),
        ],
        axis=1,
    )
    sent = jnp.broadcast_to(pieces[None], (z_count,) + pieces.shape)
    received = lax.all_to_all(
        sent.reshape(col_count, local_width + 8, tall), COLS, 0, 0
    )
    gains = received[:, local_width]
    gain_in = gains[:, :local_width].reshape(D).astype(f32)
    gain_out = gains[:, local_width : 2 * local_width].reshape(D).astype(f32)
    inputs_t = received[:, :local_width].reshape(D, tall)

    core = lax.axis_index("core")
    swap = [(0, 1), (1, 0)]
    w_in_t = w_in.T
    share = jnp.where(core == 0, w_in_t, w_out)
    shares = stack_shares(
        [
            lax.ppermute(share, "y", [(i, (i + step) % y_count) for i in range(y_count)])
            for step in range(1, y_count)
        ]
    )
    others = lax.ppermute(shares, "core", swap)

    inputs_f = inputs_t.astype(f32)
    center = jnp.mean(inputs_f, axis=0)
    spread = jnp.mean(inputs_f * inputs_f, axis=0) - center * center
    normed_t = (
        (inputs_f - center[None, :]) * lax.rsqrt(spread + norm_eps)[None, :] * gain_in[:, None]
    ).astype(bf16)
    block_part = feed_forward(core, normed_t.T, w_in_t, w_out, shares, others)
    block = scatter_sum(block_part.reshape(z_count, row_block, D), "z")
    picked = (
        jnp.arange(tall)[None, :]
        == lax.axis_index("z") * row_block + jnp.arange(row_block)[:, None]
    ).astype(bf16)
    own = lax.dot_general(picked, inputs_t, (((1,), (1,)), ((), ())), preferred_element_type=f32)
    resid = own + block
    center = jnp.mean(resid, axis=1, keepdims=True)
    spread = jnp.mean(resid * resid, axis=1, keepdims=True) - center * center
    final = (resid - center) * lax.rsqrt(spread + norm_eps) * gain_out[None, :]
    squared = jnp.sum(final * final, axis=1, keepdims=True)
    embed_part = (final * lax.rsqrt(squared + unit_eps)).astype(bf16)
    own_rows = gather_all(embed_part, "z").reshape(tall, D)

    x_index = lax.axis_index("x")
    x_count = lax.axis_size("x")
    unit, proto_len, turned = prepare(core, prototypes, x_count)
    proto_count = prototypes.shape[0]
    slice_width = turned.shape[1]

    row_parts = lax.axis_size(ROWS)
    y_index = lax.axis_index("y")
    steps = (1, 3, 2)
    rows_in = {
        step: lax.ppermute(own_rows, "y", [(i, (i + step) % y_count) for i in range(y_count)])
        for step in steps
    }
    places = jnp.stack([(y_index + y_count - step) % y_count for step in (0,) + steps])
    parts = [own_rows] + [rows_in[step] for step in steps]
    base, masses, soft_part, embed = score_pass(places, parts, unit, row_parts)
    embed_t = turn(core, embed)
    masses = lax.all_to_all(masses, ROWS, 0, 0)
    softs = images = lax.all_to_all(image_pass(masses, base, col_count, soft_part), COLS, 0, 0)
    for repeat in range(1, SINK_ITERS):
        masses = lax.all_to_all(proto_pass(images, base, row_parts), ROWS, 0, 0)
        images = lax.all_to_all(image_pass(masses, base, col_count), COLS, 0, 0)

    radial, away, stay, embed_terms = grad_pass(images, softs, masses, unit, embed, embed_t)
    arrived = lax.ppermute(away, "core", swap)
    radials = (radial, lax.ppermute(radial, "core", swap))

    def paired(step, others=()):
        place = (x_index + step) % x_count
        return pair_call(place, stay, arrived, turned, radials, proto_len, others)

    landed = tuple(
        lax.ppermute(paired(step), "x", [(i, (i + step) % x_count) for i in range(x_count)])
        for step in (2, 1, 3)
    )
    proto_grad = paired(0, landed)
    embed_grad_t = scatter_sum(embed_terms.reshape(col_count, local_width, row_count), COLS)
    embed_grad = embed_grad_t.T.reshape(view_count, image_rows, local_width)
    return (embed_grad, proto_grad)


def solution(mesh):
    sizes = {"x": mesh.shape["rows"] // 2, "core": 2, "z": mesh.shape["cols"] // 4, "y": 4}
    fine = Mesh(mesh.devices.reshape(tuple(sizes.values())), tuple(sizes))
    placed = (
        P(None, ROWS, COLS),
        P(COLS),
        P(None, COLS),
        P(COLS, None),
        P(COLS),
        P(COLS, None),
    )
    return jax.shard_map(
        body,
        mesh=fine,
        in_specs=placed,
        out_specs=(P(None, ROWS, COLS), P(ROWS, COLS)),
        check_vma=False,
    )
```

```python
import math

import jax
import jax.numpy as jnp
from jax import lax
from jax.experimental import pallas as pl
from jax.experimental.pallas import tpu as pltpu
from jax.sharding import Mesh, PartitionSpec as P

D = 1024
PROTOS = 65536
SINK_ITERS = 3


sink_temp = 0.05
soft_temp = 0.1
norm_eps = 1e-05
unit_eps = 1e-06

ROWS = ("x", "core")
COLS = ("z", "y")
f32 = jnp.float32
bf16 = jnp.bfloat16


def gather_all(values, axes):
    count = lax.axis_size(axes)
    copies = jnp.broadcast_to(values[None], (count,) + values.shape)
    return lax.all_to_all(copies, axes, 0, 0)


def sum_small(values, axes):
    return jnp.sum(gather_all(values, axes), axis=0)


def scatter_sum(blocks, axes):
    return jnp.sum(lax.all_to_all(blocks, axes, 0, 0).astype(f32), axis=0)


TILE = 512
LANES = 128
factor = 0.5 * math.sqrt(PROTOS * D)
NT = (((1,), (1,)), ((), ()))
VMEM = pl.BlockSpec(memory_space=pltpu.VMEM)
SMEM = pl.BlockSpec(memory_space=pltpu.SMEM)


def keep_hbm(values):
    return pltpu.with_memory_space_constraint(values, pltpu.HBM)


def call(kernel, scalars, arrays, outs, mib, flops, moved, in_hbm=()):
    shapes = [
        pltpu.HBM(shape, dtype) if place in in_hbm else jax.ShapeDtypeStruct(shape, dtype)
        for place, (shape, dtype) in enumerate(outs)
    ]
    many = len(shapes) > 1
    return pl.pallas_call(
        kernel,
        in_specs=[SMEM] * len(scalars) + [VMEM] * len(arrays),
        out_specs=[VMEM] * len(shapes) if many else VMEM,
        out_shape=shapes if many else shapes[0],
        compiler_params=pltpu.CompilerParams(vmem_limit_bytes=mib * 1024 * 1024),
        cost_estimate=pl.CostEstimate(flops=flops, bytes_accessed=moved, transcendentals=0),
    )(*scalars, *arrays)


def fold_lanes(values):
    width = values.shape[1]
    return sum(values[:, j : j + LANES] for j in range(0, width, LANES))


def as_column(row):
    return jnp.broadcast_to(row, (LANES, row.shape[1])).T


def as_row(column):
    return jnp.sum(column.T, axis=0, keepdims=True)


def spread_lanes(column, width):
    return jnp.concatenate([column] * (width // LANES), axis=1)


def view_rows(pair, count):
    half = count // 2
    width = pair.shape[1]
    return jnp.concatenate(
        [jnp.broadcast_to(pair[v : v + 1], (half, width)) for v in range(2)], axis=0
    )


def view_sums(values):
    half = values.shape[0] // 2
    return jnp.concatenate(
        [jnp.sum(values[v * half : (v + 1) * half], axis=0, keepdims=True) for v in range(2)],
        axis=0,
    )


def tiles(count):
    return [slice(j, j + TILE) for j in range(0, count, TILE)]


def stack_kernel(first_ref, second_ref, third_ref, out_ref):
    for place, ref in enumerate((first_ref, second_ref, third_ref)):
        out_ref[place] = ref[...]


def stack_shares(parts):
    return call(
        stack_kernel, (), parts, [((3,) + parts[0].shape, bf16)], 2, 40 * 10**9, 4 * parts[0].size
    )


def ffn_kernel(core_ref, normed_ref, w_in_ref, w_out_ref, shares_ref, others_ref, out_ref):
    normed = normed_ref[...]
    even = core_ref[0] == 0
    total = jnp.zeros(out_ref.shape, f32)
    for step in range(shares_ref.shape[0] + 1):
        if step == 0:
            enter, leave = w_in_ref[...], w_out_ref[...]
        else:
            one, other = shares_ref[step - 1], others_ref[step - 1]
            enter, leave = jnp.where(even, one, other), jnp.where(even, other, one)
        wide = lax.dot_general(normed, enter, NT, preferred_element_type=f32)
        hidden = (0.5 * wide * (1.0 + lax.erf(wide * math.sqrt(0.5)))).astype(bf16)
        total = total + jnp.dot(hidden, leave, preferred_element_type=f32)
    out_ref[...] = total.astype(bf16)


def feed_forward(core, normed, w_in_t, w_out, shares, others):
    rows = normed.shape[0]
    return call(
        ffn_kernel,
        (core.reshape(1),),
        (normed, w_in_t, w_out, shares, others),
        [((rows, D), bf16)],
        8,
        4 * rows * D * 4 * w_out.shape[0],
        8 * w_out.size,
    )


def prepare_kernel(core_ref, proto_ref, unit_ref, length_ref, turned_ref):
    even = core_ref[0] == 0
    for part in tiles(proto_ref.shape[0]):
        values = proto_ref[part, :].astype(f32)
        squares = values * values
        inverse = lax.rsqrt(jnp.sum(squares, axis=1, keepdims=True) + unit_eps)
        unit_ref[part, :] = (values * inverse).astype(bf16)
        length_ref[:, part] = jnp.sqrt(as_row(fold_lanes(squares)) + unit_eps)
        for block in range(turned_ref.shape[0]):
            start = 2 * block * LANES
            low = values[:, start : start + LANES]
            high = values[:, start + LANES : start + 2 * LANES]
            turned_ref[block, :, part] = jnp.where(even, low, high).T.astype(bf16)


def prepare(core, prototypes, x_count):
    protos = prototypes.shape[0]
    return call(
        prepare_kernel,
        (core.reshape(1),),
        (prototypes,),
        [((protos, D), bf16), ((1, protos), f32), ((x_count, LANES, protos), bf16)],
        12,
        6 * protos * D,
        5 * protos * D,
        (2,),
    )


def scores_kernel(place_ref, *rest):
    *block_refs, unit_ref, base_ref, mass_ref, soft_ref, embed_ref = rest
    height = block_refs[0].shape[0]
    for n, ref in enumerate(block_refs):
        embed_ref[pl.ds(pl.multiple_of(place_ref[n] * height, height), height), :] = ref[...]
    total = jnp.zeros((base_ref.shape[0], LANES), f32)
    for part in tiles(unit_ref.shape[0]):
        scores = lax.dot_general(
            embed_ref[...], unit_ref[part, :], NT, preferred_element_type=f32
        )
        soft = jnp.exp(scores * (1.0 / soft_temp))
        base = soft * soft
        base_ref[:, part] = base.astype(bf16)
        mass = view_sums(base)
        mass_ref[:, :, part] = jnp.broadcast_to(mass[None], (mass_ref.shape[0],) + mass.shape)
        total = total + fold_lanes(soft)
    soft_ref[...] = as_row(total)


def score_pass(places, parts, unit, copies):
    height, protos = parts[0].shape[0], unit.shape[0]
    rows = height * len(parts)
    return call(
        scores_kernel,
        (places,),
        (*parts, unit),
        [
            ((rows, protos), bf16),
            ((copies, 2, protos), f32),
            ((1, rows), f32),
            ((rows, D), bf16),
        ],
        10,
        2 * rows * protos * D,
        8 * rows * protos,
    )


def turn_kernel(core_ref, embed_ref, turned_ref):
    even = core_ref[0] == 0
    for block in range(D // (2 * LANES)):
        start = 2 * block * LANES
        low = embed_ref[:, start : start + LANES].astype(f32)
        high = embed_ref[:, start + LANES : start + 2 * LANES].astype(f32)
        rows = slice(block * LANES, (block + 1) * LANES)
        turned_ref[0, rows, :] = jnp.where(even, high, low).T.astype(bf16)
        turned_ref[1, rows, :] = jnp.where(even, low, high).T.astype(bf16)


def turn(core, embed):
    rows = embed.shape[0]
    return call(
        turn_kernel, (core.reshape(1),), (embed,), [((2, D // 2, rows), bf16)], 6, 10**9, 4 * embed.size
    )


def image_kernel(mass_ref, base_ref, *rest):
    *extra, out_ref = rest
    rows, protos = base_ref.shape
    total = jnp.zeros((rows, LANES), f32)
    for part in tiles(protos):
        scale = 1.0 / jnp.sum(mass_ref[:, :, part], axis=0)
        total = total + fold_lanes(base_ref[:, part].astype(f32) * view_rows(scale, rows))
    row = jnp.concatenate([as_row(total)] + [ref[...] for ref in extra], axis=0)
    out_ref[...] = jnp.broadcast_to(row[None], out_ref.shape)


def image_pass(masses, base, copies, *extra):
    rows, protos = base.shape
    return call(
        image_kernel,
        (),
        (masses, base, *extra),
        [((copies, 1 + len(extra), rows), f32)],
        8,
        3 * rows * protos,
        2 * rows * protos,
    )


def proto_kernel(image_ref, base_ref, mass_ref):
    column = as_column(1.0 / jnp.sum(image_ref[...], axis=0)[:1])
    for part in tiles(base_ref.shape[1]):
        mass = view_sums(base_ref[:, part].astype(f32) * spread_lanes(column, TILE))
        mass_ref[:, :, part] = jnp.broadcast_to(mass[None], (mass_ref.shape[0],) + mass.shape)


def proto_pass(images, base, copies):
    rows, protos = base.shape
    return call(
        proto_kernel,
        (),
        (images, base),
        [((copies, 2, protos), f32)],
        8,
        3 * rows * protos,
        2 * rows * protos,
    )


def grad_kernel(
    image_ref, soft_ref, mass_ref, unit_ref, embed_ref, embed_t_ref,
    radial_ref, away_ref, stay_ref, terms_ref, code_column, prob_column, total,
):
    step = pl.program_id(0)

    @pl.when(step == 0)
    def _():
        code_column[...] = as_column(factor / jnp.sum(image_ref[...], axis=0)[:1])
        prob_column[...] = as_column(factor / jnp.sum(soft_ref[...], axis=0)[1:2])
        total[...] = jnp.zeros_like(total)

    scores = lax.dot_general(embed_ref[...], unit_ref[...], NT, preferred_element_type=f32)
    rows = scores.shape[0]
    half = rows // 2
    soft = jnp.exp(scores * (1.0 / soft_temp))
    scale = 1.0 / jnp.sum(mass_ref[...], axis=0)
    codes = soft * soft * view_rows(scale, rows) * spread_lanes(code_column[...], TILE)
    swapped = jnp.concatenate([codes[half:], codes[:half]], axis=0)
    grad = (soft * spread_lanes(prob_column[...], TILE) - swapped).astype(bf16)
    radial_ref[...] = jnp.sum(grad.astype(f32) * scores, axis=0, keepdims=True)
    away = jnp.dot(embed_t_ref[0], grad, preferred_element_type=f32).astype(bf16)
    away_ref[...] = away.reshape(away_ref.shape)
    stay = jnp.dot(embed_t_ref[1], grad, preferred_element_type=f32)
    stay_ref[...] = stay.reshape(stay_ref.shape)
    total[...] += jnp.dot(grad, unit_ref[...], preferred_element_type=f32)

    @pl.when(step == pl.num_programs(0) - 1)
    def _():
        for start in range(0, D, TILE):
            part = slice(start, start + TILE)
            terms_ref[part, :] = total[:, part].T.astype(bf16)


def grad_pass(images, softs, masses, unit, embed, embed_t):
    rows, protos = embed.shape[0], unit.shape[0]
    depth = embed_t.shape[1]
    blocks = depth // LANES

    def full(values):
        return pl.BlockSpec(values.shape, lambda i: (0,) * values.ndim)

    halves = pl.BlockSpec((blocks, LANES, TILE), lambda i: (0, 0, i))
    return pl.pallas_call(
        grad_kernel,
        grid=(protos // TILE,),
        in_specs=[
            full(images),
            full(softs),
            pl.BlockSpec((masses.shape[0], 2, TILE), lambda i: (0, 0, i)),
            pl.BlockSpec((TILE, D), lambda i: (i, 0)),
            VMEM,
            VMEM,
        ],
        out_specs=[
            pl.BlockSpec((1, TILE), lambda i: (0, i)),
            halves,
            halves,
            pl.BlockSpec((D, rows), lambda i: (0, 0)),
        ],
        out_shape=[
            jax.ShapeDtypeStruct((1, protos), f32),
            pltpu.HBM((blocks, LANES, protos), bf16),
            pltpu.HBM((blocks, LANES, protos), f32),
            jax.ShapeDtypeStruct((D, rows), bf16),
        ],
        scratch_shapes=[
            pltpu.VMEM((rows, LANES), f32),
            pltpu.VMEM((rows, LANES), f32),
            pltpu.VMEM((rows, D), f32),
        ],
        compiler_params=pltpu.CompilerParams(
            dimension_semantics=("arbitrary",), vmem_limit_bytes=24 * 1024 * 1024
        ),
        cost_estimate=pl.CostEstimate(
            flops=8 * depth * rows * protos,
            bytes_accessed=10 * depth * protos,
            transcendentals=rows * protos,
        ),
    )(images, softs, masses, keep_hbm(unit), embed, embed_t)


def pair_rows(refs, rows, part):
    stay_ref, arrived_ref, turned_ref, one_ref, two_ref, length_ref = refs
    inverse = 1.0 / length_ref[:, part]
    radial = (one_ref[:, part] + two_ref[:, part]) * inverse
    total = stay_ref[0, rows, part] + arrived_ref[0, rows, part].astype(f32)
    return (total - turned_ref[0, rows, part].astype(f32) * radial) * inverse


LOWER = slice(0, LANES // 2)
UPPER = slice(LANES // 2, LANES)
ALL = slice(0, LANES)


def far_kernel(place_ref, *refs):
    *given, lower_ref, upper_ref = refs
    for part in tiles(lower_ref.shape[1]):
        lower_ref[:, part] = pair_rows(given, LOWER, part).astype(bf16)
        upper_ref[:, part] = pair_rows(given, UPPER, part).astype(bf16)


def near_kernel(place_ref, *refs):
    right, left, lines = refs[:3], refs[3:6], refs[6:9]
    right_send, left_send, right_keep, left_keep = refs[9:]
    for part in tiles(right_send.shape[1]):
        right_send[:, part] = pair_rows((*right, *lines), UPPER, part).astype(bf16)
        left_send[:, part] = pair_rows((*left, *lines), LOWER, part).astype(bf16)
        right_keep[:, part] = pair_rows((*right, *lines), LOWER, part)
        left_keep[:, part] = pair_rows((*left, *lines), UPPER, part)


def own_kernel(place_ref, *refs):
    *given, lower_ref, upper_ref, out_ref = refs
    for part in tiles(out_ref.shape[1]):
        out_ref[LOWER, part] = pair_rows(given, LOWER, part) + lower_ref[:, part].astype(f32)
        out_ref[UPPER, part] = pair_rows(given, UPPER, part) + upper_ref[:, part].astype(f32)


def relay_kernel(right_keep, left_keep, lower_ref, upper_ref, right_send, left_send):
    for part in tiles(right_send.shape[1]):
        right_send[:, part] = (right_keep[:, part] + lower_ref[:, part].astype(f32)).astype(bf16)
        left_send[:, part] = (left_keep[:, part] + upper_ref[:, part].astype(f32)).astype(bf16)


def final_kernel(sum_ref, lower_ref, upper_ref, out_ref):
    for part in tiles(out_ref.shape[1]):
        out_ref[LOWER, part] = sum_ref[LOWER, part] + lower_ref[:, part].astype(f32)
        out_ref[UPPER, part] = sum_ref[UPPER, part] + upper_ref[:, part].astype(f32)


def pair_call(kernel, places, parts, lines, outs, others=()):
    blocks, height, protos = parts[0].shape

    def picked(n):
        return pl.BlockSpec((1, height, protos), lambda i, p: (p[n], 0, 0))

    def full(shape):
        return pl.BlockSpec(shape, lambda i, p: (0,) * len(shape))

    stay, arrived, turned = parts
    given = [keep_hbm(stay), arrived, keep_hbm(turned)] * len(places)
    many = len(outs) > 1
    shapes = [jax.ShapeDtypeStruct(shape, dtype) for shape, dtype in outs]
    specs = [full(shape) for shape, dtype in outs]
    return pl.pallas_call(
        kernel,
        grid_spec=pltpu.PrefetchScalarGridSpec(
            num_scalar_prefetch=1,
            grid=(1,),
            in_specs=[picked(n) for n in range(len(places)) for _ in range(3)]
            + [full(values.shape) for values in (*lines, *others)],
            out_specs=specs if many else specs[0],
        ),
        out_shape=shapes if many else shapes[0],
        compiler_params=pltpu.CompilerParams(vmem_limit_bytes=16 * 1024 * 1024),
        cost_estimate=pl.CostEstimate(
            flops=10**9, bytes_accessed=10 * height * protos, transcendentals=0
        ),
    )(jnp.stack(places), *given, *lines, *others)


def body(hidden_states, ln_in_gain, w_in, w_out, ln_out_gain, prototypes):
    view_count, image_rows, local_width = hidden_states.shape
    row_count = view_count * image_rows
    col_count = lax.axis_size(COLS)
    row_block = row_count // col_count

    y_count = lax.axis_size("y")
    z_count = lax.axis_size("z")
    tall = row_count // y_count

    states_t = hidden_states.reshape(row_count, local_width).T
    gain_row = jnp.pad(jnp.concatenate([ln_in_gain, ln_out_gain]), (0, tall - 2 * local_width))
    pieces = jnp.concatenate(
        [
            states_t.reshape(local_width, y_count, tall).transpose(1, 0, 2),
            jnp.broadcast_to(gain_row[None, None], (y_count, 8, tall)),
        ],
        axis=1,
    )
    sent = jnp.broadcast_to(pieces[None], (z_count,) + pieces.shape)
    received = lax.all_to_all(
        sent.reshape(col_count, local_width + 8, tall), COLS, 0, 0
    )
    gains = received[:, local_width]
    gain_in = gains[:, :local_width].reshape(D).astype(f32)
    gain_out = gains[:, local_width : 2 * local_width].reshape(D).astype(f32)
    inputs_t = received[:, :local_width].reshape(D, tall)

    core = lax.axis_index("core")
    swap = [(0, 1), (1, 0)]
    w_in_t = w_in.T
    share = jnp.where(core == 0, w_in_t, w_out)
    shares = stack_shares(
        [
            lax.ppermute(share, "y", [(i, (i + step) % y_count) for i in range(y_count)])
            for step in range(1, y_count)
        ]
    )
    others = lax.ppermute(shares, "core", swap)

    inputs_f = inputs_t.astype(f32)
    center = jnp.mean(inputs_f, axis=0)
    spread = jnp.mean(inputs_f * inputs_f, axis=0) - center * center
    normed_t = (
        (inputs_f - center[None, :]) * lax.rsqrt(spread + norm_eps)[None, :] * gain_in[:, None]
    ).astype(bf16)
    block_part = feed_forward(core, normed_t.T, w_in_t, w_out, shares, others)
    block = scatter_sum(block_part.reshape(z_count, row_block, D), "z")
    picked = (
        jnp.arange(tall)[None, :]
        == lax.axis_index("z") * row_block + jnp.arange(row_block)[:, None]
    ).astype(bf16)
    own = lax.dot_general(picked, inputs_t, (((1,), (1,)), ((), ())), preferred_element_type=f32)
    resid = own + block
    center = jnp.mean(resid, axis=1, keepdims=True)
    spread = jnp.mean(resid * resid, axis=1, keepdims=True) - center * center
    final = (resid - center) * lax.rsqrt(spread + norm_eps) * gain_out[None, :]
    squared = jnp.sum(final * final, axis=1, keepdims=True)
    embed_part = (final * lax.rsqrt(squared + unit_eps)).astype(bf16)
    own_rows = gather_all(embed_part, "z").reshape(tall, D)

    x_index = lax.axis_index("x")
    x_count = lax.axis_size("x")
    unit, proto_len, turned = prepare(core, prototypes, x_count)
    proto_count = prototypes.shape[0]
    slice_width = turned.shape[1]

    row_parts = lax.axis_size(ROWS)
    y_index = lax.axis_index("y")
    steps = (1, 3, 2)
    rows_in = {
        step: lax.ppermute(own_rows, "y", [(i, (i + step) % y_count) for i in range(y_count)])
        for step in steps
    }
    places = jnp.stack([(y_index + y_count - step) % y_count for step in (0,) + steps])
    parts = [own_rows] + [rows_in[step] for step in steps]
    base, masses, soft_part, embed = score_pass(places, parts, unit, row_parts)
    embed_t = turn(core, embed)
    masses = lax.all_to_all(masses, ROWS, 0, 0)
    softs = images = lax.all_to_all(image_pass(masses, base, col_count, soft_part), COLS, 0, 0)
    for repeat in range(1, SINK_ITERS):
        masses = lax.all_to_all(proto_pass(images, base, row_parts), ROWS, 0, 0)
        images = lax.all_to_all(image_pass(masses, base, col_count), COLS, 0, 0)

    radial, away, stay, embed_terms = grad_pass(images, softs, masses, unit, embed, embed_t)
    arrived = lax.ppermute(away, "core", swap)
    parts = (stay, arrived, turned)
    lines = (radial, lax.ppermute(radial, "core", swap), proto_len)
    flat = (slice_width // 2, proto_count)

    def spot(step):
        return (x_index + step) % x_count

    def right(values):
        return lax.ppermute(values, "x", [(i, (i + 1) % x_count) for i in range(x_count)])

    def left(values):
        return lax.ppermute(values, "x", [((i + 1) % x_count, i) for i in range(x_count)])

    far_lower, far_upper = pair_call(far_kernel, (spot(2),), parts, lines, [(flat, bf16)] * 2)
    came_lower, came_upper = right(far_lower), left(far_upper)
    right_send, left_send, right_keep, left_keep = pair_call(
        near_kernel, (spot(1), spot(3)), parts, lines, [(flat, bf16)] * 2 + [(flat, f32)] * 2
    )
    near_upper, near_lower = right(right_send), left(left_send)
    own_sum = pair_call(
        own_kernel,
        (x_index,),
        parts,
        lines,
        [((slice_width, proto_count), f32)],
        (near_lower, near_upper),
    )
    right_relay, left_relay = call(
        relay_kernel,
        (),
        (right_keep, left_keep, came_lower, came_upper),
        [(flat, bf16)] * 2,
        8,
        10**8,
        10**6,
    )
    last_lower, last_upper = right(right_relay), left(left_relay)
    proto_grad = call(
        final_kernel,
        (),
        (own_sum, last_lower, last_upper),
        [((slice_width, proto_count), f32)],
        8,
        10**8,
        10**6,
    )
    embed_grad_t = scatter_sum(embed_terms.reshape(col_count, local_width, row_count), COLS)
    embed_grad = embed_grad_t.T.reshape(view_count, image_rows, local_width)
    return (embed_grad, proto_grad)


def solution(mesh):
    sizes = {"x": mesh.shape["rows"] // 2, "core": 2, "z": mesh.shape["cols"] // 4, "y": 4}
    fine = Mesh(mesh.devices.reshape(tuple(sizes.values())), tuple(sizes))
    placed = (
        P(None, ROWS, COLS),
        P(COLS),
        P(None, COLS),
        P(COLS, None),
        P(COLS),
        P(COLS, None),
    )
    return jax.shard_map(
        body,
        mesh=fine,
        in_specs=placed,
        out_specs=(P(None, ROWS, COLS), P(ROWS, COLS)),
        check_vma=False,
    )
```

```python
import functools
import math

import jax
import jax.numpy as jnp
from jax import lax
from jax.experimental import pallas as pl
from jax.experimental.pallas import tpu as pltpu
from jax.sharding import Mesh, PartitionSpec as P

D = 1024
PROTOS = 65536
SINK_ITERS = 3


sink_temp = 0.05
soft_temp = 0.1
norm_eps = 1e-05
unit_eps = 1e-06

ROWS = ("x", "core")
COLS = ("z", "y")
f32 = jnp.float32
bf16 = jnp.bfloat16


def gather_all(values, axes):
    count = lax.axis_size(axes)
    copies = jnp.broadcast_to(values[None], (count,) + values.shape)
    return lax.all_to_all(copies, axes, 0, 0)


def sum_small(values, axes):
    return jnp.sum(gather_all(values, axes), axis=0)


def scatter_sum(blocks, axes):
    return jnp.sum(lax.all_to_all(blocks, axes, 0, 0).astype(f32), axis=0)


TILE = 512
LANES = 128
factor = 0.5 * math.sqrt(PROTOS * D)
NT = (((1,), (1,)), ((), ()))
VMEM = pl.BlockSpec(memory_space=pltpu.VMEM)
SMEM = pl.BlockSpec(memory_space=pltpu.SMEM)


def keep_hbm(values):
    return pltpu.with_memory_space_constraint(values, pltpu.HBM)


def call(kernel, scalars, arrays, outs, mib, flops, moved, in_hbm=()):
    shapes = [
        pltpu.HBM(shape, dtype) if place in in_hbm else jax.ShapeDtypeStruct(shape, dtype)
        for place, (shape, dtype) in enumerate(outs)
    ]
    many = len(shapes) > 1
    return pl.pallas_call(
        kernel,
        in_specs=[SMEM] * len(scalars) + [VMEM] * len(arrays),
        out_specs=[VMEM] * len(shapes) if many else VMEM,
        out_shape=shapes if many else shapes[0],
        compiler_params=pltpu.CompilerParams(vmem_limit_bytes=mib * 1024 * 1024),
        cost_estimate=pl.CostEstimate(flops=flops, bytes_accessed=moved, transcendentals=0),
    )(*scalars, *arrays)


def fold_lanes(values):
    width = values.shape[1]
    return sum(values[:, j : j + LANES] for j in range(0, width, LANES))


def as_column(row):
    return jnp.broadcast_to(row, (LANES, row.shape[1])).T


def as_row(column):
    return jnp.sum(column.T, axis=0, keepdims=True)


def spread_lanes(column, width):
    return jnp.concatenate([column] * (width // LANES), axis=1)


def view_rows(pair, count):
    half = count // 2
    width = pair.shape[1]
    return jnp.concatenate(
        [jnp.broadcast_to(pair[v : v + 1], (half, width)) for v in range(2)], axis=0
    )


def view_sums(values):
    half = values.shape[0] // 2
    return jnp.concatenate(
        [jnp.sum(values[v * half : (v + 1) * half], axis=0, keepdims=True) for v in range(2)],
        axis=0,
    )


def tiles(count):
    return [slice(j, j + TILE) for j in range(0, count, TILE)]


def pack_kernel(y_count, states_ref, in_ref, last_ref, out_ref):
    width = in_ref.shape[1]
    height = out_ref.shape[2]
    pair = jnp.concatenate([in_ref[...].astype(f32), last_ref[...].astype(f32)], axis=0)
    row = jnp.concatenate([pair, jnp.zeros((2, height - width), f32)], axis=1)
    foot = jnp.concatenate([row, jnp.zeros((6, height), f32)], axis=0)
    for way in range(y_count):
        view, start = divmod(way * height, states_ref.shape[2])
        block = states_ref[view, :, start : start + height].astype(f32)
        piece = jnp.concatenate([block, foot], axis=0).astype(bf16)
        for group in range(out_ref.shape[0] // y_count):
            out_ref[group * y_count + way] = piece


def pack_states(states, gain_in, gain_out, z_count, y_count):
    views, width, rows = states.shape
    height = views * rows // y_count
    return call(
        functools.partial(pack_kernel, y_count),
        (),
        (states, gain_in.reshape(1, width), gain_out.reshape(1, width)),
        [((z_count * y_count, width + 8, height), bf16)],
        4,
        10**6,
        10**6,
    )


def stack_kernel(first_ref, second_ref, third_ref, out_ref):
    for place, ref in enumerate((first_ref, second_ref, third_ref)):
        out_ref[place] = ref[...]


def stack_shares(parts):
    return call(
        stack_kernel, (), parts, [((3,) + parts[0].shape, bf16)], 2, 40 * 10**9, 4 * parts[0].size
    )


def ffn_kernel(core_ref, normed_ref, w_in_ref, w_out_ref, shares_ref, others_ref, out_ref):
    normed = normed_ref[...]
    even = core_ref[0] == 0
    total = jnp.zeros(out_ref.shape, f32)
    for step in range(shares_ref.shape[0] + 1):
        if step == 0:
            enter, leave = w_in_ref[...], w_out_ref[...]
        else:
            one, other = shares_ref[step - 1], others_ref[step - 1]
            enter, leave = jnp.where(even, one, other), jnp.where(even, other, one)
        wide = lax.dot_general(normed, enter, NT, preferred_element_type=f32)
        hidden = (0.5 * wide * (1.0 + lax.erf(wide * math.sqrt(0.5)))).astype(bf16)
        total = total + jnp.dot(hidden, leave, preferred_element_type=f32)
    out_ref[...] = total.astype(bf16)


def feed_forward(core, normed, w_in_t, w_out, shares, others):
    rows = normed.shape[0]
    return call(
        ffn_kernel,
        (core.reshape(1),),
        (normed, w_in_t, w_out, shares, others),
        [((rows, D), bf16)],
        8,
        4 * rows * D * 4 * w_out.shape[0],
        8 * w_out.size,
    )


def prepare_kernel(core_ref, proto_ref, unit_ref, length_ref, turned_ref):
    even = core_ref[0] == 0
    for part in tiles(proto_ref.shape[0]):
        values = proto_ref[part, :].astype(f32)
        squares = values * values
        inverse = lax.rsqrt(jnp.sum(squares, axis=1, keepdims=True) + unit_eps)
        unit_ref[part, :] = (values * inverse).astype(bf16)
        length_ref[:, part] = jnp.sqrt(as_row(fold_lanes(squares)) + unit_eps)
        for block in range(turned_ref.shape[0]):
            start = 2 * block * LANES
            low = values[:, start : start + LANES]
            high = values[:, start + LANES : start + 2 * LANES]
            turned_ref[block, :, part] = jnp.where(even, low, high).T.astype(bf16)


def prepare(core, prototypes, x_count):
    protos = prototypes.shape[0]
    return call(
        prepare_kernel,
        (core.reshape(1),),
        (prototypes,),
        [((protos, D), bf16), ((1, protos), f32), ((x_count, LANES, protos), bf16)],
        12,
        6 * protos * D,
        5 * protos * D,
        (2,),
    )


def scores_kernel(place_ref, *rest):
    *block_refs, unit_ref, base_ref, mass_ref, soft_ref, embed_ref = rest
    height = block_refs[0].shape[0]
    for n, ref in enumerate(block_refs):
        embed_ref[pl.ds(pl.multiple_of(place_ref[n] * height, height), height), :] = ref[...]
    total = jnp.zeros((base_ref.shape[0], LANES), f32)
    for part in tiles(unit_ref.shape[0]):
        scores = lax.dot_general(
            embed_ref[...], unit_ref[part, :], NT, preferred_element_type=f32
        )
        soft = jnp.exp(scores * (1.0 / soft_temp))
        base = soft * soft
        base_ref[:, part] = base.astype(bf16)
        mass = view_sums(base)
        mass_ref[:, :, part] = jnp.broadcast_to(mass[None], (mass_ref.shape[0],) + mass.shape)
        total = total + fold_lanes(soft)
    soft_ref[...] = as_row(total)


def score_pass(places, parts, unit, copies):
    height, protos = parts[0].shape[0], unit.shape[0]
    rows = height * len(parts)
    return call(
        scores_kernel,
        (places,),
        (*parts, unit),
        [
            ((rows, protos), bf16),
            ((copies, 2, protos), f32),
            ((1, rows), f32),
            ((rows, D), bf16),
        ],
        10,
        2 * rows * protos * D,
        8 * rows * protos,
    )


def turn_kernel(core_ref, embed_ref, turned_ref):
    even = core_ref[0] == 0
    for block in range(D // (2 * LANES)):
        start = 2 * block * LANES
        low = embed_ref[:, start : start + LANES].astype(f32)
        high = embed_ref[:, start + LANES : start + 2 * LANES].astype(f32)
        rows = slice(block * LANES, (block + 1) * LANES)
        turned_ref[0, rows, :] = jnp.where(even, high, low).T.astype(bf16)
        turned_ref[1, rows, :] = jnp.where(even, low, high).T.astype(bf16)


def turn(core, embed):
    rows = embed.shape[0]
    return call(
        turn_kernel, (core.reshape(1),), (embed,), [((2, D // 2, rows), bf16)], 6, 10**9, 4 * embed.size
    )


def image_kernel(mass_ref, base_ref, *rest):
    *extra, out_ref = rest
    rows, protos = base_ref.shape
    total = jnp.zeros((rows, LANES), f32)
    for part in tiles(protos):
        scale = 1.0 / jnp.sum(mass_ref[:, :, part], axis=0)
        total = total + fold_lanes(base_ref[:, part].astype(f32) * view_rows(scale, rows))
    row = jnp.concatenate([as_row(total)] + [ref[...] for ref in extra], axis=0)
    out_ref[...] = jnp.broadcast_to(row[None], out_ref.shape)


def image_pass(masses, base, copies, *extra):
    rows, protos = base.shape
    return call(
        image_kernel,
        (),
        (masses, base, *extra),
        [((copies, 1 + len(extra), rows), f32)],
        8,
        3 * rows * protos,
        2 * rows * protos,
    )


def proto_kernel(image_ref, base_ref, mass_ref):
    column = as_column(1.0 / jnp.sum(image_ref[...], axis=0)[:1])
    for part in tiles(base_ref.shape[1]):
        mass = view_sums(base_ref[:, part].astype(f32) * spread_lanes(column, TILE))
        mass_ref[:, :, part] = jnp.broadcast_to(mass[None], (mass_ref.shape[0],) + mass.shape)


def proto_pass(images, base, copies):
    rows, protos = base.shape
    return call(
        proto_kernel,
        (),
        (images, base),
        [((copies, 2, protos), f32)],
        8,
        3 * rows * protos,
        2 * rows * protos,
    )


def grad_kernel(
    image_ref, soft_ref, mass_ref, unit_ref, embed_ref, embed_t_ref,
    radial_ref, away_ref, stay_ref, terms_ref, code_column, prob_column, total,
):
    step = pl.program_id(0)

    @pl.when(step == 0)
    def _():
        code_column[...] = as_column(factor / jnp.sum(image_ref[...], axis=0)[:1])
        prob_column[...] = as_column(factor / jnp.sum(soft_ref[...], axis=0)[1:2])
        total[...] = jnp.zeros_like(total)

    scores = lax.dot_general(embed_ref[...], unit_ref[...], NT, preferred_element_type=f32)
    rows = scores.shape[0]
    half = rows // 2
    soft = jnp.exp(scores * (1.0 / soft_temp))
    scale = 1.0 / jnp.sum(mass_ref[...], axis=0)
    codes = soft * soft * view_rows(scale, rows) * spread_lanes(code_column[...], TILE)
    swapped = jnp.concatenate([codes[half:], codes[:half]], axis=0)
    grad = (soft * spread_lanes(prob_column[...], TILE) - swapped).astype(bf16)
    radial_ref[...] = jnp.sum(grad.astype(f32) * scores, axis=0, keepdims=True)
    away = jnp.dot(embed_t_ref[0], grad, preferred_element_type=f32).astype(bf16)
    away_ref[...] = away.reshape(away_ref.shape)
    stay = jnp.dot(embed_t_ref[1], grad, preferred_element_type=f32)
    stay_ref[...] = stay.reshape(stay_ref.shape)
    total[...] += jnp.dot(grad, unit_ref[...], preferred_element_type=f32)

    @pl.when(step == pl.num_programs(0) - 1)
    def _():
        for start in range(0, D, TILE):
            part = slice(start, start + TILE)
            terms_ref[part, :] = total[:, part].T.astype(bf16)


def grad_pass(images, softs, masses, unit, embed, embed_t):
    rows, protos = embed.shape[0], unit.shape[0]
    depth = embed_t.shape[1]
    blocks = depth // LANES

    def full(values):
        return pl.BlockSpec(values.shape, lambda i: (0,) * values.ndim)

    halves = pl.BlockSpec((blocks, LANES, TILE), lambda i: (0, 0, i))
    return pl.pallas_call(
        grad_kernel,
        grid=(protos // TILE,),
        in_specs=[
            full(images),
            full(softs),
            pl.BlockSpec((masses.shape[0], 2, TILE), lambda i: (0, 0, i)),
            pl.BlockSpec((TILE, D), lambda i: (i, 0)),
            VMEM,
            VMEM,
        ],
        out_specs=[
            pl.BlockSpec((1, TILE), lambda i: (0, i)),
            halves,
            halves,
            pl.BlockSpec((D, rows), lambda i: (0, 0)),
        ],
        out_shape=[
            jax.ShapeDtypeStruct((1, protos), f32),
            pltpu.HBM((blocks, LANES, protos), bf16),
            pltpu.HBM((blocks, LANES, protos), f32),
            jax.ShapeDtypeStruct((D, rows), bf16),
        ],
        scratch_shapes=[
            pltpu.VMEM((rows, LANES), f32),
            pltpu.VMEM((rows, LANES), f32),
            pltpu.VMEM((rows, D), f32),
        ],
        compiler_params=pltpu.CompilerParams(
            dimension_semantics=("arbitrary",), vmem_limit_bytes=24 * 1024 * 1024
        ),
        cost_estimate=pl.CostEstimate(
            flops=8 * depth * rows * protos,
            bytes_accessed=10 * depth * protos,
            transcendentals=rows * protos,
        ),
    )(images, softs, masses, keep_hbm(unit), embed, embed_t)


def pair_rows(refs, rows, part):
    stay_ref, arrived_ref, turned_ref, one_ref, two_ref, length_ref = refs
    inverse = 1.0 / length_ref[:, part]
    radial = (one_ref[:, part] + two_ref[:, part]) * inverse
    total = stay_ref[0, rows, part] + arrived_ref[0, rows, part].astype(f32)
    return (total - turned_ref[0, rows, part].astype(f32) * radial) * inverse


LOWER = slice(0, LANES // 2)
UPPER = slice(LANES // 2, LANES)
ALL = slice(0, LANES)


def far_kernel(place_ref, *refs):
    *given, lower_ref, upper_ref = refs
    for part in tiles(lower_ref.shape[1]):
        lower_ref[:, part] = pair_rows(given, LOWER, part).astype(bf16)
        upper_ref[:, part] = pair_rows(given, UPPER, part).astype(bf16)


def near_kernel(place_ref, *refs):
    right, left, lines = refs[:3], refs[3:6], refs[6:9]
    right_send, left_send, right_keep, left_keep = refs[9:]
    for part in tiles(right_send.shape[1]):
        right_send[:, part] = pair_rows((*right, *lines), UPPER, part).astype(bf16)
        left_send[:, part] = pair_rows((*left, *lines), LOWER, part).astype(bf16)
        right_keep[:, part] = pair_rows((*right, *lines), LOWER, part)
        left_keep[:, part] = pair_rows((*left, *lines), UPPER, part)


def own_kernel(place_ref, *refs):
    *given, lower_ref, upper_ref, out_ref = refs
    for part in tiles(out_ref.shape[1]):
        out_ref[LOWER, part] = pair_rows(given, LOWER, part) + lower_ref[:, part].astype(f32)
        out_ref[UPPER, part] = pair_rows(given, UPPER, part) + upper_ref[:, part].astype(f32)


def relay_kernel(right_keep, left_keep, lower_ref, upper_ref, right_send, left_send):
    for part in tiles(right_send.shape[1]):
        right_send[:, part] = (right_keep[:, part] + lower_ref[:, part].astype(f32)).astype(bf16)
        left_send[:, part] = (left_keep[:, part] + upper_ref[:, part].astype(f32)).astype(bf16)


def final_kernel(sum_ref, lower_ref, upper_ref, out_ref):
    for part in tiles(out_ref.shape[1]):
        out_ref[LOWER, part] = sum_ref[LOWER, part] + lower_ref[:, part].astype(f32)
        out_ref[UPPER, part] = sum_ref[UPPER, part] + upper_ref[:, part].astype(f32)


def pair_call(kernel, places, parts, lines, outs, others=()):
    blocks, height, protos = parts[0].shape

    def picked(n):
        return pl.BlockSpec((1, height, protos), lambda i, p: (p[n], 0, 0))

    def full(shape):
        return pl.BlockSpec(shape, lambda i, p: (0,) * len(shape))

    stay, arrived, turned = parts
    given = [keep_hbm(stay), arrived, keep_hbm(turned)] * len(places)
    many = len(outs) > 1
    shapes = [jax.ShapeDtypeStruct(shape, dtype) for shape, dtype in outs]
    specs = [full(shape) for shape, dtype in outs]
    return pl.pallas_call(
        kernel,
        grid_spec=pltpu.PrefetchScalarGridSpec(
            num_scalar_prefetch=1,
            grid=(1,),
            in_specs=[picked(n) for n in range(len(places)) for _ in range(3)]
            + [full(values.shape) for values in (*lines, *others)],
            out_specs=specs if many else specs[0],
        ),
        out_shape=shapes if many else shapes[0],
        compiler_params=pltpu.CompilerParams(vmem_limit_bytes=16 * 1024 * 1024),
        cost_estimate=pl.CostEstimate(
            flops=10**9, bytes_accessed=10 * height * protos, transcendentals=0
        ),
    )(jnp.stack(places), *given, *lines, *others)


def body(hidden_states, ln_in_gain, w_in, w_out, ln_out_gain, prototypes):
    view_count, image_rows, local_width = hidden_states.shape
    row_count = view_count * image_rows
    col_count = lax.axis_size(COLS)
    row_block = row_count // col_count

    y_count = lax.axis_size("y")
    z_count = lax.axis_size("z")
    tall = row_count // y_count

    sent = pack_states(
        hidden_states.transpose(0, 2, 1), ln_in_gain, ln_out_gain, z_count, y_count
    )
    received = lax.all_to_all(sent, COLS, 0, 0)
    gain_in = received[:, local_width, :local_width].reshape(D).astype(f32)
    gain_out = received[:, local_width + 1, :local_width].reshape(D).astype(f32)
    inputs_t = received[:, :local_width].reshape(D, tall)

    core = lax.axis_index("core")
    swap = [(0, 1), (1, 0)]
    w_in_t = w_in.T
    share = jnp.where(core == 0, w_in_t, w_out)
    shares = stack_shares(
        [
            lax.ppermute(share, "y", [(i, (i + step) % y_count) for i in range(y_count)])
            for step in range(1, y_count)
        ]
    )
    others = lax.ppermute(shares, "core", swap)

    inputs_f = inputs_t.astype(f32)
    center = jnp.mean(inputs_f, axis=0)
    spread = jnp.mean(inputs_f * inputs_f, axis=0) - center * center
    normed_t = (
        (inputs_f - center[None, :]) * lax.rsqrt(spread + norm_eps)[None, :] * gain_in[:, None]
    ).astype(bf16)
    block_part = feed_forward(core, normed_t.T, w_in_t, w_out, shares, others)
    block = scatter_sum(block_part.reshape(z_count, row_block, D), "z")
    picked = (
        jnp.arange(tall)[None, :]
        == lax.axis_index("z") * row_block + jnp.arange(row_block)[:, None]
    ).astype(bf16)
    own = lax.dot_general(picked, inputs_t, (((1,), (1,)), ((), ())), preferred_element_type=f32)
    resid = own + block
    center = jnp.mean(resid, axis=1, keepdims=True)
    spread = jnp.mean(resid * resid, axis=1, keepdims=True) - center * center
    final = (resid - center) * lax.rsqrt(spread + norm_eps) * gain_out[None, :]
    squared = jnp.sum(final * final, axis=1, keepdims=True)
    embed_part = (final * lax.rsqrt(squared + unit_eps)).astype(bf16)
    own_rows = gather_all(embed_part, "z").reshape(tall, D)

    x_index = lax.axis_index("x")
    x_count = lax.axis_size("x")
    unit, proto_len, turned = prepare(core, prototypes, x_count)
    proto_count = prototypes.shape[0]
    slice_width = turned.shape[1]

    row_parts = lax.axis_size(ROWS)
    y_index = lax.axis_index("y")
    steps = (1, 3, 2)
    rows_in = {
        step: lax.ppermute(own_rows, "y", [(i, (i + step) % y_count) for i in range(y_count)])
        for step in steps
    }
    places = jnp.stack([(y_index + y_count - step) % y_count for step in (0,) + steps])
    parts = [own_rows] + [rows_in[step] for step in steps]
    base, masses, soft_part, embed = score_pass(places, parts, unit, row_parts)
    embed_t = turn(core, embed)
    masses = lax.all_to_all(masses, ROWS, 0, 0)
    softs = images = lax.all_to_all(image_pass(masses, base, col_count, soft_part), COLS, 0, 0)
    for repeat in range(1, SINK_ITERS):
        masses = lax.all_to_all(proto_pass(images, base, row_parts), ROWS, 0, 0)
        images = lax.all_to_all(image_pass(masses, base, col_count), COLS, 0, 0)

    radial, away, stay, embed_terms = grad_pass(images, softs, masses, unit, embed, embed_t)
    arrived = lax.ppermute(away, "core", swap)
    parts = (stay, arrived, turned)
    lines = (radial, lax.ppermute(radial, "core", swap), proto_len)
    flat = (slice_width // 2, proto_count)

    def spot(step):
        return (x_index + step) % x_count

    def right(values):
        return lax.ppermute(values, "x", [(i, (i + 1) % x_count) for i in range(x_count)])

    def left(values):
        return lax.ppermute(values, "x", [((i + 1) % x_count, i) for i in range(x_count)])

    far_lower, far_upper = pair_call(far_kernel, (spot(2),), parts, lines, [(flat, bf16)] * 2)
    came_lower, came_upper = right(far_lower), left(far_upper)
    right_send, left_send, right_keep, left_keep = pair_call(
        near_kernel, (spot(1), spot(3)), parts, lines, [(flat, bf16)] * 2 + [(flat, f32)] * 2
    )
    near_upper, near_lower = right(right_send), left(left_send)
    own_sum = pair_call(
        own_kernel,
        (x_index,),
        parts,
        lines,
        [((slice_width, proto_count), f32)],
        (near_lower, near_upper),
    )
    right_relay, left_relay = call(
        relay_kernel,
        (),
        (right_keep, left_keep, came_lower, came_upper),
        [(flat, bf16)] * 2,
        8,
        10**8,
        10**6,
    )
    last_lower, last_upper = right(right_relay), left(left_relay)
    proto_grad = call(
        final_kernel,
        (),
        (own_sum, last_lower, last_upper),
        [((slice_width, proto_count), f32)],
        8,
        10**8,
        10**6,
    )
    embed_parts = lax.all_to_all(
        embed_terms.reshape(col_count, local_width, row_count), COLS, 0, 0
    )
    embed_parts, proto_grad = lax.optimization_barrier((embed_parts, proto_grad))
    embed_grad_t = jnp.sum(embed_parts.astype(f32), axis=0)
    embed_grad = embed_grad_t.T.reshape(view_count, image_rows, local_width)
    return (embed_grad, proto_grad)


def solution(mesh):
    sizes = {"x": mesh.shape["rows"] // 2, "core": 2, "z": mesh.shape["cols"] // 4, "y": 4}
    fine = Mesh(mesh.devices.reshape(tuple(sizes.values())), tuple(sizes))
    placed = (
        P(None, ROWS, COLS),
        P(COLS),
        P(None, COLS),
        P(COLS, None),
        P(COLS),
        P(COLS, None),
    )
    return jax.shard_map(
        body,
        mesh=fine,
        in_specs=placed,
        out_specs=(P(None, ROWS, COLS), P(ROWS, COLS)),
        check_vma=False,
    )
```

```python
import functools
import math

import jax
import jax.numpy as jnp
from jax import lax
from jax.experimental import pallas as pl
from jax.experimental.pallas import tpu as pltpu
from jax.sharding import Mesh, PartitionSpec as P

D = 1024
PROTOS = 65536
SINK_ITERS = 3


sink_temp = 0.05
soft_temp = 0.1
norm_eps = 1e-05
unit_eps = 1e-06

ROWS = ("x", "core")
COLS = ("z", "y")
f32 = jnp.float32
bf16 = jnp.bfloat16


def gather_all(values, axes):
    count = lax.axis_size(axes)
    copies = jnp.broadcast_to(values[None], (count,) + values.shape)
    return lax.all_to_all(copies, axes, 0, 0)


def sum_small(values, axes):
    return jnp.sum(gather_all(values, axes), axis=0)


def scatter_sum(blocks, axes):
    return jnp.sum(lax.all_to_all(blocks, axes, 0, 0).astype(f32), axis=0)


TILE = 512
LANES = 128
factor = 0.5 * math.sqrt(PROTOS * D)
NT = (((1,), (1,)), ((), ()))
VMEM = pl.BlockSpec(memory_space=pltpu.VMEM)
SMEM = pl.BlockSpec(memory_space=pltpu.SMEM)


def keep_hbm(values):
    return pltpu.with_memory_space_constraint(values, pltpu.HBM)


def call(kernel, scalars, arrays, outs, mib, flops, moved, in_hbm=()):
    shapes = [
        pltpu.HBM(shape, dtype) if place in in_hbm else jax.ShapeDtypeStruct(shape, dtype)
        for place, (shape, dtype) in enumerate(outs)
    ]
    many = len(shapes) > 1
    return pl.pallas_call(
        kernel,
        in_specs=[SMEM] * len(scalars) + [VMEM] * len(arrays),
        out_specs=[VMEM] * len(shapes) if many else VMEM,
        out_shape=shapes if many else shapes[0],
        compiler_params=pltpu.CompilerParams(vmem_limit_bytes=mib * 1024 * 1024),
        cost_estimate=pl.CostEstimate(flops=flops, bytes_accessed=moved, transcendentals=0),
    )(*scalars, *arrays)


def fold_lanes(values):
    width = values.shape[1]
    return sum(values[:, j : j + LANES] for j in range(0, width, LANES))


def as_column(row):
    return jnp.broadcast_to(row, (LANES, row.shape[1])).T


def as_row(column):
    return jnp.sum(column.T, axis=0, keepdims=True)


def spread_lanes(column, width):
    return jnp.concatenate([column] * (width // LANES), axis=1)


def view_rows(pair, count):
    half = count // 2
    width = pair.shape[1]
    return jnp.concatenate(
        [jnp.broadcast_to(pair[v : v + 1], (half, width)) for v in range(2)], axis=0
    )


def view_sums(values):
    half = values.shape[0] // 2
    return jnp.concatenate(
        [jnp.sum(values[v * half : (v + 1) * half], axis=0, keepdims=True) for v in range(2)],
        axis=0,
    )


def tiles(count):
    return [slice(j, j + TILE) for j in range(0, count, TILE)]


def pack_kernel(y_count, states_ref, in_ref, last_ref, out_ref):
    width = in_ref.shape[1]
    height = out_ref.shape[2]
    pair = jnp.concatenate([in_ref[...].astype(f32), last_ref[...].astype(f32)], axis=0)
    row = jnp.concatenate([pair, jnp.zeros((2, height - width), f32)], axis=1)
    foot = jnp.concatenate([row, jnp.zeros((6, height), f32)], axis=0)
    for way in range(y_count):
        view, start = divmod(way * height, states_ref.shape[2])
        block = states_ref[view, :, start : start + height].astype(f32)
        piece = jnp.concatenate([block, foot], axis=0).astype(bf16)
        for group in range(out_ref.shape[0] // y_count):
            out_ref[group * y_count + way] = piece


def pack_states(states, gain_in, gain_out, z_count, y_count):
    views, width, rows = states.shape
    height = views * rows // y_count
    shape = (z_count * y_count, width + 8, height)
    arrays = (states, gain_in.reshape(1, width), gain_out.reshape(1, width))

    def full(shape):
        return pl.BlockSpec(shape, lambda i: (0,) * len(shape))

    return pl.pallas_call(
        functools.partial(pack_kernel, y_count),
        grid=(1,),
        in_specs=[full(values.shape) for values in arrays],
        out_specs=full(shape),
        out_shape=jax.ShapeDtypeStruct(shape, bf16),
        compiler_params=pltpu.CompilerParams(vmem_limit_bytes=4 * 1024 * 1024),
    )(*[keep_hbm(values) for values in arrays])


def stack_kernel(first_ref, second_ref, third_ref, out_ref):
    for place, ref in enumerate((first_ref, second_ref, third_ref)):
        out_ref[place] = ref[...]


def stack_shares(parts):
    return call(
        stack_kernel, (), parts, [((3,) + parts[0].shape, bf16)], 2, 40 * 10**9, 4 * parts[0].size
    )


def ffn_kernel(core_ref, normed_ref, w_in_ref, w_out_ref, shares_ref, others_ref, out_ref):
    normed = normed_ref[...]
    even = core_ref[0] == 0
    total = jnp.zeros(out_ref.shape, f32)
    for step in range(shares_ref.shape[0] + 1):
        if step == 0:
            enter, leave = w_in_ref[...], w_out_ref[...]
        else:
            one, other = shares_ref[step - 1], others_ref[step - 1]
            enter, leave = jnp.where(even, one, other), jnp.where(even, other, one)
        wide = lax.dot_general(normed, enter, NT, preferred_element_type=f32)
        hidden = (0.5 * wide * (1.0 + lax.erf(wide * math.sqrt(0.5)))).astype(bf16)
        total = total + jnp.dot(hidden, leave, preferred_element_type=f32)
    out_ref[...] = total.astype(bf16)


def feed_forward(core, normed, w_in_t, w_out, shares, others):
    rows = normed.shape[0]
    return call(
        ffn_kernel,
        (core.reshape(1),),
        (normed, w_in_t, w_out, shares, others),
        [((rows, D), bf16)],
        8,
        4 * rows * D * 4 * w_out.shape[0],
        8 * w_out.size,
    )


def prepare_kernel(core_ref, proto_ref, unit_ref, length_ref, turned_ref):
    even = core_ref[0] == 0
    for part in tiles(proto_ref.shape[0]):
        values = proto_ref[part, :].astype(f32)
        squares = values * values
        inverse = lax.rsqrt(jnp.sum(squares, axis=1, keepdims=True) + unit_eps)
        unit_ref[part, :] = (values * inverse).astype(bf16)
        length_ref[:, part] = jnp.sqrt(as_row(fold_lanes(squares)) + unit_eps)
        for block in range(turned_ref.shape[0]):
            start = 2 * block * LANES
            low = values[:, start : start + LANES]
            high = values[:, start + LANES : start + 2 * LANES]
            turned_ref[block, :, part] = jnp.where(even, low, high).T.astype(bf16)


def prepare(core, prototypes, x_count):
    protos = prototypes.shape[0]
    return call(
        prepare_kernel,
        (core.reshape(1),),
        (prototypes,),
        [((protos, D), bf16), ((1, protos), f32), ((x_count, LANES, protos), bf16)],
        12,
        6 * protos * D,
        5 * protos * D,
        (2,),
    )


def scores_kernel(place_ref, *rest):
    *block_refs, unit_ref, base_ref, mass_ref, soft_ref, embed_ref = rest
    height = block_refs[0].shape[0]
    for n, ref in enumerate(block_refs):
        embed_ref[pl.ds(pl.multiple_of(place_ref[n] * height, height), height), :] = ref[...]
    total = jnp.zeros((base_ref.shape[0], LANES), f32)
    for part in tiles(unit_ref.shape[0]):
        scores = lax.dot_general(
            embed_ref[...], unit_ref[part, :], NT, preferred_element_type=f32
        )
        soft = jnp.exp(scores * (1.0 / soft_temp))
        base = soft * soft
        base_ref[:, part] = base.astype(bf16)
        mass = view_sums(base)
        mass_ref[:, :, part] = jnp.broadcast_to(mass[None], (mass_ref.shape[0],) + mass.shape)
        total = total + fold_lanes(soft)
    soft_ref[...] = as_row(total)


def score_pass(places, parts, unit, copies):
    height, protos = parts[0].shape[0], unit.shape[0]
    rows = height * len(parts)
    return call(
        scores_kernel,
        (places,),
        (*parts, unit),
        [
            ((rows, protos), bf16),
            ((copies, 2, protos), f32),
            ((1, rows), f32),
            ((rows, D), bf16),
        ],
        10,
        2 * rows * protos * D,
        8 * rows * protos,
    )


def turn_kernel(core_ref, embed_ref, turned_ref):
    even = core_ref[0] == 0
    for block in range(D // (2 * LANES)):
        start = 2 * block * LANES
        low = embed_ref[:, start : start + LANES].astype(f32)
        high = embed_ref[:, start + LANES : start + 2 * LANES].astype(f32)
        rows = slice(block * LANES, (block + 1) * LANES)
        turned_ref[0, rows, :] = jnp.where(even, high, low).T.astype(bf16)
        turned_ref[1, rows, :] = jnp.where(even, low, high).T.astype(bf16)


def turn(core, embed):
    rows = embed.shape[0]
    return call(
        turn_kernel, (core.reshape(1),), (embed,), [((2, D // 2, rows), bf16)], 6, 10**9, 4 * embed.size
    )


def image_kernel(mass_ref, base_ref, *rest):
    *extra, out_ref = rest
    rows, protos = base_ref.shape
    total = jnp.zeros((rows, LANES), f32)
    for part in tiles(protos):
        scale = 1.0 / jnp.sum(mass_ref[:, :, part], axis=0)
        total = total + fold_lanes(base_ref[:, part].astype(f32) * view_rows(scale, rows))
    row = jnp.concatenate([as_row(total)] + [ref[...] for ref in extra], axis=1)
    out_ref[...] = jnp.broadcast_to(row[None], out_ref.shape)


def image_pass(masses, base, copies, *extra):
    rows, protos = base.shape
    return call(
        image_kernel,
        (),
        (masses, base, *extra),
        [((copies, 1, (1 + len(extra)) * rows), f32)],
        8,
        3 * rows * protos,
        2 * rows * protos,
    )


def proto_kernel(image_ref, base_ref, mass_ref):
    column = as_column(1.0 / jnp.sum(image_ref[:, :, : base_ref.shape[0]], axis=0))
    for part in tiles(base_ref.shape[1]):
        mass = view_sums(base_ref[:, part].astype(f32) * spread_lanes(column, TILE))
        mass_ref[:, :, part] = jnp.broadcast_to(mass[None], (mass_ref.shape[0],) + mass.shape)


def proto_pass(images, base, copies):
    rows, protos = base.shape
    return call(
        proto_kernel,
        (),
        (images, base),
        [((copies, 2, protos), f32)],
        8,
        3 * rows * protos,
        2 * rows * protos,
    )


WIDE = 2 * TILE


def grad_kernel(
    image_ref, soft_ref, mass_ref, unit_hbm, embed_ref, embed_t_ref,
    radial_ref, away_hbm, stay_hbm, terms_ref,
    unit_ref, away_ref, stay_ref, load_sems, away_sems, stay_sems,
):
    rows, protos = embed_ref.shape[0], unit_ref.shape[0]
    loads = []
    for n, part in enumerate(tiles(protos)):
        load = pltpu.make_async_copy(unit_hbm.at[part], unit_ref.at[part], load_sems.at[n])
        load.start()
        loads.append(load)
    code_column = spread_lanes(
        as_column(factor / jnp.sum(image_ref[:, :, :rows], axis=0)), WIDE
    )
    prob_column = spread_lanes(
        as_column(factor / jnp.sum(soft_ref[:, :, rows:], axis=0)), WIDE
    )
    half = rows // 2
    stores = []
    total = None
    for n in range(protos // WIDE):
        part = slice(n * WIDE, (n + 1) * WIDE)
        for load in loads[n * (WIDE // TILE) : (n + 1) * (WIDE // TILE)]:
            load.wait()
        unit = unit_ref[part, :]
        scores = lax.dot_general(embed_ref[...], unit, NT, preferred_element_type=f32)
        soft = jnp.exp(scores * (1.0 / soft_temp))
        scale = 1.0 / jnp.sum(mass_ref[:, :, part], axis=0)
        codes = soft * soft * view_rows(scale, rows) * code_column
        swapped = jnp.concatenate([codes[half:], codes[:half]], axis=0)
        grad = (soft * prob_column - swapped).astype(bf16)
        radial_ref[:, part] = jnp.sum(grad.astype(f32) * scores, axis=0, keepdims=True)
        shape = away_ref.shape[:2] + (WIDE,)
        away = jnp.dot(embed_t_ref[0], grad, preferred_element_type=f32).astype(bf16)
        away_ref[:, :, part] = away.reshape(shape)
        stay = jnp.dot(embed_t_ref[1], grad, preferred_element_type=f32)
        stay_ref[:, :, part] = stay.reshape(shape)
        for ref, hbm, sems in (
            (away_ref, away_hbm, away_sems),
            (stay_ref, stay_hbm, stay_sems),
        ):
            store = pltpu.make_async_copy(ref.at[:, :, part], hbm.at[:, :, part], sems.at[n])
            store.start()
            stores.append(store)
        term = jnp.dot(grad, unit, preferred_element_type=f32)
        total = term if total is None else total + term
    for start in range(0, D, TILE):
        part = slice(start, start + TILE)
        terms_ref[part, :] = total[:, part].T.astype(bf16)
    for store in stores:
        store.wait()


def grad_pass(images, softs, masses, unit, embed, embed_t):
    rows, protos = embed.shape[0], unit.shape[0]
    depth = embed_t.shape[1]
    blocks = depth // LANES
    steps = protos // WIDE
    anywhere = pl.BlockSpec(memory_space=pl.ANY)
    return pl.pallas_call(
        grad_kernel,
        in_specs=[VMEM, VMEM, VMEM, anywhere, VMEM, VMEM],
        out_specs=[VMEM, anywhere, anywhere, VMEM],
        out_shape=[
            jax.ShapeDtypeStruct((1, protos), f32),
            pltpu.HBM((blocks, LANES, protos), bf16),
            pltpu.HBM((blocks, LANES, protos), f32),
            jax.ShapeDtypeStruct((D, rows), bf16),
        ],
        scratch_shapes=[
            pltpu.VMEM((protos, D), bf16),
            pltpu.VMEM((blocks, LANES, protos), bf16),
            pltpu.VMEM((blocks, LANES, protos), f32),
            pltpu.SemaphoreType.DMA((protos // TILE,)),
            pltpu.SemaphoreType.DMA((steps,)),
            pltpu.SemaphoreType.DMA((steps,)),
        ],
        compiler_params=pltpu.CompilerParams(vmem_limit_bytes=40 * 1024 * 1024),
        cost_estimate=pl.CostEstimate(
            flops=8 * depth * rows * protos,
            bytes_accessed=10 * depth * protos,
            transcendentals=rows * protos,
        ),
    )(images, softs, masses, keep_hbm(unit), embed, embed_t)


def pair_rows(refs, rows, part):
    stay_ref, arrived_ref, turned_ref, one_ref, two_ref, length_ref = refs
    inverse = 1.0 / length_ref[:, part]
    radial = (one_ref[:, part] + two_ref[:, part]) * inverse
    total = stay_ref[0, rows, part] + arrived_ref[0, rows, part].astype(f32)
    return (total - turned_ref[0, rows, part].astype(f32) * radial) * inverse


LOWER = slice(0, LANES // 2)
UPPER = slice(LANES // 2, LANES)
ALL = slice(0, LANES)


def far_kernel(place_ref, *refs):
    *given, lower_ref, upper_ref = refs
    for part in tiles(lower_ref.shape[1]):
        lower_ref[:, part] = pair_rows(given, LOWER, part).astype(bf16)
        upper_ref[:, part] = pair_rows(given, UPPER, part).astype(bf16)


def near_kernel(place_ref, *refs):
    right, left, lines = refs[:3], refs[3:6], refs[6:9]
    right_send, left_send, right_keep, left_keep = refs[9:]
    for part in tiles(right_send.shape[1]):
        right_send[:, part] = pair_rows((*right, *lines), UPPER, part).astype(bf16)
        left_send[:, part] = pair_rows((*left, *lines), LOWER, part).astype(bf16)
        right_keep[:, part] = pair_rows((*right, *lines), LOWER, part)
        left_keep[:, part] = pair_rows((*left, *lines), UPPER, part)


def own_kernel(place_ref, *refs):
    *given, lower_ref, upper_ref, out_ref = refs
    for part in tiles(out_ref.shape[1]):
        out_ref[LOWER, part] = pair_rows(given, LOWER, part) + lower_ref[:, part].astype(f32)
        out_ref[UPPER, part] = pair_rows(given, UPPER, part) + upper_ref[:, part].astype(f32)


def relay_kernel(right_keep, left_keep, lower_ref, upper_ref, right_send, left_send):
    for part in tiles(right_send.shape[1]):
        right_send[:, part] = (right_keep[:, part] + lower_ref[:, part].astype(f32)).astype(bf16)
        left_send[:, part] = (left_keep[:, part] + upper_ref[:, part].astype(f32)).astype(bf16)


def final_kernel(sum_ref, lower_ref, upper_ref, out_ref):
    for part in tiles(out_ref.shape[1]):
        out_ref[LOWER, part] = sum_ref[LOWER, part] + lower_ref[:, part].astype(f32)
        out_ref[UPPER, part] = sum_ref[UPPER, part] + upper_ref[:, part].astype(f32)


def pair_call(kernel, places, parts, lines, outs, others=()):
    blocks, height, protos = parts[0].shape

    def picked(n):
        return pl.BlockSpec((1, height, protos), lambda i, p: (p[n], 0, 0))

    def full(shape):
        return pl.BlockSpec(shape, lambda i, p: (0,) * len(shape))

    stay, arrived, turned = parts
    given = [keep_hbm(stay), arrived, keep_hbm(turned)] * len(places)
    many = len(outs) > 1
    shapes = [jax.ShapeDtypeStruct(shape, dtype) for shape, dtype in outs]
    specs = [full(shape) for shape, dtype in outs]
    return pl.pallas_call(
        kernel,
        grid_spec=pltpu.PrefetchScalarGridSpec(
            num_scalar_prefetch=1,
            grid=(1,),
            in_specs=[picked(n) for n in range(len(places)) for _ in range(3)]
            + [full(values.shape) for values in (*lines, *others)],
            out_specs=specs if many else specs[0],
        ),
        out_shape=shapes if many else shapes[0],
        compiler_params=pltpu.CompilerParams(vmem_limit_bytes=16 * 1024 * 1024),
        cost_estimate=pl.CostEstimate(
            flops=10**9, bytes_accessed=10 * height * protos, transcendentals=0
        ),
    )(jnp.stack(places), *given, *lines, *others)


def body(hidden_states, ln_in_gain, w_in, w_out, ln_out_gain, prototypes):
    view_count, image_rows, local_width = hidden_states.shape
    row_count = view_count * image_rows
    col_count = lax.axis_size(COLS)
    row_block = row_count // col_count

    y_count = lax.axis_size("y")
    z_count = lax.axis_size("z")
    tall = row_count // y_count

    sent = pack_states(
        hidden_states.transpose(0, 2, 1), ln_in_gain, ln_out_gain, z_count, y_count
    )
    received = lax.all_to_all(sent, COLS, 0, 0)
    gain_in = received[:, local_width, :local_width].reshape(D).astype(f32)
    gain_out = received[:, local_width + 1, :local_width].reshape(D).astype(f32)
    inputs_t = received[:, :local_width].reshape(D, tall)

    core = lax.axis_index("core")
    swap = [(0, 1), (1, 0)]
    w_in_t = w_in.T
    share = jnp.where(core == 0, w_in_t, w_out)
    shares = stack_shares(
        [
            lax.ppermute(share, "y", [(i, (i + step) % y_count) for i in range(y_count)])
            for step in range(1, y_count)
        ]
    )
    others = lax.ppermute(shares, "core", swap)

    inputs_f = inputs_t.astype(f32)
    center = jnp.mean(inputs_f, axis=0)
    spread = jnp.mean(inputs_f * inputs_f, axis=0) - center * center
    normed_t = (
        (inputs_f - center[None, :]) * lax.rsqrt(spread + norm_eps)[None, :] * gain_in[:, None]
    ).astype(bf16)
    block_part = feed_forward(core, normed_t.T, w_in_t, w_out, shares, others)
    block = scatter_sum(block_part.reshape(z_count, row_block, D), "z")
    picked = (
        jnp.arange(tall)[None, :]
        == lax.axis_index("z") * row_block + jnp.arange(row_block)[:, None]
    ).astype(bf16)
    own = lax.dot_general(picked, inputs_t, (((1,), (1,)), ((), ())), preferred_element_type=f32)
    resid = own + block
    center = jnp.mean(resid, axis=1, keepdims=True)
    spread = jnp.mean(resid * resid, axis=1, keepdims=True) - center * center
    final = (resid - center) * lax.rsqrt(spread + norm_eps) * gain_out[None, :]
    squared = jnp.sum(final * final, axis=1, keepdims=True)
    embed_part = (final * lax.rsqrt(squared + unit_eps)).astype(bf16)
    own_rows = gather_all(embed_part, "z").reshape(tall, D)

    x_index = lax.axis_index("x")
    x_count = lax.axis_size("x")
    unit, proto_len, turned = prepare(core, prototypes, x_count)
    proto_count = prototypes.shape[0]
    slice_width = turned.shape[1]

    row_parts = lax.axis_size(ROWS)
    y_index = lax.axis_index("y")
    steps = (1, 3, 2)
    rows_in = {
        step: lax.ppermute(own_rows, "y", [(i, (i + step) % y_count) for i in range(y_count)])
        for step in steps
    }
    places = jnp.stack([(y_index + y_count - step) % y_count for step in (0,) + steps])
    parts = [own_rows] + [rows_in[step] for step in steps]
    base, masses, soft_part, embed = score_pass(places, parts, unit, row_parts)
    embed_t = turn(core, embed)
    masses = lax.all_to_all(masses, ROWS, 0, 0)
    softs = images = lax.all_to_all(image_pass(masses, base, col_count, soft_part), COLS, 0, 0)
    for repeat in range(1, SINK_ITERS):
        masses = lax.all_to_all(proto_pass(images, base, row_parts), ROWS, 0, 0)
        images = lax.all_to_all(image_pass(masses, base, col_count), COLS, 0, 0)

    radial, away, stay, embed_terms = grad_pass(images, softs, masses, unit, embed, embed_t)
    arrived = lax.ppermute(away, "core", swap)
    parts = (stay, arrived, turned)
    lines = (radial, lax.ppermute(radial, "core", swap), proto_len)
    flat = (slice_width // 2, proto_count)

    def spot(step):
        return (x_index + step) % x_count

    def right(values):
        return lax.ppermute(values, "x", [(i, (i + 1) % x_count) for i in range(x_count)])

    def left(values):
        return lax.ppermute(values, "x", [((i + 1) % x_count, i) for i in range(x_count)])

    far_lower, far_upper = pair_call(far_kernel, (spot(2),), parts, lines, [(flat, bf16)] * 2)
    came_lower, came_upper = right(far_lower), left(far_upper)
    right_send, left_send, right_keep, left_keep = pair_call(
        near_kernel, (spot(1), spot(3)), parts, lines, [(flat, bf16)] * 2 + [(flat, f32)] * 2
    )
    near_upper, near_lower = right(right_send), left(left_send)
    own_sum = pair_call(
        own_kernel,
        (x_index,),
        parts,
        lines,
        [((slice_width, proto_count), f32)],
        (near_lower, near_upper),
    )
    right_relay, left_relay = call(
        relay_kernel,
        (),
        (right_keep, left_keep, came_lower, came_upper),
        [(flat, bf16)] * 2,
        8,
        10**8,
        10**6,
    )
    last_lower, last_upper = right(right_relay), left(left_relay)
    proto_grad = call(
        final_kernel,
        (),
        (own_sum, last_lower, last_upper),
        [((slice_width, proto_count), f32)],
        8,
        10**8,
        10**6,
    )
    embed_parts = lax.all_to_all(
        embed_terms.reshape(col_count, local_width, row_count), COLS, 0, 0
    )
    embed_parts, proto_grad = lax.optimization_barrier((embed_parts, proto_grad))
    embed_grad_t = jnp.sum(embed_parts.astype(f32), axis=0)
    embed_grad = embed_grad_t.T.reshape(view_count, image_rows, local_width)
    return (embed_grad, proto_grad)


def solution(mesh):
    sizes = {"x": mesh.shape["rows"] // 2, "core": 2, "z": mesh.shape["cols"] // 4, "y": 4}
    fine = Mesh(mesh.devices.reshape(tuple(sizes.values())), tuple(sizes))
    placed = (
        P(None, ROWS, COLS),
        P(COLS),
        P(None, COLS),
        P(COLS, None),
        P(COLS),
        P(COLS, None),
    )
    return jax.shard_map(
        body,
        mesh=fine,
        in_specs=placed,
        out_specs=(P(None, ROWS, COLS), P(ROWS, COLS)),
        check_vma=False,
    )
```

```python
import functools
import math

import jax
import jax.numpy as jnp
from jax import lax
from jax.experimental import pallas as pl
from jax.experimental.pallas import tpu as pltpu
from jax.sharding import Mesh, PartitionSpec as P

D = 1024
PROTOS = 65536
SINK_ITERS = 3


sink_temp = 0.05
soft_temp = 0.1
norm_eps = 1e-05
unit_eps = 1e-06

ROWS = ("x", "core")
COLS = ("z", "y")
f32 = jnp.float32
bf16 = jnp.bfloat16


def gather_all(values, axes):
    count = lax.axis_size(axes)
    copies = jnp.broadcast_to(values[None], (count,) + values.shape)
    return lax.all_to_all(copies, axes, 0, 0)


def sum_small(values, axes):
    return jnp.sum(gather_all(values, axes), axis=0)


def scatter_sum(blocks, axes):
    return jnp.sum(lax.all_to_all(blocks, axes, 0, 0).astype(f32), axis=0)


TILE = 512
LANES = 128
factor = 0.5 * math.sqrt(PROTOS * D)
NT = (((1,), (1,)), ((), ()))
VMEM = pl.BlockSpec(memory_space=pltpu.VMEM)
SMEM = pl.BlockSpec(memory_space=pltpu.SMEM)


def keep_hbm(values):
    return pltpu.with_memory_space_constraint(values, pltpu.HBM)


def call(kernel, scalars, arrays, outs, mib, flops, moved, in_hbm=()):
    shapes = [
        pltpu.HBM(shape, dtype) if place in in_hbm else jax.ShapeDtypeStruct(shape, dtype)
        for place, (shape, dtype) in enumerate(outs)
    ]
    many = len(shapes) > 1
    return pl.pallas_call(
        kernel,
        in_specs=[SMEM] * len(scalars) + [VMEM] * len(arrays),
        out_specs=[VMEM] * len(shapes) if many else VMEM,
        out_shape=shapes if many else shapes[0],
        compiler_params=pltpu.CompilerParams(vmem_limit_bytes=mib * 1024 * 1024),
        cost_estimate=pl.CostEstimate(flops=flops, bytes_accessed=moved, transcendentals=0),
    )(*scalars, *arrays)


def fold_lanes(values):
    width = values.shape[1]
    return sum(values[:, j : j + LANES] for j in range(0, width, LANES))


def as_column(row):
    return jnp.broadcast_to(row, (LANES, row.shape[1])).T


def as_row(column):
    return jnp.sum(column.T, axis=0, keepdims=True)


def spread_lanes(column, width):
    return jnp.concatenate([column] * (width // LANES), axis=1)


def view_rows(pair, count):
    half = count // 2
    width = pair.shape[1]
    return jnp.concatenate(
        [jnp.broadcast_to(pair[v : v + 1], (half, width)) for v in range(2)], axis=0
    )


def view_sums(values):
    half = values.shape[0] // 2
    return jnp.concatenate(
        [jnp.sum(values[v * half : (v + 1) * half], axis=0, keepdims=True) for v in range(2)],
        axis=0,
    )


def tiles(count):
    return [slice(j, j + TILE) for j in range(0, count, TILE)]


def pack_kernel(y_count, states_ref, in_ref, last_ref, out_ref):
    width = in_ref.shape[1]
    height = out_ref.shape[2]
    pair = jnp.concatenate([in_ref[...].astype(f32), last_ref[...].astype(f32)], axis=0)
    row = jnp.concatenate([pair, jnp.zeros((2, height - width), f32)], axis=1)
    foot = jnp.concatenate([row, jnp.zeros((6, height), f32)], axis=0)
    for way in range(y_count):
        view, start = divmod(way * height, states_ref.shape[2])
        block = states_ref[view, :, start : start + height].astype(f32)
        piece = jnp.concatenate([block, foot], axis=0).astype(bf16)
        for group in range(out_ref.shape[0] // y_count):
            out_ref[group * y_count + way] = piece


def pack_states(states, gain_in, gain_out, z_count, y_count):
    views, width, rows = states.shape
    height = views * rows // y_count
    shape = (z_count * y_count, width + 8, height)
    arrays = (states, gain_in.reshape(1, width), gain_out.reshape(1, width))

    def full(shape):
        return pl.BlockSpec(shape, lambda i: (0,) * len(shape))

    return pl.pallas_call(
        functools.partial(pack_kernel, y_count),
        grid=(1,),
        in_specs=[full(values.shape) for values in arrays],
        out_specs=full(shape),
        out_shape=jax.ShapeDtypeStruct(shape, bf16),
        compiler_params=pltpu.CompilerParams(vmem_limit_bytes=4 * 1024 * 1024),
    )(*[keep_hbm(values) for values in arrays])


def stack_kernel(first_ref, second_ref, third_ref, out_ref):
    for place, ref in enumerate((first_ref, second_ref, third_ref)):
        out_ref[place] = ref[...]


def stack_shares(parts):
    return call(
        stack_kernel, (), parts, [((3,) + parts[0].shape, bf16)], 2, 40 * 10**9, 4 * parts[0].size
    )


def ffn_kernel(core_ref, normed_ref, w_in_ref, w_out_ref, shares_ref, others_ref, out_ref):
    normed = normed_ref[...]
    even = core_ref[0] == 0
    total = jnp.zeros(out_ref.shape, f32)
    for step in range(shares_ref.shape[0] + 1):
        if step == 0:
            enter, leave = w_in_ref[...], w_out_ref[...]
        else:
            one, other = shares_ref[step - 1], others_ref[step - 1]
            enter, stacked = jnp.where(even, one, other), jnp.where(even, other, one)
            width = stacked.shape[1]
            leave = jnp.concatenate(
                [stacked[j : j + width] for j in range(0, stacked.shape[0], width)], axis=1
            )
        wide = jnp.dot(normed, enter, preferred_element_type=f32)
        hidden = (0.5 * wide * (1.0 + lax.erf(wide * math.sqrt(0.5)))).astype(bf16)
        total = total + jnp.dot(hidden, leave, preferred_element_type=f32)
    out_ref[...] = total.astype(bf16)


def feed_forward(core, normed, w_in, w_out, shares, others):
    rows = normed.shape[0]
    return call(
        ffn_kernel,
        (core.reshape(1),),
        (normed, w_in, w_out, shares, others),
        [((rows, D), bf16)],
        8,
        4 * rows * D * 4 * w_out.shape[0],
        8 * w_out.size,
    )


def prepare_kernel(core_ref, proto_ref, unit_ref, length_ref, turned_ref):
    even = core_ref[0] == 0
    for part in tiles(proto_ref.shape[0]):
        values = proto_ref[part, :].astype(f32)
        squares = values * values
        inverse = lax.rsqrt(jnp.sum(squares, axis=1, keepdims=True) + unit_eps)
        unit_ref[part, :] = (values * inverse).astype(bf16)
        length_ref[:, part] = jnp.sqrt(as_row(fold_lanes(squares)) + unit_eps)
        for block in range(turned_ref.shape[0]):
            start = 2 * block * LANES
            low = values[:, start : start + LANES]
            high = values[:, start + LANES : start + 2 * LANES]
            turned_ref[block, :, part] = jnp.where(even, low, high).T.astype(bf16)


def prepare(core, prototypes, x_count):
    protos = prototypes.shape[0]
    return call(
        prepare_kernel,
        (core.reshape(1),),
        (prototypes,),
        [((protos, D), bf16), ((1, protos), f32), ((x_count, LANES, protos), bf16)],
        12,
        6 * protos * D,
        5 * protos * D,
        (2,),
    )


def scores_kernel(place_ref, *rest):
    *block_refs, unit_ref, base_ref, mass_ref, soft_ref, embed_ref = rest
    height = block_refs[0].shape[0]
    for n, ref in enumerate(block_refs):
        embed_ref[pl.ds(pl.multiple_of(place_ref[n] * height, height), height), :] = ref[...]
    total = jnp.zeros((base_ref.shape[0], LANES), f32)
    for part in tiles(unit_ref.shape[0]):
        scores = lax.dot_general(
            embed_ref[...], unit_ref[part, :], NT, preferred_element_type=f32
        )
        soft = jnp.exp(scores * (1.0 / soft_temp))
        base = soft * soft
        base_ref[:, part] = base.astype(bf16)
        mass = view_sums(base)
        mass_ref[:, :, part] = jnp.broadcast_to(mass[None], (mass_ref.shape[0],) + mass.shape)
        total = total + fold_lanes(soft)
    soft_ref[...] = as_row(total)


def score_pass(places, parts, unit, copies):
    height, protos = parts[0].shape[0], unit.shape[0]
    rows = height * len(parts)
    return call(
        scores_kernel,
        (places,),
        (*parts, unit),
        [
            ((rows, protos), bf16),
            ((copies, 2, protos), f32),
            ((1, rows), f32),
            ((rows, D), bf16),
        ],
        10,
        2 * rows * protos * D,
        8 * rows * protos,
    )


def image_kernel(mass_ref, base_ref, *rest):
    *extra, out_ref = rest
    rows, protos = base_ref.shape
    total = jnp.zeros((rows, LANES), f32)
    for part in tiles(protos):
        scale = 1.0 / jnp.sum(mass_ref[:, :, part], axis=0)
        total = total + fold_lanes(base_ref[:, part].astype(f32) * view_rows(scale, rows))
    row = jnp.concatenate([as_row(total)] + [ref[...] for ref in extra], axis=1)
    out_ref[...] = jnp.broadcast_to(row[None], out_ref.shape)


def image_pass(masses, base, copies, *extra):
    rows, protos = base.shape
    return call(
        image_kernel,
        (),
        (masses, base, *extra),
        [((copies, 1, (1 + len(extra)) * rows), f32)],
        8,
        3 * rows * protos,
        2 * rows * protos,
    )


def proto_kernel(image_ref, base_ref, mass_ref):
    column = as_column(1.0 / jnp.sum(image_ref[:, :, : base_ref.shape[0]], axis=0))
    for part in tiles(base_ref.shape[1]):
        mass = view_sums(base_ref[:, part].astype(f32) * spread_lanes(column, TILE))
        mass_ref[:, :, part] = jnp.broadcast_to(mass[None], (mass_ref.shape[0],) + mass.shape)


def proto_pass(images, base, copies):
    rows, protos = base.shape
    return call(
        proto_kernel,
        (),
        (images, base),
        [((copies, 2, protos), f32)],
        8,
        3 * rows * protos,
        2 * rows * protos,
    )


WIDE = 2 * TILE


def grad_kernel(
    core_ref, image_ref, soft_ref, mass_ref, unit_hbm, embed_ref,
    radial_ref, away_hbm, stay_hbm, terms_ref,
    unit_ref, away_ref, stay_ref, embed_t_ref, load_sems, away_sems, stay_sems,
):
    rows, protos = embed_ref.shape[0], unit_ref.shape[0]
    loads = []
    for n, part in enumerate(tiles(protos)):
        load = pltpu.make_async_copy(unit_hbm.at[part], unit_ref.at[part], load_sems.at[n])
        load.start()
        loads.append(load)
    even = core_ref[0] == 0
    for block in range(D // (2 * LANES)):
        start = 2 * block * LANES
        low = embed_ref[:, start : start + LANES].astype(f32)
        high = embed_ref[:, start + LANES : start + 2 * LANES].astype(f32)
        place = slice(block * LANES, (block + 1) * LANES)
        embed_t_ref[0, place, :] = jnp.where(even, high, low).T.astype(bf16)
        embed_t_ref[1, place, :] = jnp.where(even, low, high).T.astype(bf16)
    code_column = spread_lanes(
        as_column(factor / jnp.sum(image_ref[:, :, :rows], axis=0)), WIDE
    )
    prob_column = spread_lanes(
        as_column(factor / jnp.sum(soft_ref[:, :, rows:], axis=0)), WIDE
    )
    half = rows // 2
    stores = []
    total = None
    for n in range(protos // WIDE):
        part = slice(n * WIDE, (n + 1) * WIDE)
        for load in loads[n * (WIDE // TILE) : (n + 1) * (WIDE // TILE)]:
            load.wait()
        unit = unit_ref[part, :]
        scores = lax.dot_general(embed_ref[...], unit, NT, preferred_element_type=f32)
        soft = jnp.exp(scores * (1.0 / soft_temp))
        scale = 1.0 / jnp.sum(mass_ref[:, :, part], axis=0)
        codes = soft * soft * view_rows(scale, rows) * code_column
        swapped = jnp.concatenate([codes[half:], codes[:half]], axis=0)
        grad = (soft * prob_column - swapped).astype(bf16)
        radial_ref[:, part] = jnp.sum(grad.astype(f32) * scores, axis=0, keepdims=True)
        shape = away_ref.shape[:2] + (WIDE,)
        away = jnp.dot(embed_t_ref[0], grad, preferred_element_type=f32).astype(bf16)
        away_ref[:, :, part] = away.reshape(shape)
        stay = jnp.dot(embed_t_ref[1], grad, preferred_element_type=f32)
        stay_ref[:, :, part] = stay.reshape(shape)
        for ref, hbm, sems in (
            (away_ref, away_hbm, away_sems),
            (stay_ref, stay_hbm, stay_sems),
        ):
            store = pltpu.make_async_copy(ref.at[:, :, part], hbm.at[:, :, part], sems.at[n])
            store.start()
            stores.append(store)
        term = jnp.dot(grad, unit, preferred_element_type=f32)
        total = term if total is None else total + term
    for start in range(0, D, TILE):
        part = slice(start, start + TILE)
        terms_ref[part, :] = total[:, part].T.astype(bf16)
    for store in stores:
        store.wait()


def grad_pass(core, images, softs, masses, unit, embed):
    rows, protos = embed.shape[0], unit.shape[0]
    depth = D // 2
    blocks = depth // LANES
    steps = protos // WIDE
    anywhere = pl.BlockSpec(memory_space=pl.ANY)
    return pl.pallas_call(
        grad_kernel,
        in_specs=[SMEM, VMEM, VMEM, VMEM, anywhere, VMEM],
        out_specs=[VMEM, anywhere, anywhere, VMEM],
        out_shape=[
            jax.ShapeDtypeStruct((1, protos), f32),
            pltpu.HBM((blocks, LANES, protos), bf16),
            pltpu.HBM((blocks, LANES, protos), f32),
            jax.ShapeDtypeStruct((D, rows), bf16),
        ],
        scratch_shapes=[
            pltpu.VMEM((protos, D), bf16),
            pltpu.VMEM((blocks, LANES, protos), bf16),
            pltpu.VMEM((blocks, LANES, protos), f32),
            pltpu.VMEM((2, depth, rows), bf16),
            pltpu.SemaphoreType.DMA((protos // TILE,)),
            pltpu.SemaphoreType.DMA((steps,)),
            pltpu.SemaphoreType.DMA((steps,)),
        ],
        compiler_params=pltpu.CompilerParams(vmem_limit_bytes=40 * 1024 * 1024),
        cost_estimate=pl.CostEstimate(
            flops=8 * depth * rows * protos,
            bytes_accessed=10 * depth * protos,
            transcendentals=rows * protos,
        ),
    )(core.reshape(1), images, softs, masses, keep_hbm(unit), embed)


def pair_rows(refs, rows, part):
    stay_ref, arrived_ref, turned_ref, one_ref, two_ref, length_ref = refs
    inverse = 1.0 / length_ref[:, part]
    radial = (one_ref[:, part] + two_ref[:, part]) * inverse
    total = stay_ref[0, rows, part] + arrived_ref[0, rows, part].astype(f32)
    return (total - turned_ref[0, rows, part].astype(f32) * radial) * inverse


LOWER = slice(0, LANES // 2)
UPPER = slice(LANES // 2, LANES)
ALL = slice(0, LANES)


def far_kernel(place_ref, *refs):
    *given, lower_ref, upper_ref = refs
    for part in tiles(lower_ref.shape[1]):
        lower_ref[:, part] = pair_rows(given, LOWER, part).astype(bf16)
        upper_ref[:, part] = pair_rows(given, UPPER, part).astype(bf16)


def near_kernel(place_ref, *refs):
    right, left, lines = refs[:3], refs[3:6], refs[6:9]
    right_send, left_send, right_keep, left_keep = refs[9:]
    for part in tiles(right_send.shape[1]):
        right_send[:, part] = pair_rows((*right, *lines), UPPER, part).astype(bf16)
        left_send[:, part] = pair_rows((*left, *lines), LOWER, part).astype(bf16)
        right_keep[:, part] = pair_rows((*right, *lines), LOWER, part)
        left_keep[:, part] = pair_rows((*left, *lines), UPPER, part)


def own_kernel(place_ref, *refs):
    *given, lower_ref, upper_ref, out_ref = refs
    for part in tiles(out_ref.shape[1]):
        out_ref[LOWER, part] = pair_rows(given, LOWER, part) + lower_ref[:, part].astype(f32)
        out_ref[UPPER, part] = pair_rows(given, UPPER, part) + upper_ref[:, part].astype(f32)


def relay_kernel(right_keep, left_keep, lower_ref, upper_ref, right_send, left_send):
    for part in tiles(right_send.shape[1]):
        right_send[:, part] = (right_keep[:, part] + lower_ref[:, part].astype(f32)).astype(bf16)
        left_send[:, part] = (left_keep[:, part] + upper_ref[:, part].astype(f32)).astype(bf16)


def final_kernel(sum_ref, lower_ref, upper_ref, out_ref):
    for part in tiles(out_ref.shape[1]):
        out_ref[LOWER, part] = sum_ref[LOWER, part] + lower_ref[:, part].astype(f32)
        out_ref[UPPER, part] = sum_ref[UPPER, part] + upper_ref[:, part].astype(f32)


def pair_call(kernel, places, parts, lines, outs, others=()):
    blocks, height, protos = parts[0].shape

    def picked(n):
        return pl.BlockSpec((1, height, protos), lambda i, p: (p[n], 0, 0))

    def full(shape):
        return pl.BlockSpec(shape, lambda i, p: (0,) * len(shape))

    stay, arrived, turned = parts
    given = [keep_hbm(stay), arrived, keep_hbm(turned)] * len(places)
    many = len(outs) > 1
    shapes = [jax.ShapeDtypeStruct(shape, dtype) for shape, dtype in outs]
    specs = [full(shape) for shape, dtype in outs]
    return pl.pallas_call(
        kernel,
        grid_spec=pltpu.PrefetchScalarGridSpec(
            num_scalar_prefetch=1,
            grid=(1,),
            in_specs=[picked(n) for n in range(len(places)) for _ in range(3)]
            + [full(values.shape) for values in (*lines, *others)],
            out_specs=specs if many else specs[0],
        ),
        out_shape=shapes if many else shapes[0],
        compiler_params=pltpu.CompilerParams(vmem_limit_bytes=16 * 1024 * 1024),
        cost_estimate=pl.CostEstimate(
            flops=10**9, bytes_accessed=10 * height * protos, transcendentals=0
        ),
    )(jnp.stack(places), *given, *lines, *others)


def body(hidden_states, ln_in_gain, w_in, w_out, ln_out_gain, prototypes):
    view_count, image_rows, local_width = hidden_states.shape
    row_count = view_count * image_rows
    col_count = lax.axis_size(COLS)
    row_block = row_count // col_count

    y_count = lax.axis_size("y")
    z_count = lax.axis_size("z")
    tall = row_count // y_count

    sent = pack_states(
        hidden_states.transpose(0, 2, 1), ln_in_gain, ln_out_gain, z_count, y_count
    )
    received = lax.all_to_all(sent, COLS, 0, 0)
    gain_in = received[:, local_width, :local_width].reshape(D).astype(f32)
    gain_out = received[:, local_width + 1, :local_width].reshape(D).astype(f32)
    inputs_t = received[:, :local_width].reshape(D, tall)

    core = lax.axis_index("core")
    swap = [(0, 1), (1, 0)]
    width = w_in.shape[1]
    stacked = w_out.reshape(width, D // width, width).transpose(1, 0, 2).reshape(D, width)
    share = jnp.where(core == 0, w_in, stacked)
    shares = stack_shares(
        [
            lax.ppermute(share, "y", [(i, (i + step) % y_count) for i in range(y_count)])
            for step in range(1, y_count)
        ]
    )
    others = lax.ppermute(shares, "core", swap)

    inputs_f = inputs_t.astype(f32)
    center = jnp.mean(inputs_f, axis=0)
    spread = jnp.mean(inputs_f * inputs_f, axis=0) - center * center
    normed_t = (
        (inputs_f - center[None, :]) * lax.rsqrt(spread + norm_eps)[None, :] * gain_in[:, None]
    ).astype(bf16)
    block_part = feed_forward(core, normed_t.T, w_in, w_out, shares, others)
    block = scatter_sum(block_part.reshape(z_count, row_block, D), "z")
    picked = (
        jnp.arange(tall)[None, :]
        == lax.axis_index("z") * row_block + jnp.arange(row_block)[:, None]
    ).astype(bf16)
    own = lax.dot_general(picked, inputs_t, (((1,), (1,)), ((), ())), preferred_element_type=f32)
    resid = own + block
    center = jnp.mean(resid, axis=1, keepdims=True)
    spread = jnp.mean(resid * resid, axis=1, keepdims=True) - center * center
    final = (resid - center) * lax.rsqrt(spread + norm_eps) * gain_out[None, :]
    squared = jnp.sum(final * final, axis=1, keepdims=True)
    embed_part = (final * lax.rsqrt(squared + unit_eps)).astype(bf16)
    own_rows = gather_all(embed_part, "z").reshape(tall, D)

    x_index = lax.axis_index("x")
    x_count = lax.axis_size("x")
    unit, proto_len, turned = prepare(core, prototypes, x_count)
    proto_count = prototypes.shape[0]
    slice_width = turned.shape[1]

    row_parts = lax.axis_size(ROWS)
    y_index = lax.axis_index("y")
    steps = (1, 3, 2)
    rows_in = {
        step: lax.ppermute(own_rows, "y", [(i, (i + step) % y_count) for i in range(y_count)])
        for step in steps
    }
    places = jnp.stack([(y_index + y_count - step) % y_count for step in (0,) + steps])
    parts = [own_rows] + [rows_in[step] for step in steps]
    base, masses, soft_part, embed = score_pass(places, parts, unit, row_parts)
    masses = lax.all_to_all(masses, ROWS, 0, 0)
    softs = images = lax.all_to_all(image_pass(masses, base, col_count, soft_part), COLS, 0, 0)
    for repeat in range(1, SINK_ITERS):
        masses = lax.all_to_all(proto_pass(images, base, row_parts), ROWS, 0, 0)
        images = lax.all_to_all(image_pass(masses, base, col_count), COLS, 0, 0)

    radial, away, stay, embed_terms = grad_pass(core, images, softs, masses, unit, embed)
    arrived = lax.ppermute(away, "core", swap)
    parts = (stay, arrived, turned)
    lines = (radial, lax.ppermute(radial, "core", swap), proto_len)
    flat = (slice_width // 2, proto_count)

    def spot(step):
        return (x_index + step) % x_count

    def right(values):
        return lax.ppermute(values, "x", [(i, (i + 1) % x_count) for i in range(x_count)])

    def left(values):
        return lax.ppermute(values, "x", [((i + 1) % x_count, i) for i in range(x_count)])

    far_lower, far_upper = pair_call(far_kernel, (spot(2),), parts, lines, [(flat, bf16)] * 2)
    came_lower, came_upper = right(far_lower), left(far_upper)
    right_send, left_send, right_keep, left_keep = pair_call(
        near_kernel, (spot(1), spot(3)), parts, lines, [(flat, bf16)] * 2 + [(flat, f32)] * 2
    )
    near_upper, near_lower = right(right_send), left(left_send)
    own_sum = pair_call(
        own_kernel,
        (x_index,),
        parts,
        lines,
        [((slice_width, proto_count), f32)],
        (near_lower, near_upper),
    )
    right_relay, left_relay = call(
        relay_kernel,
        (),
        (right_keep, left_keep, came_lower, came_upper),
        [(flat, bf16)] * 2,
        8,
        10**8,
        10**6,
    )
    last_lower, last_upper = right(right_relay), left(left_relay)
    proto_grad = call(
        final_kernel,
        (),
        (own_sum, last_lower, last_upper),
        [((slice_width, proto_count), f32)],
        8,
        10**8,
        10**6,
    )
    embed_parts = lax.all_to_all(
        embed_terms.reshape(col_count, local_width, row_count), COLS, 0, 0
    )
    embed_parts, proto_grad = lax.optimization_barrier((embed_parts, proto_grad))
    embed_grad_t = jnp.sum(embed_parts.astype(f32), axis=0)
    embed_grad = embed_grad_t.T.reshape(view_count, image_rows, local_width)
    return (embed_grad, proto_grad)


def solution(mesh):
    sizes = {"x": mesh.shape["rows"] // 2, "core": 2, "z": mesh.shape["cols"] // 4, "y": 4}
    fine = Mesh(mesh.devices.reshape(tuple(sizes.values())), tuple(sizes))
    placed = (
        P(None, ROWS, COLS),
        P(COLS),
        P(None, COLS),
        P(COLS, None),
        P(COLS),
        P(COLS, None),
    )
    return jax.shard_map(
        body,
        mesh=fine,
        in_specs=placed,
        out_specs=(P(None, ROWS, COLS), P(ROWS, COLS)),
        check_vma=False,
    )
```

```python
import functools
import math

import jax
import jax.numpy as jnp
from jax import lax
from jax.experimental import pallas as pl
from jax.experimental.pallas import tpu as pltpu
from jax.sharding import Mesh, PartitionSpec as P

D = 1024
PROTOS = 65536
SINK_ITERS = 3


sink_temp = 0.05
soft_temp = 0.1
norm_eps = 1e-05
unit_eps = 1e-06

ROWS = ("x", "core")
COLS = ("z", "y")
f32 = jnp.float32
bf16 = jnp.bfloat16


def gather_all(values, axes):
    count = lax.axis_size(axes)
    copies = jnp.broadcast_to(values[None], (count,) + values.shape)
    return lax.all_to_all(copies, axes, 0, 0)


def sum_small(values, axes):
    return jnp.sum(gather_all(values, axes), axis=0)


def scatter_sum(blocks, axes):
    return jnp.sum(lax.all_to_all(blocks, axes, 0, 0).astype(f32), axis=0)


TILE = 512
LANES = 128
factor = 0.5 * math.sqrt(PROTOS * D)
NT = (((1,), (1,)), ((), ()))
VMEM = pl.BlockSpec(memory_space=pltpu.VMEM)
SMEM = pl.BlockSpec(memory_space=pltpu.SMEM)


def keep_hbm(values):
    return pltpu.with_memory_space_constraint(values, pltpu.HBM)


def call(kernel, scalars, arrays, outs, mib, flops, moved, in_hbm=()):
    shapes = [
        pltpu.HBM(shape, dtype) if place in in_hbm else jax.ShapeDtypeStruct(shape, dtype)
        for place, (shape, dtype) in enumerate(outs)
    ]
    many = len(shapes) > 1
    return pl.pallas_call(
        kernel,
        in_specs=[SMEM] * len(scalars) + [VMEM] * len(arrays),
        out_specs=[VMEM] * len(shapes) if many else VMEM,
        out_shape=shapes if many else shapes[0],
        compiler_params=pltpu.CompilerParams(vmem_limit_bytes=mib * 1024 * 1024),
        cost_estimate=pl.CostEstimate(flops=flops, bytes_accessed=moved, transcendentals=0),
    )(*scalars, *arrays)


def fold_lanes(values):
    width = values.shape[1]
    return sum(values[:, j : j + LANES] for j in range(0, width, LANES))


def as_column(row):
    return jnp.broadcast_to(row, (LANES, row.shape[1])).T


def as_row(column):
    return jnp.sum(column.T, axis=0, keepdims=True)


def spread_lanes(column, width):
    return jnp.concatenate([column] * (width // LANES), axis=1)


def view_rows(pair, count):
    half = count // 2
    width = pair.shape[1]
    return jnp.concatenate(
        [jnp.broadcast_to(pair[v : v + 1], (half, width)) for v in range(2)], axis=0
    )


def view_sums(values):
    half = values.shape[0] // 2
    return jnp.concatenate(
        [jnp.sum(values[v * half : (v + 1) * half], axis=0, keepdims=True) for v in range(2)],
        axis=0,
    )


def tiles(count):
    return [slice(j, j + TILE) for j in range(0, count, TILE)]


def pack_kernel(
    y_count, core_ref, states_ref, in_ref, last_ref, w_in_ref, w_out_ref, out_ref, share_ref
):
    width = in_ref.shape[1]
    height = out_ref.shape[2]
    pair = jnp.concatenate([in_ref[...].astype(f32), last_ref[...].astype(f32)], axis=0)
    row = jnp.concatenate([pair, jnp.zeros((2, height - width), f32)], axis=1)
    foot = jnp.concatenate([row, jnp.zeros((6, height), f32)], axis=0)
    for way in range(y_count):
        view, start = divmod(way * height, states_ref.shape[2])
        block = states_ref[view, :, start : start + height].astype(f32)
        piece = jnp.concatenate([block, foot], axis=0).astype(bf16)
        for group in range(out_ref.shape[0] // y_count):
            out_ref[group * y_count + way] = piece
    even = core_ref[0] == 0
    units = w_in_ref.shape[1]
    for start in range(0, D, units):
        part = slice(start, start + units)
        share_ref[part, :] = jnp.where(even, w_in_ref[part, :], w_out_ref[:, part])


def pack(core, states, gain_in, gain_out, w_in, w_out, z_count, y_count):
    views, width, rows = states.shape
    height = views * rows // y_count
    shape = (z_count * y_count, width + 8, height)
    arrays = (states, gain_in.reshape(1, width), gain_out.reshape(1, width), w_in, w_out)

    def full(shape):
        return pl.BlockSpec(shape, lambda i: (0,) * len(shape))

    return pl.pallas_call(
        functools.partial(pack_kernel, y_count),
        grid=(1,),
        in_specs=[SMEM] + [full(values.shape) for values in arrays],
        out_specs=[full(shape), full(w_in.shape)],
        out_shape=[
            jax.ShapeDtypeStruct(shape, bf16),
            jax.ShapeDtypeStruct(w_in.shape, bf16),
        ],
        compiler_params=pltpu.CompilerParams(vmem_limit_bytes=6 * 1024 * 1024),
    )(core.reshape(1), *[keep_hbm(values) for values in arrays])


def stack_kernel(first_ref, second_ref, third_ref, out_ref):
    for place, ref in enumerate((first_ref, second_ref, third_ref)):
        out_ref[place] = ref[...]


def stack_shares(parts):
    return call(
        stack_kernel, (), parts, [((3,) + parts[0].shape, bf16)], 2, 40 * 10**9, 4 * parts[0].size
    )


def ffn_kernel(core_ref, normed_ref, w_in_ref, w_out_ref, shares_ref, others_ref, out_ref):
    normed = normed_ref[...]
    even = core_ref[0] == 0
    total = jnp.zeros(out_ref.shape, f32)
    for step in range(shares_ref.shape[0] + 1):
        if step == 0:
            enter, leave = w_in_ref[...], w_out_ref[...]
        else:
            one, other = shares_ref[step - 1], others_ref[step - 1]
            enter, stacked = jnp.where(even, one, other), jnp.where(even, other, one)
            width = stacked.shape[1]
            leave = jnp.concatenate(
                [stacked[j : j + width] for j in range(0, stacked.shape[0], width)], axis=1
            )
        wide = jnp.dot(normed, enter, preferred_element_type=f32)
        hidden = (0.5 * wide * (1.0 + lax.erf(wide * math.sqrt(0.5)))).astype(bf16)
        total = total + jnp.dot(hidden, leave, preferred_element_type=f32)
    out_ref[...] = total.astype(bf16)


def feed_forward(core, normed, w_in, w_out, shares, others):
    rows = normed.shape[0]
    return call(
        ffn_kernel,
        (core.reshape(1),),
        (normed, w_in, w_out, shares, others),
        [((rows, D), bf16)],
        8,
        4 * rows * D * 4 * w_out.shape[0],
        8 * w_out.size,
    )


def prepare_kernel(core_ref, proto_ref, unit_ref, length_ref, turned_ref):
    even = core_ref[0] == 0
    for part in tiles(proto_ref.shape[0]):
        values = proto_ref[part, :].astype(f32)
        squares = values * values
        inverse = lax.rsqrt(jnp.sum(squares, axis=1, keepdims=True) + unit_eps)
        unit_ref[part, :] = (values * inverse).astype(bf16)
        length_ref[:, part] = jnp.sqrt(as_row(fold_lanes(squares)) + unit_eps)
        for block in range(turned_ref.shape[0]):
            start = 2 * block * LANES
            low = values[:, start : start + LANES]
            high = values[:, start + LANES : start + 2 * LANES]
            turned_ref[block, :, part] = jnp.where(even, low, high).T.astype(bf16)


def prepare(core, prototypes, x_count):
    protos = prototypes.shape[0]
    return call(
        prepare_kernel,
        (core.reshape(1),),
        (prototypes,),
        [((protos, D), bf16), ((1, protos), f32), ((x_count, LANES, protos), bf16)],
        12,
        6 * protos * D,
        5 * protos * D,
        (2,),
    )


def scores_kernel(place_ref, *rest):
    *block_refs, unit_ref, base_ref, mass_ref, soft_ref, embed_ref = rest
    height = block_refs[0].shape[0]
    for n, ref in enumerate(block_refs):
        embed_ref[pl.ds(pl.multiple_of(place_ref[n] * height, height), height), :] = ref[...]
    total = jnp.zeros((base_ref.shape[0], LANES), f32)
    for part in tiles(unit_ref.shape[0]):
        scores = lax.dot_general(
            embed_ref[...], unit_ref[part, :], NT, preferred_element_type=f32
        )
        soft = jnp.exp(scores * (1.0 / soft_temp))
        base = soft * soft
        base_ref[:, part] = base.astype(bf16)
        mass = view_sums(base)
        mass_ref[:, :, part] = jnp.broadcast_to(mass[None], (mass_ref.shape[0],) + mass.shape)
        total = total + fold_lanes(soft)
    soft_ref[...] = as_row(total)


def score_pass(places, parts, unit, copies):
    height, protos = parts[0].shape[0], unit.shape[0]
    rows = height * len(parts)
    return call(
        scores_kernel,
        (places,),
        (*parts, unit),
        [
            ((rows, protos), bf16),
            ((copies, 2, protos), f32),
            ((1, rows), f32),
            ((rows, D), bf16),
        ],
        10,
        2 * rows * protos * D,
        8 * rows * protos,
    )


def image_kernel(mass_ref, base_ref, *rest):
    *extra, out_ref = rest
    rows, protos = base_ref.shape
    total = jnp.zeros((rows, LANES), f32)
    for part in tiles(protos):
        scale = 1.0 / jnp.sum(mass_ref[:, :, part], axis=0)
        total = total + fold_lanes(base_ref[:, part].astype(f32) * view_rows(scale, rows))
    row = jnp.concatenate([as_row(total)] + [ref[...] for ref in extra], axis=1)
    out_ref[...] = jnp.broadcast_to(row[None], out_ref.shape)


def image_pass(masses, base, copies, *extra):
    rows, protos = base.shape
    return call(
        image_kernel,
        (),
        (masses, base, *extra),
        [((copies, 1, (1 + len(extra)) * rows), f32)],
        8,
        3 * rows * protos,
        2 * rows * protos,
    )


def proto_kernel(image_ref, base_ref, mass_ref):
    column = as_column(1.0 / jnp.sum(image_ref[:, :, : base_ref.shape[0]], axis=0))
    for part in tiles(base_ref.shape[1]):
        mass = view_sums(base_ref[:, part].astype(f32) * spread_lanes(column, TILE))
        mass_ref[:, :, part] = jnp.broadcast_to(mass[None], (mass_ref.shape[0],) + mass.shape)


def proto_pass(images, base, copies):
    rows, protos = base.shape
    return call(
        proto_kernel,
        (),
        (images, base),
        [((copies, 2, protos), f32)],
        8,
        3 * rows * protos,
        2 * rows * protos,
    )


WIDE = 2 * TILE


def grad_kernel(
    core_ref, image_ref, soft_ref, mass_ref, unit_hbm, embed_ref,
    radial_ref, away_hbm, stay_hbm, terms_ref,
    unit_ref, away_ref, stay_ref, embed_t_ref, load_sems, away_sems, stay_sems,
):
    rows, protos = embed_ref.shape[0], unit_ref.shape[0]
    loads = []
    for n, part in enumerate(tiles(protos)):
        load = pltpu.make_async_copy(unit_hbm.at[part], unit_ref.at[part], load_sems.at[n])
        load.start()
        loads.append(load)
    even = core_ref[0] == 0
    for block in range(D // (2 * LANES)):
        start = 2 * block * LANES
        low = embed_ref[:, start : start + LANES].astype(f32)
        high = embed_ref[:, start + LANES : start + 2 * LANES].astype(f32)
        place = slice(block * LANES, (block + 1) * LANES)
        embed_t_ref[0, place, :] = jnp.where(even, high, low).T.astype(bf16)
        embed_t_ref[1, place, :] = jnp.where(even, low, high).T.astype(bf16)
    code_column = spread_lanes(
        as_column(factor / jnp.sum(image_ref[:, :, :rows], axis=0)), WIDE
    )
    prob_column = spread_lanes(
        as_column(factor / jnp.sum(soft_ref[:, :, rows:], axis=0)), WIDE
    )
    half = rows // 2
    stores = []
    total = None
    for n in range(protos // WIDE):
        part = slice(n * WIDE, (n + 1) * WIDE)
        for load in loads[n * (WIDE // TILE) : (n + 1) * (WIDE // TILE)]:
            load.wait()
        unit = unit_ref[part, :]
        scores = lax.dot_general(embed_ref[...], unit, NT, preferred_element_type=f32)
        soft = jnp.exp(scores * (1.0 / soft_temp))
        scale = 1.0 / jnp.sum(mass_ref[:, :, part], axis=0)
        codes = soft * soft * view_rows(scale, rows) * code_column
        swapped = jnp.concatenate([codes[half:], codes[:half]], axis=0)
        grad = (soft * prob_column - swapped).astype(bf16)
        radial_ref[:, part] = jnp.sum(grad.astype(f32) * scores, axis=0, keepdims=True)
        shape = away_ref.shape[:2] + (WIDE,)
        away = jnp.dot(embed_t_ref[0], grad, preferred_element_type=f32).astype(bf16)
        away_ref[:, :, part] = away.reshape(shape)
        stay = jnp.dot(embed_t_ref[1], grad, preferred_element_type=f32)
        stay_ref[:, :, part] = stay.reshape(shape)
        for ref, hbm, sems in (
            (away_ref, away_hbm, away_sems),
            (stay_ref, stay_hbm, stay_sems),
        ):
            store = pltpu.make_async_copy(ref.at[:, :, part], hbm.at[:, :, part], sems.at[n])
            store.start()
            stores.append(store)
        term = jnp.dot(grad, unit, preferred_element_type=f32)
        total = term if total is None else total + term
    for start in range(0, D, TILE):
        part = slice(start, start + TILE)
        terms_ref[part, :] = total[:, part].T.astype(bf16)
    for store in stores:
        store.wait()


def grad_pass(core, images, softs, masses, unit, embed):
    rows, protos = embed.shape[0], unit.shape[0]
    depth = D // 2
    blocks = depth // LANES
    steps = protos // WIDE
    anywhere = pl.BlockSpec(memory_space=pl.ANY)
    return pl.pallas_call(
        grad_kernel,
        in_specs=[SMEM, VMEM, VMEM, VMEM, anywhere, VMEM],
        out_specs=[VMEM, anywhere, anywhere, VMEM],
        out_shape=[
            jax.ShapeDtypeStruct((1, protos), f32),
            pltpu.HBM((blocks, LANES, protos), bf16),
            pltpu.HBM((blocks, LANES, protos), f32),
            jax.ShapeDtypeStruct((D, rows), bf16),
        ],
        scratch_shapes=[
            pltpu.VMEM((protos, D), bf16),
            pltpu.VMEM((blocks, LANES, protos), bf16),
            pltpu.VMEM((blocks, LANES, protos), f32),
            pltpu.VMEM((2, depth, rows), bf16),
            pltpu.SemaphoreType.DMA((protos // TILE,)),
            pltpu.SemaphoreType.DMA((steps,)),
            pltpu.SemaphoreType.DMA((steps,)),
        ],
        compiler_params=pltpu.CompilerParams(vmem_limit_bytes=40 * 1024 * 1024),
        cost_estimate=pl.CostEstimate(
            flops=8 * depth * rows * protos,
            bytes_accessed=10 * depth * protos,
            transcendentals=rows * protos,
        ),
    )(core.reshape(1), images, softs, masses, keep_hbm(unit), embed)


def pair_rows(refs, rows, part):
    stay_ref, arrived_ref, turned_ref, one_ref, two_ref, length_ref = refs
    inverse = 1.0 / length_ref[:, part]
    radial = (one_ref[:, part] + two_ref[:, part]) * inverse
    total = stay_ref[0, rows, part] + arrived_ref[0, rows, part].astype(f32)
    return (total - turned_ref[0, rows, part].astype(f32) * radial) * inverse


LOWER = slice(0, LANES // 2)
UPPER = slice(LANES // 2, LANES)
ALL = slice(0, LANES)


def far_kernel(place_ref, *refs):
    *given, lower_ref, upper_ref = refs
    for part in tiles(lower_ref.shape[1]):
        lower_ref[:, part] = pair_rows(given, LOWER, part).astype(bf16)
        upper_ref[:, part] = pair_rows(given, UPPER, part).astype(bf16)


def near_kernel(place_ref, *refs):
    right, left, lines = refs[:3], refs[3:6], refs[6:9]
    right_send, left_send, right_keep, left_keep = refs[9:]
    for part in tiles(right_send.shape[1]):
        right_send[:, part] = pair_rows((*right, *lines), UPPER, part).astype(bf16)
        left_send[:, part] = pair_rows((*left, *lines), LOWER, part).astype(bf16)
        right_keep[:, part] = pair_rows((*right, *lines), LOWER, part)
        left_keep[:, part] = pair_rows((*left, *lines), UPPER, part)


def own_kernel(place_ref, *refs):
    *given, lower_ref, upper_ref, out_ref = refs
    for part in tiles(out_ref.shape[1]):
        out_ref[LOWER, part] = pair_rows(given, LOWER, part) + lower_ref[:, part].astype(f32)
        out_ref[UPPER, part] = pair_rows(given, UPPER, part) + upper_ref[:, part].astype(f32)


def relay_kernel(right_keep, left_keep, lower_ref, upper_ref, right_send, left_send):
    for part in tiles(right_send.shape[1]):
        right_send[:, part] = (right_keep[:, part] + lower_ref[:, part].astype(f32)).astype(bf16)
        left_send[:, part] = (left_keep[:, part] + upper_ref[:, part].astype(f32)).astype(bf16)


def final_kernel(sum_ref, lower_ref, upper_ref, out_ref):
    for part in tiles(out_ref.shape[1]):
        out_ref[LOWER, part] = sum_ref[LOWER, part] + lower_ref[:, part].astype(f32)
        out_ref[UPPER, part] = sum_ref[UPPER, part] + upper_ref[:, part].astype(f32)


def pair_call(kernel, places, parts, lines, outs, others=()):
    blocks, height, protos = parts[0].shape

    def picked(n):
        return pl.BlockSpec((1, height, protos), lambda i, p: (p[n], 0, 0))

    def full(shape):
        return pl.BlockSpec(shape, lambda i, p: (0,) * len(shape))

    stay, arrived, turned = parts
    given = [keep_hbm(stay), arrived, keep_hbm(turned)] * len(places)
    many = len(outs) > 1
    shapes = [jax.ShapeDtypeStruct(shape, dtype) for shape, dtype in outs]
    specs = [full(shape) for shape, dtype in outs]
    return pl.pallas_call(
        kernel,
        grid_spec=pltpu.PrefetchScalarGridSpec(
            num_scalar_prefetch=1,
            grid=(1,),
            in_specs=[picked(n) for n in range(len(places)) for _ in range(3)]
            + [full(values.shape) for values in (*lines, *others)],
            out_specs=specs if many else specs[0],
        ),
        out_shape=shapes if many else shapes[0],
        compiler_params=pltpu.CompilerParams(vmem_limit_bytes=16 * 1024 * 1024),
        cost_estimate=pl.CostEstimate(
            flops=10**9, bytes_accessed=10 * height * protos, transcendentals=0
        ),
    )(jnp.stack(places), *given, *lines, *others)


def body(hidden_states, ln_in_gain, w_in, w_out, ln_out_gain, prototypes):
    view_count, image_rows, local_width = hidden_states.shape
    row_count = view_count * image_rows
    col_count = lax.axis_size(COLS)
    row_block = row_count // col_count

    y_count = lax.axis_size("y")
    z_count = lax.axis_size("z")
    tall = row_count // y_count

    core = lax.axis_index("core")
    swap = [(0, 1), (1, 0)]
    sent, share = pack(
        core, hidden_states.transpose(0, 2, 1), ln_in_gain, ln_out_gain, w_in, w_out, z_count, y_count
    )
    received = lax.all_to_all(sent, COLS, 0, 0)
    gain_in = received[:, local_width, :local_width].reshape(D).astype(f32)
    gain_out = received[:, local_width + 1, :local_width].reshape(D).astype(f32)
    inputs_t = received[:, :local_width].reshape(D, tall)

    shares = stack_shares(
        [
            lax.ppermute(share, "y", [(i, (i + step) % y_count) for i in range(y_count)])
            for step in range(1, y_count)
        ]
    )
    others = lax.ppermute(shares, "core", swap)

    inputs_f = inputs_t.astype(f32)
    center = jnp.mean(inputs_f, axis=0)
    spread = jnp.mean(inputs_f * inputs_f, axis=0) - center * center
    normed_t = (
        (inputs_f - center[None, :]) * lax.rsqrt(spread + norm_eps)[None, :] * gain_in[:, None]
    ).astype(bf16)
    block_part = feed_forward(core, normed_t.T, w_in, w_out, shares, others)
    block = scatter_sum(block_part.reshape(z_count, row_block, D), "z")
    picked = (
        jnp.arange(tall)[None, :]
        == lax.axis_index("z") * row_block + jnp.arange(row_block)[:, None]
    ).astype(bf16)
    own = lax.dot_general(picked, inputs_t, (((1,), (1,)), ((), ())), preferred_element_type=f32)
    resid = own + block
    center = jnp.mean(resid, axis=1, keepdims=True)
    spread = jnp.mean(resid * resid, axis=1, keepdims=True) - center * center
    final = (resid - center) * lax.rsqrt(spread + norm_eps) * gain_out[None, :]
    squared = jnp.sum(final * final, axis=1, keepdims=True)
    embed_part = (final * lax.rsqrt(squared + unit_eps)).astype(bf16)
    own_rows = gather_all(embed_part, "z").reshape(tall, D)

    x_index = lax.axis_index("x")
    x_count = lax.axis_size("x")
    unit, proto_len, turned = prepare(core, prototypes, x_count)
    proto_count = prototypes.shape[0]
    slice_width = turned.shape[1]

    row_parts = lax.axis_size(ROWS)
    y_index = lax.axis_index("y")
    steps = (1, 3, 2)
    rows_in = {
        step: lax.ppermute(own_rows, "y", [(i, (i + step) % y_count) for i in range(y_count)])
        for step in steps
    }
    places = jnp.stack([(y_index + y_count - step) % y_count for step in (0,) + steps])
    parts = [own_rows] + [rows_in[step] for step in steps]
    base, masses, soft_part, embed = score_pass(places, parts, unit, row_parts)
    masses = lax.all_to_all(masses, ROWS, 0, 0)
    softs = images = lax.all_to_all(image_pass(masses, base, col_count, soft_part), COLS, 0, 0)
    for repeat in range(1, SINK_ITERS):
        masses = lax.all_to_all(proto_pass(images, base, row_parts), ROWS, 0, 0)
        images = lax.all_to_all(image_pass(masses, base, col_count), COLS, 0, 0)

    radial, away, stay, embed_terms = grad_pass(core, images, softs, masses, unit, embed)
    arrived = lax.ppermute(away, "core", swap)
    parts = (stay, arrived, turned)
    lines = (radial, lax.ppermute(radial, "core", swap), proto_len)
    flat = (slice_width // 2, proto_count)

    def spot(step):
        return (x_index + step) % x_count

    def right(values):
        return lax.ppermute(values, "x", [(i, (i + 1) % x_count) for i in range(x_count)])

    def left(values):
        return lax.ppermute(values, "x", [((i + 1) % x_count, i) for i in range(x_count)])

    far_lower, far_upper = pair_call(far_kernel, (spot(2),), parts, lines, [(flat, bf16)] * 2)
    came_lower, came_upper = right(far_lower), left(far_upper)
    right_send, left_send, right_keep, left_keep = pair_call(
        near_kernel, (spot(1), spot(3)), parts, lines, [(flat, bf16)] * 2 + [(flat, f32)] * 2
    )
    near_upper, near_lower = right(right_send), left(left_send)
    own_sum = pair_call(
        own_kernel,
        (x_index,),
        parts,
        lines,
        [((slice_width, proto_count), f32)],
        (near_lower, near_upper),
    )
    right_relay, left_relay = call(
        relay_kernel,
        (),
        (right_keep, left_keep, came_lower, came_upper),
        [(flat, bf16)] * 2,
        8,
        10**8,
        10**6,
    )
    last_lower, last_upper = right(right_relay), left(left_relay)
    proto_grad = call(
        final_kernel,
        (),
        (own_sum, last_lower, last_upper),
        [((slice_width, proto_count), f32)],
        8,
        10**8,
        10**6,
    )
    embed_parts = lax.all_to_all(
        embed_terms.reshape(col_count, local_width, row_count), COLS, 0, 0
    )
    embed_parts, proto_grad = lax.optimization_barrier((embed_parts, proto_grad))
    embed_grad_t = jnp.sum(embed_parts.astype(f32), axis=0)
    embed_grad = embed_grad_t.T.reshape(view_count, image_rows, local_width)
    return (embed_grad, proto_grad)


def solution(mesh):
    sizes = {"x": mesh.shape["rows"] // 2, "core": 2, "z": mesh.shape["cols"] // 4, "y": 4}
    fine = Mesh(mesh.devices.reshape(tuple(sizes.values())), tuple(sizes))
    placed = (
        P(None, ROWS, COLS),
        P(COLS),
        P(None, COLS),
        P(COLS, None),
        P(COLS),
        P(COLS, None),
    )
    return jax.shard_map(
        body,
        mesh=fine,
        in_specs=placed,
        out_specs=(P(None, ROWS, COLS), P(ROWS, COLS)),
        check_vma=False,
    )
```

```python
import functools
import math

import jax
import jax.numpy as jnp
from jax import lax
from jax.experimental import pallas as pl
from jax.experimental.pallas import tpu as pltpu
from jax.sharding import Mesh, PartitionSpec as P

D = 1024
PROTOS = 65536
SINK_ITERS = 3


sink_temp = 0.05
soft_temp = 0.1
norm_eps = 1e-05
unit_eps = 1e-06

ROWS = ("x", "core")
COLS = ("z", "y")
f32 = jnp.float32
bf16 = jnp.bfloat16


def gather_all(values, axes):
    count = lax.axis_size(axes)
    copies = jnp.broadcast_to(values[None], (count,) + values.shape)
    return lax.all_to_all(copies, axes, 0, 0)


def sum_small(values, axes):
    return jnp.sum(gather_all(values, axes), axis=0)


def scatter_sum(blocks, axes):
    return jnp.sum(lax.all_to_all(blocks, axes, 0, 0).astype(f32), axis=0)


TILE = 512
LANES = 128
factor = 0.5 * math.sqrt(PROTOS * D)
NT = (((1,), (1,)), ((), ()))
VMEM = pl.BlockSpec(memory_space=pltpu.VMEM)
SMEM = pl.BlockSpec(memory_space=pltpu.SMEM)


def keep_hbm(values):
    return pltpu.with_memory_space_constraint(values, pltpu.HBM)


def call(kernel, scalars, arrays, outs, mib, flops, moved, in_hbm=()):
    shapes = [
        pltpu.HBM(shape, dtype) if place in in_hbm else jax.ShapeDtypeStruct(shape, dtype)
        for place, (shape, dtype) in enumerate(outs)
    ]
    many = len(shapes) > 1
    return pl.pallas_call(
        kernel,
        in_specs=[SMEM] * len(scalars) + [VMEM] * len(arrays),
        out_specs=[VMEM] * len(shapes) if many else VMEM,
        out_shape=shapes if many else shapes[0],
        compiler_params=pltpu.CompilerParams(vmem_limit_bytes=mib * 1024 * 1024),
        cost_estimate=pl.CostEstimate(flops=flops, bytes_accessed=moved, transcendentals=0),
    )(*scalars, *arrays)


def fold_lanes(values):
    width = values.shape[1]
    return sum(values[:, j : j + LANES] for j in range(0, width, LANES))


def as_column(row):
    return jnp.broadcast_to(row, (LANES, row.shape[1])).T


def as_row(column):
    return jnp.sum(column.T, axis=0, keepdims=True)


def spread_lanes(column, width):
    return jnp.concatenate([column] * (width // LANES), axis=1)


def view_rows(pair, count):
    half = count // 2
    width = pair.shape[1]
    return jnp.concatenate(
        [jnp.broadcast_to(pair[v : v + 1], (half, width)) for v in range(2)], axis=0
    )


def view_sums(values):
    half = values.shape[0] // 2
    return jnp.concatenate(
        [jnp.sum(values[v * half : (v + 1) * half], axis=0, keepdims=True) for v in range(2)],
        axis=0,
    )


def tiles(count):
    return [slice(j, j + TILE) for j in range(0, count, TILE)]


def pack_kernel(
    y_count, core_ref, states_ref, in_ref, last_ref, w_in_ref, w_out_ref, out_ref, share_ref
):
    width = in_ref.shape[1]
    height = out_ref.shape[2]
    pair = jnp.concatenate([in_ref[...].astype(f32), last_ref[...].astype(f32)], axis=0)
    row = jnp.concatenate([pair, jnp.zeros((2, height - width), f32)], axis=1)
    foot = jnp.concatenate([row, jnp.zeros((6, height), f32)], axis=0)
    for way in range(y_count):
        view, start = divmod(way * height, states_ref.shape[2])
        block = states_ref[view, :, start : start + height].astype(f32)
        piece = jnp.concatenate([block, foot], axis=0).astype(bf16)
        for group in range(out_ref.shape[0] // y_count):
            out_ref[group * y_count + way] = piece
    even = core_ref[0] == 0
    units = w_in_ref.shape[1]
    for start in range(0, D, units):
        part = slice(start, start + units)
        share_ref[part, :] = jnp.where(even, w_in_ref[part, :], w_out_ref[:, part])


def pack(core, states, gain_in, gain_out, w_in, w_out, z_count, y_count):
    views, width, rows = states.shape
    height = views * rows // y_count
    shape = (z_count * y_count, width + 8, height)
    arrays = (states, gain_in.reshape(1, width), gain_out.reshape(1, width), w_in, w_out)

    def full(shape):
        return pl.BlockSpec(shape, lambda i: (0,) * len(shape))

    return pl.pallas_call(
        functools.partial(pack_kernel, y_count),
        grid=(1,),
        in_specs=[SMEM] + [full(values.shape) for values in arrays],
        out_specs=[full(shape), full(w_in.shape)],
        out_shape=[
            jax.ShapeDtypeStruct(shape, bf16),
            jax.ShapeDtypeStruct(w_in.shape, bf16),
        ],
        compiler_params=pltpu.CompilerParams(vmem_limit_bytes=6 * 1024 * 1024),
    )(core.reshape(1), *[keep_hbm(values) for values in arrays])


def stack_kernel(first_ref, second_ref, third_ref, out_ref):
    for place, ref in enumerate((first_ref, second_ref, third_ref)):
        out_ref[place] = ref[...]


def stack_shares(parts):
    return call(
        stack_kernel, (), parts, [((3,) + parts[0].shape, bf16)], 2, 40 * 10**9, 4 * parts[0].size
    )


def ffn_kernel(core_ref, normed_ref, w_in_ref, w_out_ref, shares_ref, others_ref, out_ref):
    normed = normed_ref[...]
    even = core_ref[0] == 0
    total = jnp.zeros(out_ref.shape, f32)
    for step in range(shares_ref.shape[0] + 1):
        if step == 0:
            enter, leave = w_in_ref[...], w_out_ref[...]
        else:
            one, other = shares_ref[step - 1], others_ref[step - 1]
            enter, stacked = jnp.where(even, one, other), jnp.where(even, other, one)
            width = stacked.shape[1]
            leave = jnp.concatenate(
                [stacked[j : j + width] for j in range(0, stacked.shape[0], width)], axis=1
            )
        wide = jnp.dot(normed, enter, preferred_element_type=f32)
        hidden = (0.5 * wide * (1.0 + lax.erf(wide * math.sqrt(0.5)))).astype(bf16)
        total = total + jnp.dot(hidden, leave, preferred_element_type=f32)
    out_ref[...] = total.astype(bf16)


def feed_forward(core, normed, w_in, w_out, shares, others):
    rows = normed.shape[0]
    return call(
        ffn_kernel,
        (core.reshape(1),),
        (normed, w_in, w_out, shares, others),
        [((rows, D), bf16)],
        8,
        4 * rows * D * 4 * w_out.shape[0],
        8 * w_out.size,
    )


def prepare_kernel(core_ref, proto_ref, unit_ref, length_ref, turned_ref):
    even = core_ref[0] == 0
    for part in tiles(proto_ref.shape[0]):
        values = proto_ref[part, :].astype(f32)
        squares = values * values
        inverse = lax.rsqrt(jnp.sum(squares, axis=1, keepdims=True) + unit_eps)
        unit_ref[part, :] = (values * inverse).astype(bf16)
        length_ref[:, part] = jnp.sqrt(as_row(fold_lanes(squares)) + unit_eps)
        for block in range(turned_ref.shape[0]):
            start = 2 * block * LANES
            low = values[:, start : start + LANES]
            high = values[:, start + LANES : start + 2 * LANES]
            turned_ref[block, :, part] = jnp.where(even, low, high).T.astype(bf16)


def prepare(core, prototypes, x_count):
    protos = prototypes.shape[0]
    return call(
        prepare_kernel,
        (core.reshape(1),),
        (prototypes,),
        [((protos, D), bf16), ((1, protos), f32), ((x_count, LANES, protos), bf16)],
        12,
        6 * protos * D,
        5 * protos * D,
        (2,),
    )


def scores_kernel(place_ref, *rest):
    *block_refs, unit_ref, base_ref, mass_ref, soft_ref, embed_ref = rest
    height = block_refs[0].shape[0]
    for n, ref in enumerate(block_refs):
        embed_ref[pl.ds(pl.multiple_of(place_ref[n] * height, height), height), :] = ref[...]
    total = jnp.zeros((base_ref.shape[0], LANES), f32)
    for part in tiles(unit_ref.shape[0]):
        scores = lax.dot_general(
            embed_ref[...], unit_ref[part, :], NT, preferred_element_type=f32
        )
        soft = jnp.exp(scores * (1.0 / soft_temp))
        base = soft * soft
        base_ref[:, part] = base.astype(bf16)
        mass = view_sums(base)
        mass_ref[:, :, part] = jnp.broadcast_to(mass[None], (mass_ref.shape[0],) + mass.shape)
        total = total + fold_lanes(soft)
    soft_ref[...] = as_row(total)


def score_pass(places, parts, unit, copies):
    height, protos = parts[0].shape[0], unit.shape[0]
    rows = height * len(parts)
    return call(
        scores_kernel,
        (places,),
        (*parts, unit),
        [
            ((rows, protos), bf16),
            ((copies, 2, protos), f32),
            ((1, rows), f32),
            ((rows, D), bf16),
        ],
        10,
        2 * rows * protos * D,
        8 * rows * protos,
    )


def image_kernel(mass_ref, base_ref, *rest):
    *extra, out_ref = rest
    rows, protos = base_ref.shape
    total = jnp.zeros((rows, LANES), f32)
    for part in tiles(protos):
        scale = 1.0 / jnp.sum(mass_ref[:, :, part], axis=0)
        total = total + fold_lanes(base_ref[:, part].astype(f32) * view_rows(scale, rows))
    row = jnp.concatenate([as_row(total)] + [ref[...] for ref in extra], axis=1)
    out_ref[...] = jnp.broadcast_to(row[None], out_ref.shape)


def image_pass(masses, base, copies, *extra):
    rows, protos = base.shape
    return call(
        image_kernel,
        (),
        (masses, base, *extra),
        [((copies, 1, (1 + len(extra)) * rows), f32)],
        8,
        3 * rows * protos,
        2 * rows * protos,
    )


def proto_kernel(image_ref, base_ref, mass_ref):
    column = as_column(1.0 / jnp.sum(image_ref[:, :, : base_ref.shape[0]], axis=0))
    for part in tiles(base_ref.shape[1]):
        mass = view_sums(base_ref[:, part].astype(f32) * spread_lanes(column, TILE))
        mass_ref[:, :, part] = jnp.broadcast_to(mass[None], (mass_ref.shape[0],) + mass.shape)


def proto_pass(images, base, copies):
    rows, protos = base.shape
    return call(
        proto_kernel,
        (),
        (images, base),
        [((copies, 2, protos), f32)],
        8,
        3 * rows * protos,
        2 * rows * protos,
    )


WIDE = 2 * TILE


def grad_kernel(
    core_ref, image_ref, soft_ref, mass_ref, unit_hbm, embed_ref,
    radial_ref, away_hbm, grad_hbm, embed_t_ref, terms_ref,
    unit_ref, away_ref, grad_ref, load_sems, away_sems, grad_sems,
):
    rows, protos = embed_ref.shape[0], unit_ref.shape[0]
    loads = []
    for n, part in enumerate(tiles(protos)):
        load = pltpu.make_async_copy(unit_hbm.at[part], unit_ref.at[part], load_sems.at[n])
        load.start()
        loads.append(load)
    even = core_ref[0] == 0
    for block in range(D // (2 * LANES)):
        start = 2 * block * LANES
        low = embed_ref[:, start : start + LANES].astype(f32)
        high = embed_ref[:, start + LANES : start + 2 * LANES].astype(f32)
        place = slice(block * LANES, (block + 1) * LANES)
        embed_t_ref[0, place, :] = jnp.where(even, high, low).T.astype(bf16)
        embed_t_ref[1, place, :] = jnp.where(even, low, high).T.astype(bf16)
    code_column = spread_lanes(
        as_column(factor / jnp.sum(image_ref[:, :, :rows], axis=0)), WIDE
    )
    prob_column = spread_lanes(
        as_column(factor / jnp.sum(soft_ref[:, :, rows:], axis=0)), WIDE
    )
    half = rows // 2
    stores = []
    total = None
    for n in range(protos // WIDE):
        part = slice(n * WIDE, (n + 1) * WIDE)
        for load in loads[n * (WIDE // TILE) : (n + 1) * (WIDE // TILE)]:
            load.wait()
        unit = unit_ref[part, :]
        scores = lax.dot_general(embed_ref[...], unit, NT, preferred_element_type=f32)
        soft = jnp.exp(scores * (1.0 / soft_temp))
        scale = 1.0 / jnp.sum(mass_ref[:, :, part], axis=0)
        codes = soft * soft * view_rows(scale, rows) * code_column
        swapped = jnp.concatenate([codes[half:], codes[:half]], axis=0)
        grad = (soft * prob_column - swapped).astype(bf16)
        radial_ref[:, part] = jnp.sum(grad.astype(f32) * scores, axis=0, keepdims=True)
        shape = away_ref.shape[:2] + (WIDE,)
        away = jnp.dot(embed_t_ref[0], grad, preferred_element_type=f32).astype(bf16)
        away_ref[:, :, part] = away.reshape(shape)
        grad_ref[:, part] = grad
        for store in (
            pltpu.make_async_copy(
                away_ref.at[:, :, part], away_hbm.at[:, :, part], away_sems.at[n]
            ),
            pltpu.make_async_copy(grad_ref.at[:, part], grad_hbm.at[:, part], grad_sems.at[n]),
        ):
            store.start()
            stores.append(store)
        term = jnp.dot(grad, unit, preferred_element_type=f32)
        total = term if total is None else total + term
    for start in range(0, D, TILE):
        part = slice(start, start + TILE)
        terms_ref[part, :] = total[:, part].T.astype(bf16)
    for store in stores:
        store.wait()


def grad_pass(core, images, softs, masses, unit, embed):
    rows, protos = embed.shape[0], unit.shape[0]
    depth = D // 2
    blocks = depth // LANES
    steps = protos // WIDE
    anywhere = pl.BlockSpec(memory_space=pl.ANY)
    return pl.pallas_call(
        grad_kernel,
        in_specs=[SMEM, VMEM, VMEM, VMEM, anywhere, VMEM],
        out_specs=[VMEM, anywhere, anywhere, VMEM, VMEM],
        out_shape=[
            jax.ShapeDtypeStruct((1, protos), f32),
            pltpu.HBM((blocks, LANES, protos), bf16),
            pltpu.HBM((rows, protos), bf16),
            jax.ShapeDtypeStruct((2, depth, rows), bf16),
            pltpu.HBM((D, rows), bf16),
        ],
        scratch_shapes=[
            pltpu.VMEM((protos, D), bf16),
            pltpu.VMEM((blocks, LANES, protos), bf16),
            pltpu.VMEM((rows, protos), bf16),
            pltpu.SemaphoreType.DMA((protos // TILE,)),
            pltpu.SemaphoreType.DMA((steps,)),
            pltpu.SemaphoreType.DMA((steps,)),
        ],
        compiler_params=pltpu.CompilerParams(vmem_limit_bytes=40 * 1024 * 1024),
        cost_estimate=pl.CostEstimate(
            flops=8 * depth * rows * protos,
            bytes_accessed=10 * depth * protos,
            transcendentals=rows * protos,
        ),
    )(core.reshape(1), images, softs, masses, keep_hbm(unit), embed)


def stay_kernel(embed_t_ref, grad_ref, out_ref):
    stay = jnp.dot(embed_t_ref[0], grad_ref[...], preferred_element_type=f32)
    out_ref[...] = stay.reshape(out_ref.shape)


def stay_pass(embed_t, grad):
    _, depth, rows = embed_t.shape
    protos = grad.shape[1]
    blocks = depth // LANES
    return pl.pallas_call(
        stay_kernel,
        grid=(protos // TILE,),
        in_specs=[
            pl.BlockSpec((1, depth, rows), lambda i: (1, 0, 0)),
            pl.BlockSpec((rows, TILE), lambda i: (0, i)),
        ],
        out_specs=pl.BlockSpec((blocks, LANES, TILE), lambda i: (0, 0, i)),
        out_shape=pltpu.HBM((blocks, LANES, protos), f32),
        compiler_params=pltpu.CompilerParams(
            dimension_semantics=("arbitrary",), vmem_limit_bytes=10 * 1024 * 1024
        ),
        cost_estimate=pl.CostEstimate(
            flops=2 * depth * rows * protos, bytes_accessed=6 * rows * protos, transcendentals=0
        ),
    )(embed_t, keep_hbm(grad))


def pair_rows(refs, rows, part):
    stay_ref, arrived_ref, turned_ref, one_ref, two_ref, length_ref = refs
    inverse = 1.0 / length_ref[:, part]
    radial = (one_ref[:, part] + two_ref[:, part]) * inverse
    total = stay_ref[0, rows, part] + arrived_ref[0, rows, part].astype(f32)
    return (total - turned_ref[0, rows, part].astype(f32) * radial) * inverse


LOWER = slice(0, LANES // 2)
UPPER = slice(LANES // 2, LANES)
ALL = slice(0, LANES)


def far_kernel(place_ref, *refs):
    *given, lower_ref, upper_ref = refs
    for part in tiles(lower_ref.shape[1]):
        lower_ref[:, part] = pair_rows(given, LOWER, part).astype(bf16)
        upper_ref[:, part] = pair_rows(given, UPPER, part).astype(bf16)


def near_kernel(place_ref, *refs):
    right, left, lines = refs[:3], refs[3:6], refs[6:9]
    right_send, left_send, right_keep, left_keep = refs[9:]
    for part in tiles(right_send.shape[1]):
        right_send[:, part] = pair_rows((*right, *lines), UPPER, part).astype(bf16)
        left_send[:, part] = pair_rows((*left, *lines), LOWER, part).astype(bf16)
        right_keep[:, part] = pair_rows((*right, *lines), LOWER, part)
        left_keep[:, part] = pair_rows((*left, *lines), UPPER, part)


def own_kernel(place_ref, *refs):
    *given, lower_ref, upper_ref, out_ref = refs
    for part in tiles(out_ref.shape[1]):
        out_ref[LOWER, part] = pair_rows(given, LOWER, part) + lower_ref[:, part].astype(f32)
        out_ref[UPPER, part] = pair_rows(given, UPPER, part) + upper_ref[:, part].astype(f32)


def relay_kernel(right_keep, left_keep, lower_ref, upper_ref, right_send, left_send):
    for part in tiles(right_send.shape[1]):
        right_send[:, part] = (right_keep[:, part] + lower_ref[:, part].astype(f32)).astype(bf16)
        left_send[:, part] = (left_keep[:, part] + upper_ref[:, part].astype(f32)).astype(bf16)


def final_kernel(sum_ref, lower_ref, upper_ref, out_ref):
    for part in tiles(out_ref.shape[1]):
        out_ref[LOWER, part] = sum_ref[LOWER, part] + lower_ref[:, part].astype(f32)
        out_ref[UPPER, part] = sum_ref[UPPER, part] + upper_ref[:, part].astype(f32)


def pair_call(kernel, places, parts, lines, outs, others=()):
    blocks, height, protos = parts[0].shape

    def picked(n):
        return pl.BlockSpec((1, height, protos), lambda i, p: (p[n], 0, 0))

    def full(shape):
        return pl.BlockSpec(shape, lambda i, p: (0,) * len(shape))

    stay, arrived, turned = parts
    given = [keep_hbm(stay), arrived, keep_hbm(turned)] * len(places)
    many = len(outs) > 1
    shapes = [jax.ShapeDtypeStruct(shape, dtype) for shape, dtype in outs]
    specs = [full(shape) for shape, dtype in outs]
    return pl.pallas_call(
        kernel,
        grid_spec=pltpu.PrefetchScalarGridSpec(
            num_scalar_prefetch=1,
            grid=(1,),
            in_specs=[picked(n) for n in range(len(places)) for _ in range(3)]
            + [full(values.shape) for values in (*lines, *others)],
            out_specs=specs if many else specs[0],
        ),
        out_shape=shapes if many else shapes[0],
        compiler_params=pltpu.CompilerParams(vmem_limit_bytes=16 * 1024 * 1024),
        cost_estimate=pl.CostEstimate(
            flops=10**9, bytes_accessed=10 * height * protos, transcendentals=0
        ),
    )(jnp.stack(places), *given, *lines, *others)


def body(hidden_states, ln_in_gain, w_in, w_out, ln_out_gain, prototypes):
    view_count, image_rows, local_width = hidden_states.shape
    row_count = view_count * image_rows
    col_count = lax.axis_size(COLS)
    row_block = row_count // col_count

    y_count = lax.axis_size("y")
    z_count = lax.axis_size("z")
    tall = row_count // y_count

    core = lax.axis_index("core")
    swap = [(0, 1), (1, 0)]
    sent, share = pack(
        core, hidden_states.transpose(0, 2, 1), ln_in_gain, ln_out_gain, w_in, w_out, z_count, y_count
    )
    received = lax.all_to_all(sent, COLS, 0, 0)
    gain_in = received[:, local_width, :local_width].reshape(D).astype(f32)
    gain_out = received[:, local_width + 1, :local_width].reshape(D).astype(f32)
    inputs_t = received[:, :local_width].reshape(D, tall)

    shares = stack_shares(
        [
            lax.ppermute(share, "y", [(i, (i + step) % y_count) for i in range(y_count)])
            for step in range(1, y_count)
        ]
    )
    others = lax.ppermute(shares, "core", swap)

    inputs_f = inputs_t.astype(f32)
    center = jnp.mean(inputs_f, axis=0)
    spread = jnp.mean(inputs_f * inputs_f, axis=0) - center * center
    normed_t = (
        (inputs_f - center[None, :]) * lax.rsqrt(spread + norm_eps)[None, :] * gain_in[:, None]
    ).astype(bf16)
    block_part = feed_forward(core, normed_t.T, w_in, w_out, shares, others)
    block = scatter_sum(block_part.reshape(z_count, row_block, D), "z")
    picked = (
        jnp.arange(tall)[None, :]
        == lax.axis_index("z") * row_block + jnp.arange(row_block)[:, None]
    ).astype(bf16)
    own = lax.dot_general(picked, inputs_t, (((1,), (1,)), ((), ())), preferred_element_type=f32)
    resid = own + block
    center = jnp.mean(resid, axis=1, keepdims=True)
    spread = jnp.mean(resid * resid, axis=1, keepdims=True) - center * center
    final = (resid - center) * lax.rsqrt(spread + norm_eps) * gain_out[None, :]
    squared = jnp.sum(final * final, axis=1, keepdims=True)
    embed_part = (final * lax.rsqrt(squared + unit_eps)).astype(bf16)
    own_rows = gather_all(embed_part, "z").reshape(tall, D)

    x_index = lax.axis_index("x")
    x_count = lax.axis_size("x")
    unit, proto_len, turned = prepare(core, prototypes, x_count)
    proto_count = prototypes.shape[0]
    slice_width = turned.shape[1]

    row_parts = lax.axis_size(ROWS)
    y_index = lax.axis_index("y")
    steps = (1, 3, 2)
    rows_in = {
        step: lax.ppermute(own_rows, "y", [(i, (i + step) % y_count) for i in range(y_count)])
        for step in steps
    }
    places = jnp.stack([(y_index + y_count - step) % y_count for step in (0,) + steps])
    parts = [own_rows] + [rows_in[step] for step in steps]
    base, masses, soft_part, embed = score_pass(places, parts, unit, row_parts)
    masses = lax.all_to_all(masses, ROWS, 0, 0)
    softs = images = lax.all_to_all(image_pass(masses, base, col_count, soft_part), COLS, 0, 0)
    for repeat in range(1, SINK_ITERS):
        masses = lax.all_to_all(proto_pass(images, base, row_parts), ROWS, 0, 0)
        images = lax.all_to_all(image_pass(masses, base, col_count), COLS, 0, 0)

    radial, away, grad, embed_t, embed_terms = grad_pass(core, images, softs, masses, unit, embed)
    stay = stay_pass(embed_t, grad)
    arrived = lax.ppermute(away, "core", swap)
    parts = (stay, arrived, turned)
    lines = (radial, lax.ppermute(radial, "core", swap), proto_len)
    flat = (slice_width // 2, proto_count)

    def spot(step):
        return (x_index + step) % x_count

    def right(values):
        return lax.ppermute(values, "x", [(i, (i + 1) % x_count) for i in range(x_count)])

    def left(values):
        return lax.ppermute(values, "x", [((i + 1) % x_count, i) for i in range(x_count)])

    far_lower, far_upper = pair_call(far_kernel, (spot(2),), parts, lines, [(flat, bf16)] * 2)
    came_lower, came_upper = right(far_lower), left(far_upper)
    right_send, left_send, right_keep, left_keep = pair_call(
        near_kernel, (spot(1), spot(3)), parts, lines, [(flat, bf16)] * 2 + [(flat, f32)] * 2
    )
    near_upper, near_lower = right(right_send), left(left_send)
    own_sum = pair_call(
        own_kernel,
        (x_index,),
        parts,
        lines,
        [((slice_width, proto_count), f32)],
        (near_lower, near_upper),
    )
    right_relay, left_relay = call(
        relay_kernel,
        (),
        (right_keep, left_keep, came_lower, came_upper),
        [(flat, bf16)] * 2,
        8,
        10**8,
        10**6,
    )
    last_lower, last_upper = right(right_relay), left(left_relay)
    proto_grad = call(
        final_kernel,
        (),
        (own_sum, last_lower, last_upper),
        [((slice_width, proto_count), f32)],
        8,
        10**8,
        10**6,
    )
    embed_parts = lax.all_to_all(
        embed_terms.reshape(col_count, local_width, row_count), COLS, 0, 0
    )
    embed_parts, proto_grad = lax.optimization_barrier((embed_parts, proto_grad))
    embed_grad_t = jnp.sum(embed_parts.astype(f32), axis=0)
    embed_grad = embed_grad_t.T.reshape(view_count, image_rows, local_width)
    return (embed_grad, proto_grad)


def solution(mesh):
    sizes = {"x": mesh.shape["rows"] // 2, "core": 2, "z": mesh.shape["cols"] // 4, "y": 4}
    fine = Mesh(mesh.devices.reshape(tuple(sizes.values())), tuple(sizes))
    placed = (
        P(None, ROWS, COLS),
        P(COLS),
        P(None, COLS),
        P(COLS, None),
        P(COLS),
        P(COLS, None),
    )
    return jax.shard_map(
        body,
        mesh=fine,
        in_specs=placed,
        out_specs=(P(None, ROWS, COLS), P(ROWS, COLS)),
        check_vma=False,
    )
```
